128 devices in a mesh: dp: 16 (over y_hi, x, core), shard: 8 (over y_lo, z).
Axes of the slice: x: 4, y: 4 (y_hi: 2, y_lo: 2; y = y_hi * 2 + y_lo), z: 4, core: 2. Of those that a mesh axis runs over, the one named last changes fastest.
Arguments:
- hidden: bfloat16 [16, 1024, 1536], P('dp', 'shard'), may hold values from -6 to 6
- cotangent: bfloat16 [16, 1024, 1536], P('dp', 'shard'), may hold values from -6 to 6
- in_master: float32 [1536, 6448], P('shard'), may hold values from -0.15625 to 0.15625
- in_first: float32 [1536, 6448], P('shard'), may hold values from -24 to 24
- in_second: float32 [1536, 6448], P('shard'), may hold values from 73.728 to 294.912
- out_master: float32 [3072, 1536], P('shard'), may hold values from -0.109375 to 0.109375
- out_first: float32 [3072, 1536], P('shard'), may hold values from -80 to 80
- out_second: float32 [3072, 1536], P('shard'), may hold values from 819.2 to 3276.8
- gain_master: float32 [4608], P('shard'), may hold values from 0.5 to 1.5
- gain_first: float32 [4608], P('shard'), may hold values from -24 to 24
- gain_second: float32 [4608], P('shard'), may hold values from 73.728 to 294.912
- conv_master: float32 [5, 3328], P(None, 'shard'), may hold values from -3 to 3
- conv_first: float32 [5, 3328], P(None, 'shard'), may hold values from -24 to 24
- conv_second: float32 [5, 3328], P(None, 'shard'), may hold values from 73.728 to 294.912
- head_master: float32 [3, 48], P(None, 'shard'), may hold values from -10 to 2
- head_first: float32 [3, 48], P(None, 'shard'), may hold values from -80 to 80
- head_second: float32 [3, 48], P(None, 'shard'), may hold values from 819.2 to 3276.8
Outputs:
- layer_out: bfloat16 [16, 1024, 1536], P('dp', 'shard')
- input_grad: bfloat16 [16, 1024, 1536], P('dp', 'shard')
- in_moment: float32 [1536, 6448], P('shard')
- in_square: float32 [1536, 6448], P('shard')
- in_weight: float32 [1536, 6448], P('shard')
- out_moment: float32 [3072, 1536], P('shard')
- out_square: float32 [3072, 1536], P('shard')
- out_weight: float32 [3072, 1536], P('shard')
- gain_moment: float32 [4608], P('shard')
- gain_square: float32 [4608], P('shard')
- gain_value: float32 [4608], P('shard')
- conv_moment: float32 [5, 3328], P(None, 'shard')
- conv_square: float32 [5, 3328], P(None, 'shard')
- conv_value: float32 [5, 3328], P(None, 'shard')
- head_moment: float32 [3, 48], P(None, 'shard')
- head_square: float32 [3, 48], P(None, 'shard')
- head_value: float32 [3, 48], P(None, 'shard')
The draws below stay inside these ranges and needn't reach their ends.
All inputs are finite; a program needn't handle non-finite values.
Results may differ from the reference program's by a relative error of at most 0.0044.
The reference program's roundings to bfloat16 on the way count: a program that leaves them out, or rounds other values in their place, can miss the bound.
Values may be sent and summed in bfloat16 or wider, within the bound.
A program may use at most 320 MiB of HBM per device.

```python
import math
import jax
import jax.numpy as jnp
from jax import lax

D = 1536
DI = 3072
H = 48
HD = 64
NS = 128
KCONV = 4
STEP = 5
BLOCK = 128
CONVC = 3328
PROJ = 6448
LEN = 1024
SEQS = 16
N_DP = 16


def draw_head_master(key, part):
    key = jax.random.fold_in(key, 7)
    subkeys = jax.random.split(key, 5)
    slow_share = 0.5
    bias_row = jax.random.uniform(subkeys[0], (H,), jnp.float32, -2.5, -1.0)
    slow_heads = jax.random.bernoulli(subkeys[1], slow_share, (H,))
    slow_rate = jnp.exp(jax.random.uniform(subkeys[2], (H,), jnp.float32, math.log(0.3 / LEN), math.log(1.5 / LEN)))
    fast_rate = jnp.exp(jax.random.uniform(subkeys[3], (H,), jnp.float32, math.log(1.0 / 60.0), math.log(1.0 / 25.0)))
    rate_row = jnp.where(slow_heads, slow_rate, fast_rate)
    skip_row = jax.random.uniform(subkeys[4], (H,), jnp.float32, 0.5, 1.5)
    return jnp.stack([bias_row, jnp.log(rate_row / 0.25), skip_row]).astype(jnp.float32)


def levels(rng, dims, cuts, smallest, top_value):
    loudness, own = 1.0, jax.random.fold_in(rng, 6)
    for dim, blocks in cuts:
        steps = jnp.exp(jax.random.uniform(jax.random.fold_in(own, dim), (blocks,), jnp.float32, smallest / len(cuts), top_value / len(cuts)))
        loudness = loudness * jnp.repeat(steps, dims[dim] // blocks).reshape([-1 if axis == dim else 1 for axis in range(len(dims))])
    return loudness


def scatter_about(own_key, extent, spread, bound, cuts=(), kind=jnp.bfloat16):
    drawn = spread * jax.random.normal(own_key, extent, jnp.float32)
    if cuts:
        drawn = drawn * levels(own_key, extent, cuts, -0.22, 0.18)
    return jnp.clip(drawn, -bound, bound).astype(kind)


def setup_inputs(seed: int = 0) -> dict:
    keys = jax.random.split(jax.random.key(seed), 18)
    hidden = scatter_about(keys[0], (SEQS, LEN, D), 1.0, 6.0, ((0, 16), (1, 8)))
    cotangent = scatter_about(keys[1], (SEQS, LEN, D), 1.0, 6.0, ((0, 16), (1, 8)))
    in_master = scatter_about(keys[2], (D, PROJ), D ** -0.5, 0.15625, ((0, 8),), jnp.float32)
    in_first = scatter_about(keys[3], (D, PROJ), (0.033 * (N_DP * LEN) ** 0.5), 24.0, ((0, 8),), jnp.float32)
    in_second = jnp.clip(jnp.exp(math.log(294.912) - 1.3862944 * jax.random.uniform(keys[4], (D, PROJ), jnp.float32) ** levels(keys[4], (D, PROJ), ((0, 8),), -0.2, 0.2)), 73.728, 294.912)
    out_master = scatter_about(keys[5], (DI, D), DI ** -0.5, 0.109375, ((0, 8),), jnp.float32)
    out_first = scatter_about(keys[6], (DI, D), (0.11 * (N_DP * LEN) ** 0.5), 80.0, ((0, 8),), jnp.float32)
    out_second = jnp.clip(jnp.exp(math.log(3276.8) - 1.3862944 * jax.random.uniform(keys[7], (DI, D), jnp.float32) ** levels(keys[7], (DI, D), ((0, 8),), -0.2, 0.2)), 819.2, 3276.8)
    gain_master = jnp.clip(1.0 + 0.1 * jax.random.normal(keys[8], (D + DI,), jnp.float32), 0.5, 1.5)
    gain_first = scatter_about(keys[9], (D + DI,), (0.033 * (N_DP * LEN) ** 0.5), 24.0, ((0, 8),), jnp.float32)
    gain_second = jnp.clip(jnp.exp(math.log(294.912) - 1.3862944 * jax.random.uniform(keys[10], (D + DI,), jnp.float32) ** levels(keys[10], (D + DI,), ((0, 8),), -0.2, 0.2)), 73.728, 294.912)
    conv_master = scatter_about(keys[11], (KCONV + 1, CONVC), 0.5, 3.0, ((1, 8),), jnp.float32)
    conv_first = scatter_about(keys[12], (KCONV + 1, CONVC), (0.033 * (N_DP * LEN) ** 0.5), 24.0, ((1, 8),), jnp.float32)
    conv_second = jnp.clip(jnp.exp(math.log(294.912) - 1.3862944 * jax.random.uniform(keys[13], (KCONV + 1, CONVC), jnp.float32) ** levels(keys[13], (KCONV + 1, CONVC), ((1, 8),), -0.2, 0.2)), 73.728, 294.912)
    head_master = draw_head_master(jax.random.fold_in(keys[17], 71), 0)
    head_first = scatter_about(keys[15], (3, H), (0.11 * (N_DP * LEN) ** 0.5), 80.0, ((1, 8),), jnp.float32)
    head_second = jnp.clip(jnp.exp(math.log(3276.8) - 1.3862944 * jax.random.uniform(keys[16], (3, H), jnp.float32) ** levels(keys[16], (3, H), ((1, 8),), -0.2, 0.2)), 819.2, 3276.8)
    return {"hidden": hidden, "cotangent": cotangent, "in_master": in_master, "in_first": in_first, "in_second": in_second, "out_master": out_master, "out_first": out_first, "out_second": out_second, "gain_master": gain_master, "gain_first": gain_first, "gain_second": gain_second, "conv_master": conv_master, "conv_first": conv_first, "conv_second": conv_second, "head_master": head_master, "head_first": head_first, "head_second": head_second}


highest = lax.Precision.HIGHEST
epsilon = 1e-05
beta_one = 0.9
beta_two = 0.95
adam_epsilon = 1e-08
rates = (0.05, 0.04, 0.25, 0.5, 0.5)
decays = (0.1, 0.1, 0.0, 0.0, 0.0)

@jax.custom_vjp
def low(v):
    return lax.optimization_barrier(v.astype(jnp.bfloat16)).astype(jnp.float32)

@jax.custom_vjp
def low_back(v):
    return v

def low_keep(v):
    return (low(v), None)

def low_pass(kept, grad):
    return (grad,)

def back_keep(v):
    return (v, None)

def back_low(kept, grad):
    return (low(grad),)
low.defvjp(low_keep, low_pass)
low_back.defvjp(back_keep, back_low)

def rms_scale(values):
    return lax.rsqrt(lax.optimization_barrier(jnp.mean(values * values, axis=-1, keepdims=True)) + epsilon)

def front_norm(inputs, norm_gain):
    return inputs * rms_scale(inputs) * norm_gain

def block_step(carry_state, pieces):
    block_input, block_keys, block_query, block_sizes, block_decay = pieces
    length = block_input.shape[0]
    cumulative = jnp.cumsum(block_decay, axis=0)
    query_pos = lax.broadcasted_iota(jnp.int32, (length, length), 0)
    source_pos = lax.broadcasted_iota(jnp.int32, (length, length), 1)
    causal = (query_pos >= source_pos)[None]
    heads_first = jnp.transpose(cumulative)
    differ = heads_first[:, :, None] - heads_first[:, None, :]
    mixing = jnp.exp(jnp.where(causal, differ, -jnp.inf))
    contact = jnp.dot(block_query, jnp.transpose(block_keys), precision=highest)
    scaled_input = block_input * block_sizes[:, :, None]
    within = jnp.einsum('hts,shp->thp', mixing * contact[None], scaled_input, precision=highest)
    carried = jnp.einsum('tn,hpn->thp', block_query, carry_state, precision=highest) * jnp.exp(cumulative)[:, :, None]
    remaining = jnp.exp(cumulative[length - 1][None, :] - cumulative)
    added_state = jnp.einsum('sh,shp,sn->hpn', remaining, scaled_input, block_keys, precision=highest)
    new_state = jnp.exp(cumulative[length - 1])[:, None, None] * carry_state + added_state
    return (new_state, within + carried)

def local_scan(head_values, state_keys, state_queries, step_sizes, log_decay):
    block_count = head_values.shape[0] // BLOCK
    stacked = (head_values.reshape(block_count, BLOCK, H, HD), state_keys.reshape(block_count, BLOCK, NS), state_queries.reshape(block_count, BLOCK, NS), step_sizes.reshape(block_count, BLOCK, H), log_decay.reshape(block_count, BLOCK, H))
    initial = jnp.zeros((H, HD, NS), jnp.float32)
    final_state, outputs = lax.scan(jax.checkpoint(block_step), initial, stacked)
    return (outputs.reshape(block_count * BLOCK, H, HD), final_state, lax.optimization_barrier(jnp.sum(log_decay, axis=0)))

def mixer_inputs(rim_rows, mixed_in, step_raw, conv_params, head_params):
    length = mixed_in.shape[0]
    extended = jnp.concatenate([rim_rows, mixed_in], axis=0)
    conv_out = conv_params[KCONV] + sum((conv_params[offset] * extended[offset:offset + length] for offset in range(KCONV)))
    activated = jax.nn.silu(conv_out)
    head_values = activated[:, :DI].reshape(length, H, HD)
    state_keys = activated[:, DI:DI + NS]
    state_queries = activated[:, DI + NS:]
    step_sizes = jax.nn.softplus(step_raw + head_params[0])
    log_decay = -jnp.exp(head_params[1]) * step_sizes
    return (head_values, state_keys, state_queries, step_sizes, log_decay)

def mixer_outputs(core_values, head_values, gate_raw, gate_gain, skip_weight):
    length = core_values.shape[0]
    with_skip = core_values + skip_weight[None, :, None] * head_values
    gated = with_skip.reshape(length, DI) * jax.nn.silu(gate_raw)
    return gated * rms_scale(gated) * gate_gain

def layer_forward(inputs, in_weights, out_weights, gains, conv_params, head_params):
    normed = low(front_norm(inputs, gains[:D]))
    project = low_back(jnp.dot(normed, in_weights, precision=highest))
    rim_rows = jnp.zeros((KCONV - 1, CONVC), jnp.float32)
    prepared = mixer_inputs(rim_rows, project[:, DI:DI + CONVC], project[:, DI + CONVC:], conv_params, head_params)
    scanned = local_scan(prepared[0], prepared[1], prepared[2], prepared[3], prepared[4])
    mixed = low(mixer_outputs(scanned[0], prepared[0], project[:, :DI], gains[D:], head_params[2]))
    return inputs + jnp.dot(mixed, out_weights, precision=highest)

def adam_update(master, first, second, gradient, rate, decay):
    first_new = beta_one * first + (1.0 - beta_one) * gradient
    second_new = beta_two * second + (1.0 - beta_two) * gradient * gradient
    scaled = first_new / (1.0 - beta_one ** STEP) / (jnp.sqrt(second_new / (1.0 - beta_two ** STEP)) + adam_epsilon)
    return (first_new, second_new, master - rate * (scaled + decay * master))

def reference(hidden, cotangent, in_master, in_first, in_second, out_master, out_first, out_second, gain_master, gain_first, gain_second, conv_master, conv_first, conv_second, head_master, head_first, head_second):
    masters = (in_master, out_master, gain_master, conv_master, head_master)
    firsts = (in_first, out_first, gain_first, conv_first, head_first)
    seconds = (in_second, out_second, gain_second, conv_second, head_second)
    params = tuple((lax.optimization_barrier(master.astype(jnp.bfloat16)).astype(jnp.float32) for master in masters))

    def one_sequence(summed, pieces):
        seq_hidden, seq_cotangent = pieces
        result, pullback = jax.vjp(layer_forward, seq_hidden.astype(jnp.float32), params[0], params[1], params[2], params[3], params[4])
        gradients = pullback(seq_cotangent.astype(jnp.float32))
        summed = tuple((before + gradient for before, gradient in zip(summed, gradients[1:])))
        return (summed, (result.astype(jnp.bfloat16), gradients[0].astype(jnp.bfloat16)))
    initial = tuple((jnp.zeros(param.shape, jnp.float32) for param in params))
    summed, outputs = lax.scan(one_sequence, initial, (hidden, cotangent))
    updated = [adam_update(masters[group], firsts[group], seconds[group], summed[group], rates[group], decays[group]) for group in range(5)]
    return (outputs[0], outputs[1], updated[0][0], updated[0][1], updated[0][2], updated[1][0], updated[1][1], updated[1][2], updated[2][0], updated[2][1], updated[2][2], updated[3][0], updated[3][1], updated[3][2], updated[4][0], updated[4][1], updated[4][2])
```

```python
import functools

import jax
import jax.numpy as jnp
from jax import lax
from jax.experimental import pallas as pl
from jax.experimental.pallas import tpu as pltpu
from jax.sharding import PartitionSpec as P

D = 1536
DI = 3072
H = 48
HD = 64
NS = 128
KCONV = 4
STEP = 5
BLOCK = 128
CONVC = 3328
PROJ = 6448
LEN = 1024
OWN = 384
COLS = 1152
WIDE = 6528
BLOCKS = LEN // BLOCK

f32 = jnp.float32
bf16 = jnp.bfloat16
highest = lax.Precision.HIGHEST
MESH = pl.DeviceIdType.MESH
epsilon = 1e-05
beta_one = 0.9
beta_two = 0.95
adam_epsilon = 1e-08
rates = (0.05, 0.04, 0.25, 0.5, 0.5)
decays = (0.1, 0.1, 0.0, 0.0, 0.0)
VMEM_LIMIT = 60 * 2**20


class Place:
    def __init__(self):
        self.d = lax.axis_index("dp")
        self.s = lax.axis_index("shard")
        self.c = lax.rem(self.d, 2)
        self.x = lax.rem(self.d // 2, 4)
        self.yh = self.d // 8
        self.big = self.d // 2
        self.z = lax.rem(self.s, 4)
        self.yl = self.s // 4

    def shard_of(self, k):
        return lax.rem(self.yl + k // 4, 2) * 4 + lax.rem(self.z + k % 4, 4)

    def shard_peer(self, k):
        return (self.d, self.shard_of(k))

    def big_of(self, k):
        return lax.rem(self.yh + k // 4, 2) * 4 + lax.rem(self.x + k % 4, 4)

    def big_peer(self, k):
        return (self.big_of(k) * 2 + self.c, self.s)

    def core_peer(self):
        return (self.big * 2 + 1 - self.c, self.s)

    def other_core_of(self, k):
        return (self.big_of(k) * 2 + 1 - self.c, self.s)


ORDER = (6, 2, 5, 7, 1, 3, 4)


def exchange(cid, body, ins, outs, sems, locals_):
    def kernel(*refs):
        in_refs = refs[: len(ins)]
        out_refs = refs[len(ins) : len(ins) + len(outs)]
        send, recv, own = refs[len(ins) + len(outs) :]
        place = Place()

        def meet(peers):
            barrier = pltpu.get_barrier_semaphore()
            for peer in peers:
                pl.semaphore_signal(barrier, inc=1, device_id=peer, device_id_type=MESH)
            pl.semaphore_wait(barrier, len(peers))

        def remote(src, dst, index, peer):
            return pltpu.make_async_remote_copy(
                src_ref=src,
                dst_ref=dst,
                send_sem=send.at[index],
                recv_sem=recv.at[index],
                device_id=peer,
                device_id_type=MESH,
            )

        def local(src, dst, index):
            return pltpu.make_async_copy(src, dst, own.at[index])

        body(place, meet, remote, local, in_refs, out_refs)

    any_spec = pl.BlockSpec(memory_space=pl.ANY)
    return pl.pallas_call(
        kernel,
        out_shape=outs,
        in_specs=[any_spec] * len(ins),
        out_specs=tuple([any_spec] * len(outs)),
        scratch_shapes=[
            pltpu.SemaphoreType.DMA((sems,)),
            pltpu.SemaphoreType.DMA((sems,)),
            pltpu.SemaphoreType.DMA((max(locals_, 1),)),
        ],
        compiler_params=pltpu.CompilerParams(collective_id=cid, has_side_effects=True),
    )(*ins)


def gather_body(place, meet, remote, local, ins, outs):
    hid, cot, wide, small = ins
    u_out, ct_out, w_out, sm_out = outs
    meet([place.shard_peer(k) for k in ORDER])
    me = place.s
    copies = []
    own = [
        local(hid, u_out.at[me], 0),
        local(cot, ct_out.at[me], 1),
        local(small, sm_out.at[me], 2),
    ]

    def weight_parts(k):
        them = place.shard_of(k)
        at = pl.multiple_of(them * OWN, 128)
        return (
            (wide.at[:, pl.ds(at, OWN)], w_out.at[me, :, pl.ds(0, OWN)]),
            (wide.at[:, pl.ds(at + DI, OWN)], w_out.at[me, :, pl.ds(OWN, OWN)]),
            (wide.at[:, pl.ds(2 * DI, OWN)], w_out.at[me, :, pl.ds(2 * OWN, OWN)]),
        )

    for i, (src, dst) in enumerate(weight_parts(0)):
        own.append(local(src, dst, 3 + i))
    for copy in own:
        copy.start()
    for n, k in enumerate(ORDER):
        peer = place.shard_peer(k)
        copies.append(remote(small, sm_out.at[me], n, peer))
    for n, k in enumerate(ORDER):
        peer = place.shard_peer(k)
        for i, (src, dst) in enumerate(weight_parts(k)):
            copies.append(remote(src, dst, 7 + 3 * n + i, peer))
    for n, k in enumerate(ORDER):
        copies.append(remote(hid, u_out.at[me], 28 + n, place.shard_peer(k)))
    for n, k in enumerate(ORDER):
        copies.append(remote(cot, ct_out.at[me], 35 + n, place.shard_peer(k)))
    for copy in copies:
        copy.start()
    for copy in own + copies:
        copy.wait()


def all_body(place, meet, remote, local, ins, outs):
    (block,) = ins
    (out,) = outs
    meet([place.shard_peer(k) for k in ORDER])
    own = local(block, out.at[place.s], 0)
    own.start()
    copies = [
        remote(block, out.at[place.s], n, place.shard_peer(k)) for n, k in enumerate(ORDER)
    ]
    for copy in copies:
        copy.start()
    own.wait()
    for copy in copies:
        copy.wait()


def scatter_body(place, meet, remote, local, ins, outs):
    meet([place.shard_peer(k) for k in ORDER])
    copies = []
    for a in range(len(ins)):
        copies.append(local(ins[a].at[place.s], outs[a].at[place.s], a))
    for n, k in enumerate(ORDER):
        for a in range(len(ins)):
            copies.append(
                remote(
                    ins[a].at[place.shard_of(k)],
                    outs[a].at[place.s],
                    n * len(ins) + a,
                    place.shard_peer(k),
                )
            )
    for copy in copies:
        copy.start()
    for copy in copies:
        copy.wait()


def swap_body(place, meet, remote, local, ins, outs):
    gw, go = ins
    gw_out, go_out = outs
    meet([place.core_peer()])
    other = 1 - place.c
    copies = [
        remote(gw.at[pl.ds(other * 4, 4)], gw_out, 0, place.core_peer()),
        remote(
            go.at[:, :, pl.ds(pl.multiple_of(other * 768, 128), 768)],
            go_out,
            1,
            place.core_peer(),
        ),
    ]
    for copy in copies:
        copy.start()
    for copy in copies:
        copy.wait()


def reduce_body(place, meet, remote, local, ins, outs):
    hw, ho = ins
    hw_out, ho_out = outs
    meet([place.big_peer(k) for k in ORDER])
    copies = [
        local(hw.at[:, place.big], hw_out.at[0], 0),
        local(ho.at[place.big], ho_out.at[0], 1),
    ]
    for n, k in enumerate(ORDER):
        them = place.big_of(k)
        copies.append(remote(hw.at[:, them], hw_out.at[k], 2 * n, place.big_peer(k)))
        copies.append(remote(ho.at[them], ho_out.at[k], 2 * n + 1, place.big_peer(k)))
    for copy in copies:
        copy.start()
    for copy in copies:
        copy.wait()


def owner_body(place, meet, remote, local, ins, outs):
    piece, small = ins
    piece_out, small_out = outs
    meet([place.shard_peer(k) for k in ORDER])
    valid = place.yl == place.c
    own_small = local(small, small_out.at[place.s], 0)
    own_small.start()
    own_piece = local(piece.at[place.z], piece_out.at[place.s], 1)

    @pl.when(valid)
    def _():
        own_piece.start()

    smalls = [
        remote(small, small_out.at[place.s], n, place.shard_peer(k))
        for n, k in enumerate(ORDER)
    ]
    for copy in smalls:
        copy.start()
    pieces = []
    for n, k in enumerate(ORDER):
        them = place.shard_of(k)
        copy = remote(
            piece.at[lax.rem(them, 4)], piece_out.at[place.s], 7 + n, place.shard_peer(k)
        )
        goes = them // 4 == place.c
        pl.when(goes)(copy.start)
        pieces.append((copy, goes))
    own_small.wait()
    pl.when(valid)(own_piece.wait)
    for copy in smalls:
        copy.wait()
    for copy, goes in pieces:
        pl.when(goes)(copy.wait_send)
        pl.when(valid)(copy.wait_recv)


def spread_body(place, meet, remote, local, ins, outs):
    slab, go, small = ins
    slab_out, go_out, small_out = outs
    core = place.core_peer()
    everyone = [place.big_peer(k) for k in ORDER] + [core]
    everyone += [place.other_core_of(k) for k in ORDER]
    meet(everyone)
    valid = place.yl == place.c
    at = pl.multiple_of(place.c * 768, 128)

    def half(index):
        return go_out.at[index, :, pl.ds(at, 768)]

    other_at = pl.multiple_of((1 - place.c) * 768, 128)
    own_small = local(small, small_out.at[place.d], 0)
    own_go = local(go, half(place.big), 1)
    own_slab = local(slab, slab_out.at[place.big], 2)
    own_small.start()
    own_go.start()
    smalls = [
        remote(small, small_out.at[place.d], n, peer) for n, peer in enumerate(everyone)
    ]
    slabs = [
        remote(slab, slab_out.at[place.big], 15 + n, place.big_peer(k))
        for n, k in enumerate(ORDER)
    ]
    gos = [
        remote(go, half(place.big), 22 + n, place.big_peer(k)) for n, k in enumerate(ORDER)
    ]
    to_core_slab = remote(slab, slab_out.at[place.big], 29, core)
    to_core_go = remote(go, half(place.big), 30, core)

    @pl.when(valid)
    def _():
        own_slab.start()
        for copy in slabs:
            copy.start()
        to_core_slab.start()

    for copy in gos:
        copy.start()
    to_core_go.start()
    for copy in smalls:
        copy.start()
    forward_gos = []
    forward_slabs = []
    for n, k in enumerate(ORDER):
        origin = lax.rem(place.yh + k // 4, 2) * 4 + lax.rem(place.x + 4 - k % 4, 4)
        gos[n].wait_recv()
        go_copy = remote(half(origin), half(origin), 31 + n, core)
        go_copy.start()
        forward_gos.append(go_copy)
        slab_copy = remote(slab_out.at[origin], slab_out.at[origin], 38 + n, core)

        @pl.when(valid)
        def _(n=n, slab_copy=slab_copy):
            slabs[n].wait_recv()
            slab_copy.start()

        forward_slabs.append(slab_copy)
    own_small.wait()
    own_go.wait()
    for copy in smalls:
        copy.wait()
    for copy in gos:
        copy.wait_send()
    to_core_go.wait()
    for copy in forward_gos:
        copy.wait()

    @pl.when(valid)
    def _():
        own_slab.wait()
        for copy in slabs:
            copy.wait_send()
        to_core_slab.wait_send()
        for copy in forward_slabs:
            copy.wait_send()

    @pl.when(jnp.logical_not(valid))
    def _():
        to_core_slab.wait_recv()
        for copy in forward_slabs:
            copy.wait_recv()


def dot(a, b, ca, cb, precision=None):
    return lax.dot_general(
        a, b, (((ca,), (cb,)), ((), ())), precision=precision, preferred_element_type=f32
    )


def mm(a, b, ca=1, cb=0):
    return dot(a.astype(f32), b.astype(f32), ca, cb, highest)


def lanes(shape):
    return lax.broadcasted_iota(jnp.int32, shape, 1)


def rows_of(shape):
    return lax.broadcasted_iota(jnp.int32, shape, 0)


def widen(m):
    low = lanes((m.shape[0], 128)) < HD
    return jnp.concatenate(
        [jnp.where(low, m[:, 2 * i : 2 * i + 1], m[:, 2 * i + 1 : 2 * i + 2]) for i in range(3)],
        axis=1,
    )


def lower_ones():
    return (rows_of((BLOCK, BLOCK)) >= lanes((BLOCK, BLOCK))).astype(f32)


def head_ones():
    return (rows_of((OWN, BLOCK)) // HD == lanes((OWN, BLOCK))).astype(f32)


def split_pair(pair):
    low = lanes(pair.shape) < HD
    zero = jnp.zeros_like(pair)
    return jnp.concatenate([jnp.where(low, pair, zero), jnp.where(low, zero, pair)], axis=0)


def decay_parts(log_decay):
    cumulative = dot(lower_ones(), log_decay, 1, 0, highest)
    return cumulative, cumulative.T, widen(cumulative)


def head_mixing(cumulative, turned, h):
    causal = rows_of((BLOCK, BLOCK)) >= lanes((BLOCK, BLOCK))
    differ = cumulative[:, h : h + 1] - turned[h : h + 1, :]
    return jnp.exp(jnp.where(causal, differ, -jnp.inf))


def softplus(v):
    return jnp.maximum(v, 0.0) + jnp.log1p(jnp.exp(-jnp.abs(v)))


TB = 256


def forward_kernel(
    u_ref, ct_ref, w_ref, wo_ref, gn_ref, gg_ref, cv_ref, hd_ref, sk_ref,
    n_ref, z_ref, xbc_ref, cvo_ref, raw_ref, core_ref, dm_ref, st_ref, sums_ref,
    state, halo,
):
    i = pl.program_id(0)

    @pl.when(i == 0)
    def _():
        state[...] = jnp.zeros_like(state)
        halo[...] = jnp.zeros_like(halo)

    u = u_ref[...].astype(f32)
    scale = lax.rsqrt(jnp.mean(u * u, axis=1, keepdims=True) + epsilon)
    normed = (u * scale * gn_ref[0:1, :]).astype(bf16)
    n_ref[...] = normed
    project = dot(normed, w_ref[...], 1, 0)
    z = project[:, :OWN]
    xbc = project[:, OWN : OWN + 640]
    back = 128 - 6 * lax.axis_index("shard")
    raw = pltpu.roll(project[:, 1024:1152], back, 1)
    z_ref[...] = z
    xbc_ref[...] = xbc
    raw_ref[...] = raw
    extended = jnp.concatenate([halo[...], xbc], axis=0)
    halo[...] = xbc[TB - 8 :, :]
    conv = cv_ref[KCONV : KCONV + 1, :] + sum(
        cv_ref[k : k + 1, :] * extended[5 + k : 5 + k + TB, :] for k in range(KCONV)
    )
    cvo_ref[...] = conv
    act = conv * jax.nn.sigmoid(conv)
    dt = softplus(raw + hd_ref[0:1, :])
    log_decay = -jnp.exp(hd_ref[1:2, :]) * dt
    gate = z * jax.nn.sigmoid(z)
    dm = dot(ct_ref[...], wo_ref[...], 1, 1)
    dm_ref[...] = dm
    for j in range(TB // BLOCK):
        at = slice(j * BLOCK, (j + 1) * BLOCK)
        x, keys, query = act[at, :OWN], act[at, OWN : OWN + NS], act[at, OWN + NS :]
        cumulative, turned, wide = decay_parts(log_decay[at])
        contact = mm(query, keys, 1, 1)
        scaled = x * widen(dt[at])
        within = []
        for p in range(3):
            pair = split_pair(scaled[:, 128 * p : 128 * p + 128])
            both = jnp.concatenate(
                [
                    (head_mixing(cumulative, turned, 2 * p + q) * contact)
                    for q in range(2)
                ],
                axis=1,
            )
            within.append(dot(both, pair, 1, 0, highest))
        last = wide[BLOCK - 1 : BLOCK, :]
        before = state[...]
        st_ref[j] = before
        core = jnp.concatenate(within, axis=1) + mm(query, before) * jnp.exp(wide)
        state[...] = jnp.exp(last) * before + mm(keys, scaled * jnp.exp(last - wide), 0, 0)
        core_ref[at, :] = core
        gated = (core + sk_ref[0:1, :] * x) * gate[at]
        ones = jnp.ones((8, OWN), f32)
        first = dot(ones, gated * gated, 1, 1, highest)
        second = dot(ones, gated * (gg_ref[0:1, :] * dm[at]), 1, 1, highest)
        b = (TB // BLOCK) * i + j
        sums_ref[pl.ds(b, 1), :] = first[0:1]
        sums_ref[pl.ds(b + 8, 1), :] = second[0:1]


def backward_kernel(
    z_ref, xbc_ref, cvo_ref, raw_ref, core_ref, dm_ref, st_ref, sums_ref,
    gg_ref, cv_ref, hd_ref, sk_ref,
    dp_ref, mixed_ref, dgain_ref, dskip_ref, dconv_ref, dhead_ref,
    adjoint, halo,
):
    i = pl.program_id(0)

    @pl.when(i == 0)
    def _():
        adjoint[...] = jnp.zeros_like(adjoint)
        halo[...] = jnp.zeros_like(halo)
        dgain_ref[...] = jnp.zeros_like(dgain_ref)
        dskip_ref[...] = jnp.zeros_like(dskip_ref)
        dconv_ref[...] = jnp.zeros_like(dconv_ref)
        dhead_ref[...] = jnp.zeros_like(dhead_ref)

    b = BLOCKS - 1 - i
    totals = sums_ref[0]
    for j in range(1, 8):
        totals += sums_ref[j]
    column = jnp.concatenate([totals, jnp.zeros((112, 128), f32)], axis=0).T
    lane = lanes((BLOCK, 128))
    first = jnp.sum(jnp.where(lane == b, column, 0.0), axis=1, keepdims=True)
    second = jnp.sum(jnp.where(lane == b + 8, column, 0.0), axis=1, keepdims=True)
    z, conv, raw, core, dm = z_ref[...], cvo_ref[...], raw_ref[...], core_ref[...], dm_ref[...]
    sig = jax.nn.sigmoid(conv)
    act = conv * sig
    x, keys, query = act[:, :OWN], act[:, OWN : OWN + NS], act[:, OWN + NS :]
    shifted = raw + hd_ref[0:1, :]
    dt = softplus(shifted)
    rate = jnp.exp(hd_ref[1:2, :])
    log_decay = -rate * dt
    sig_z = jax.nn.sigmoid(z)
    gate = z * sig_z
    skip = sk_ref[0:1, :]
    with_skip = core + skip * x
    gated = with_skip * gate
    scale = lax.rsqrt(first * (1.0 / DI) + epsilon)
    gain = gg_ref[0:1, :]
    unit = gated * scale
    mixed_ref[...] = (unit * gain).astype(bf16)
    dgain_ref[0:1, :] += jnp.sum(dm * unit, axis=0, keepdims=True)
    dgated = scale * (gain * dm) - unit * (scale * scale * (second * (1.0 / DI)))
    dz = dgated * with_skip * (sig_z * (1.0 + z * (1.0 - sig_z)))
    dcore = dgated * gate
    dskip_ref[0:1, :] += jnp.sum(dcore * x, axis=0, keepdims=True)

    cumulative, turned, wide = decay_parts(log_decay)
    contact = mm(query, keys, 1, 1)
    dt_wide = widen(dt)
    scaled = x * dt_wide
    scaled_low = scaled
    dcore_low = dcore
    dcontact = jnp.zeros((BLOCK, BLOCK), f32)
    dscaled = []
    for p in range(3):
        at = slice(128 * p, 128 * p + 128)
        mixing = [head_mixing(cumulative, turned, 2 * p + q) for q in range(2)]
        both = jnp.concatenate([(m * contact) for m in mixing], axis=0)
        pair = split_pair(dcore_low[:, at])
        dscaled.append(dot(both, pair, 0, 0, highest))
        dmix = dot(pair, scaled_low[:, at], 1, 1, highest)
        dcontact += dmix[:BLOCK] * mixing[0] + dmix[BLOCK:] * mixing[1]
    last = wide[BLOCK - 1 : BLOCK, :]
    before = st_ref[0]
    after_adj = adjoint[...]
    grown = jnp.exp(wide)
    left = jnp.exp(last - wide)
    from_core = dcore * grown
    dquery = mm(from_core, before, 1, 1) + mm(dcontact, keys)
    carried = mm(keys, after_adj) * left
    dscaled = jnp.concatenate(dscaled, axis=1) + carried
    dkeys = mm(scaled * left, after_adj, 1, 1) + mm(dcontact, query, 0, 0)
    end = jnp.exp(last)
    adjoint[...] = end * after_adj + mm(query, from_core, 0, 0)
    heads = head_ones()
    last_add = dot(
        jnp.sum(carried * scaled, axis=0, keepdims=True)
        + end * jnp.sum(after_adj * before, axis=0, keepdims=True),
        heads, 1, 0, highest,
    )
    dcum = dot(
        dcore_low.astype(f32) * core - dscaled * scaled_low.astype(f32), heads, 1, 0, highest
    )
    dlog = dot(lower_ones(), dcum, 0, 0, highest) + last_add
    ddt = dot(dscaled * x, heads, 1, 0, highest) - rate * dlog
    draw = ddt * jax.nn.sigmoid(shifted)
    dhead_ref[0:1, :] += jnp.sum(draw, axis=0, keepdims=True)
    dhead_ref[1:2, :] += jnp.sum(dlog * log_decay, axis=0, keepdims=True)
    dx = dscaled * dt_wide + skip * dcore
    dact = jnp.concatenate([dx, dkeys, dquery], axis=1)
    dconv = dact * (sig * (1.0 + conv * (1.0 - sig)))
    extended = jnp.concatenate([dconv, halo[...]], axis=0)
    halo[...] = dconv[:8, :]
    xbc = xbc_ref[...]
    dxbc = jnp.zeros_like(xbc)
    for k in range(KCONV):
        moved = extended[3 - k : 3 - k + BLOCK, :]
        dxbc += cv_ref[k : k + 1, :] * moved
        dconv_ref[k : k + 1, :] += jnp.sum(xbc * moved, axis=0, keepdims=True)
    dconv_ref[KCONV : KCONV + 1, :] += jnp.sum(dconv, axis=0, keepdims=True)
    own_head = lane < 6
    draw_low = jnp.where(own_head, draw, 0.0)
    dp_ref[:, :OWN] = dz.astype(bf16)
    dp_ref[:, OWN : OWN + 640] = dxbc.astype(bf16)
    dp_ref[:, 1024:] = pltpu.roll(draw_low, 6 * lax.axis_index("shard"), 1).astype(bf16)


def sds(shape, dtype=f32):
    return jax.ShapeDtypeStruct(shape, dtype)


def fixed(shape):
    return pl.BlockSpec(shape, lambda i: (0,) * len(shape))


def run_forward(u, ct, w, wo, gn, gg, cv, hd, sk):
    def tokens(columns):
        return pl.BlockSpec((TB, columns), lambda i: (i, 0))

    per = TB // BLOCK
    return pl.pallas_call(
        forward_kernel,
        grid=(LEN // TB,),
        in_specs=[
            tokens(D), tokens(D), fixed((D, COLS)), fixed((OWN, D)),
            fixed((1, D)), fixed((1, OWN)), fixed((8, 640)), fixed((8, 128)), fixed((1, OWN)),
        ],
        out_specs=(
            tokens(D), tokens(OWN), tokens(640), tokens(640), tokens(128), tokens(OWN), tokens(OWN),
            pl.BlockSpec((per, NS, OWN), lambda i: (i, 0, 0)), fixed((16, 128)),
        ),
        out_shape=(
            sds((LEN, D), bf16), sds((LEN, OWN)), sds((LEN, 640)), sds((LEN, 640)),
            sds((LEN, 128)), sds((LEN, OWN)), sds((LEN, OWN)), sds((BLOCKS, NS, OWN)),
            sds((16, 128)),
        ),
        scratch_shapes=[pltpu.VMEM((NS, OWN), f32), pltpu.VMEM((8, 640), f32)],
        compiler_params=pltpu.CompilerParams(vmem_limit_bytes=VMEM_LIMIT),
    )(u, ct, w, wo, gn, gg, cv, hd, sk)


def run_backward(z, xbc, cvo, raw, core, dm, st, sums, gg, cv, hd, sk):
    def tokens(columns):
        return pl.BlockSpec((BLOCK, columns), lambda i: (BLOCKS - 1 - i, 0))

    return pl.pallas_call(
        backward_kernel,
        grid=(BLOCKS,),
        in_specs=[
            tokens(OWN), tokens(640), tokens(640), tokens(128), tokens(OWN), tokens(OWN),
            pl.BlockSpec((1, NS, OWN), lambda i: (BLOCKS - 1 - i, 0, 0)),
            fixed((8, 16, 128)), fixed((1, OWN)), fixed((8, 640)), fixed((8, 128)), fixed((1, OWN)),
        ],
        out_specs=(
            tokens(COLS), tokens(OWN), fixed((8, OWN)), fixed((8, OWN)), fixed((8, 640)),
            fixed((8, 128)),
        ),
        out_shape=(
            sds((LEN, COLS), bf16), sds((LEN, OWN), bf16), sds((8, OWN)), sds((8, OWN)),
            sds((8, 640)), sds((8, 128)),
        ),
        scratch_shapes=[pltpu.VMEM((NS, OWN), f32), pltpu.VMEM((8, 640), f32)],
        compiler_params=pltpu.CompilerParams(vmem_limit_bytes=VMEM_LIMIT),
    )(z, xbc, cvo, raw, core, dm, st, sums, gg, cv, hd, sk)


def adam_update(master, first, second, gradient, rate, decay):
    first_new = beta_one * first + (1.0 - beta_one) * gradient
    second_new = beta_two * second + (1.0 - beta_two) * gradient * gradient
    scaled = (
        first_new
        / (1.0 - beta_one**STEP)
        / (jnp.sqrt(second_new / (1.0 - beta_two**STEP)) + adam_epsilon)
    )
    return (first_new, second_new, master - rate * (scaled + decay * master))


def on_device(
    hidden, cotangent, in_master, in_first, in_second, out_master, out_first, out_second,
    gain_master, gain_first, gain_second, conv_master, conv_first, conv_second,
    head_master, head_first, head_second,
):
    s = lax.axis_index("shard")
    c = lax.rem(lax.axis_index("dp"), 2)
    low = lambda v: lax.reduce_precision(v, 8, 7)
    wide = jnp.pad(in_master.astype(bf16), ((0, 0), (0, WIDE - PROJ)))
    wo = out_master.astype(bf16)
    small = jnp.concatenate(
        [low(gain_master), low(conv_master).reshape(-1), jnp.zeros((416,), f32)]
    ).reshape(24, 128)
    u, ct, w, sm = exchange(
        1, gather_body, (hidden[0], cotangent[0], wide, small),
        (
            sds((8, BLOCK, D), bf16), sds((8, BLOCK, D), bf16), sds((8, 192, COLS), bf16),
            sds((8, 24, 128)),
        ),
        42, 6,
    )
    u, ct, w = u.reshape(LEN, D), ct.reshape(LEN, D), w.reshape(D, COLS)
    sm = sm.reshape(8, 3072)
    gains = sm[:, :576].reshape(4608)
    conv_all = sm[:, 576:2656].reshape(8, 5, 416).transpose(1, 0, 2).reshape(5, CONVC)
    gn = gains[None, :D]
    gg = lax.dynamic_slice(gains, (D + OWN * s,), (OWN,))[None]
    cv = jnp.concatenate(
        [lax.dynamic_slice(conv_all, (0, OWN * s), (5, OWN)), conv_all[:, DI:]], axis=1
    )
    cv = jnp.pad(cv, ((0, 3), (0, 0)))
    heads = low(head_master)
    hd = jnp.pad(heads, ((0, 5), (0, 122)))
    sk = jnp.repeat(heads[2], HD)[None]

    normed, z, xbc, cvo, raw, core, dm, st, sums = run_forward(u, ct, w, wo, gn, gg, cv, hd, sk)
    (sums,) = exchange(2, all_body, (sums,), (sds((8, 16, 128)),), 7, 1)
    dproj, mixed, dgain, dskip, dconv, dhead = run_backward(
        z, xbc, cvo, raw, core, dm, st, sums, gg, cv, hd, sk
    )
    dgain, dskip, dconv, dhead = dgain[0], dskip[0], dconv[:5], dhead[:2, :6]
    part_out = dot(mixed, wo, 1, 0).astype(bf16).reshape(8, BLOCK, D)
    grad_o = dot(mixed, ct, 0, 0)
    grad_w = dot(normed, dproj, 0, 0)
    part_in = dot(dproj, w, 1, 1).astype(bf16).reshape(8, BLOCK, D)
    got_out, got_in = exchange(
        3, scatter_body, (part_out, part_in),
        (sds((8, BLOCK, D), bf16), sds((8, BLOCK, D), bf16)), 14, 2,
    )
    inputs = hidden[0].astype(f32)
    layer_out = (inputs + jnp.sum(got_out.astype(f32), axis=0)).astype(bf16)
    d_normed = jnp.sum(got_in.astype(f32), axis=0)
    scale = lax.rsqrt(jnp.mean(inputs * inputs, axis=-1, keepdims=True) + epsilon)
    gained = gn * d_normed
    grad_inputs = scale * gained - inputs * scale**3 * jnp.mean(
        inputs * gained, axis=-1, keepdims=True
    )
    input_grad = (cotangent[0].astype(f32) + grad_inputs).astype(bf16)
    dnorm = jnp.sum(d_normed * inputs * scale, axis=0)
    small_grad = jnp.concatenate(
        [
            dnorm, dgain, dconv[:, :OWN].reshape(-1), dconv[:, OWN:].reshape(-1),
            dhead.reshape(-1), jnp.sum(dskip.reshape(6, HD), axis=1), jnp.zeros((1006,), f32),
        ]
    ).reshape(48, 128)

    grad_w = grad_w.reshape(8, 8, 24, COLS)
    grad_o = grad_o.reshape(8, 48, D)
    swap_w, swap_o = exchange(
        4, swap_body, (grad_w, grad_o), (sds((4, 8, 24, COLS), f32), sds((8, 48, 768), f32)), 2, 0
    )
    half_w = (
        lax.dynamic_slice_in_dim(grad_w, 4 * c, 4, 0).astype(f32) + swap_w.astype(f32)
    ).astype(bf16)
    half_o = (
        lax.dynamic_slice_in_dim(grad_o, 768 * c, 768, 2).astype(f32) + swap_o.astype(f32)
    ).astype(bf16)
    got_w, got_o = exchange(
        5, reduce_body, (half_w, half_o),
        (sds((8, 4, 24, COLS), bf16), sds((8, 48, 768), bf16)), 14, 2,
    )
    piece_w = jnp.sum(got_w.astype(f32), axis=0)
    piece_o = jnp.sum(got_o.astype(f32), axis=0)
    own_w, small_all = exchange(
        6, owner_body, (piece_w, small_grad), (sds((8, 24, COLS)), sds((8, 48, 128))), 14, 2
    )
    own_w = own_w.transpose(1, 0, 2)
    slab = jnp.concatenate(
        [
            own_w[:, :, :OWN].reshape(24, DI),
            own_w[:, :, OWN : 2 * OWN].reshape(24, DI),
            jnp.sum(own_w[:, :, 2 * OWN :], axis=1),
        ],
        axis=1,
    )
    flat = small_all.reshape(8, 6144)
    g_gain = jnp.concatenate([jnp.sum(flat[:, :D], axis=0), flat[:, D : D + OWN].reshape(-1)])
    g_conv = jnp.concatenate(
        [
            flat[:, 1920:3840].reshape(8, 5, OWN).transpose(1, 0, 2).reshape(5, DI),
            jnp.sum(flat[:, 3840:5120], axis=0).reshape(5, 256),
        ],
        axis=1,
    )
    own_small = jnp.concatenate(
        [
            lax.dynamic_slice(g_gain, (576 * s,), (576,)),
            lax.dynamic_slice(g_conv, (0, 416 * s), (5, 416)).reshape(-1),
            lax.dynamic_slice(flat, (s, 5120), (1, 18))[0],
            jnp.zeros((398,), f32),
        ]
    ).reshape(24, 128)
    total_w, total_o, total_small = exchange(
        7, spread_body, (slab, piece_o, own_small),
        (sds((8, 24, WIDE)), sds((8, 48, D)), sds((16, 24, 128))), 45, 3,
    )
    total_small = jnp.sum(total_small, axis=0).reshape(-1)
    totals = (
        total_w.reshape(192, WIDE)[:, :PROJ].astype(f32),
        total_o.reshape(OWN, D).astype(f32),
        total_small[:576],
        total_small[576:2656].reshape(5, 416),
        total_small[2656:2674].reshape(3, 6),
    )
    masters = (in_master, out_master, gain_master, conv_master, head_master)
    firsts = (in_first, out_first, gain_first, conv_first, head_first)
    seconds = (in_second, out_second, gain_second, conv_second, head_second)
    updated = [
        adam_update(masters[g], firsts[g], seconds[g], totals[g], rates[g], decays[g])
        for g in range(5)
    ]
    return (layer_out[None], input_grad[None]) + tuple(v for group in updated for v in group)


def solution(mesh):
    rows, columns = P("shard", None), P(None, "shard")
    tokens = P("dp", "shard", None)
    state = (rows,) * 6 + (P("shard"),) * 3 + (columns,) * 6
    return jax.shard_map(
        on_device,
        mesh=mesh,
        in_specs=(tokens, tokens) + state,
        out_specs=(tokens, tokens) + state,
        check_vma=False,
    )
```

```python
import functools

import jax
import jax.numpy as jnp
from jax import lax
from jax.experimental import pallas as pl
from jax.experimental.pallas import tpu as pltpu
from jax.sharding import PartitionSpec as P

D = 1536
DI = 3072
H = 48
HD = 64
NS = 128
KCONV = 4
STEP = 5
BLOCK = 128
CONVC = 3328
PROJ = 6448
LEN = 1024
OWN = 384
COLS = 1152
WIDE = 6528
BLOCKS = LEN // BLOCK

f32 = jnp.float32
bf16 = jnp.bfloat16
highest = lax.Precision.HIGHEST
MESH = pl.DeviceIdType.MESH
epsilon = 1e-05
beta_one = 0.9
beta_two = 0.95
adam_epsilon = 1e-08
rates = (0.05, 0.04, 0.25, 0.5, 0.5)
decays = (0.1, 0.1, 0.0, 0.0, 0.0)
VMEM_LIMIT = 60 * 2**20


class Place:
    def __init__(self):
        self.d = lax.axis_index("dp")
        self.s = lax.axis_index("shard")
        self.c = lax.rem(self.d, 2)
        self.x = lax.rem(self.d // 2, 4)
        self.yh = self.d // 8
        self.big = self.d // 2
        self.z = lax.rem(self.s, 4)
        self.yl = self.s // 4

    def shard_of(self, k):
        return lax.rem(self.yl + k // 4, 2) * 4 + lax.rem(self.z + k % 4, 4)

    def shard_peer(self, k):
        return (self.d, self.shard_of(k))

    def big_of(self, k):
        return lax.rem(self.yh + k // 4, 2) * 4 + lax.rem(self.x + k % 4, 4)

    def big_peer(self, k):
        return (self.big_of(k) * 2 + self.c, self.s)

    def core_peer(self):
        return (self.big * 2 + 1 - self.c, self.s)

    def other_core_of(self, k):
        return (self.big_of(k) * 2 + 1 - self.c, self.s)


ORDER = (6, 2, 5, 7, 1, 3, 4)


def exchange(cid, body, ins, outs, sems, locals_):
    def kernel(*refs):
        in_refs = refs[: len(ins)]
        out_refs = refs[len(ins) : len(ins) + len(outs)]
        send, recv, own = refs[len(ins) + len(outs) :]
        place = Place()

        def meet(peers):
            barrier = pltpu.get_barrier_semaphore()
            for peer in peers:
                pl.semaphore_signal(barrier, inc=1, device_id=peer, device_id_type=MESH)
            pl.semaphore_wait(barrier, len(peers))

        def remote(src, dst, index, peer):
            return pltpu.make_async_remote_copy(
                src_ref=src,
                dst_ref=dst,
                send_sem=send.at[index],
                recv_sem=recv.at[index],
                device_id=peer,
                device_id_type=MESH,
            )

        def local(src, dst, index):
            return pltpu.make_async_copy(src, dst, own.at[index])

        body(place, meet, remote, local, in_refs, out_refs)

    any_spec = pl.BlockSpec(memory_space=pl.ANY)
    return pl.pallas_call(
        kernel,
        out_shape=outs,
        in_specs=[any_spec] * len(ins),
        out_specs=tuple([any_spec] * len(outs)),
        scratch_shapes=[
            pltpu.SemaphoreType.DMA((sems,)),
            pltpu.SemaphoreType.DMA((sems,)),
            pltpu.SemaphoreType.DMA((max(locals_, 1),)),
        ],
        compiler_params=pltpu.CompilerParams(collective_id=cid, has_side_effects=True),
    )(*ins)


def scatter_body(place, meet, remote, local, ins, outs):
    meet([place.shard_peer(k) for k in ORDER])
    copies = []
    for a in range(len(ins)):
        copies.append(local(ins[a].at[place.s], outs[a].at[place.s], a))
    for n, k in enumerate(ORDER):
        for a in range(len(ins)):
            copies.append(
                remote(
                    ins[a].at[place.shard_of(k)],
                    outs[a].at[place.s],
                    n * len(ins) + a,
                    place.shard_peer(k),
                )
            )
    for copy in copies:
        copy.start()
    for copy in copies:
        copy.wait()


def swap_body(place, meet, remote, local, ins, outs):
    gw, go = ins
    gw_out, go_out = outs
    meet([place.core_peer()])
    other = 1 - place.c
    copies = [
        remote(gw.at[pl.ds(other * 4, 4)], gw_out, 0, place.core_peer()),
        remote(
            go.at[:, :, pl.ds(pl.multiple_of(other * 768, 128), 768)],
            go_out,
            1,
            place.core_peer(),
        ),
    ]
    for copy in copies:
        copy.start()
    for copy in copies:
        copy.wait()


def reduce_body(place, meet, remote, local, ins, outs):
    hw, ho = ins
    hw_out, ho_out = outs
    meet([place.big_peer(k) for k in ORDER])
    copies = [
        local(hw.at[:, place.big], hw_out.at[0], 0),
        local(ho.at[place.big], ho_out.at[0], 1),
    ]
    for n, k in enumerate(ORDER):
        them = place.big_of(k)
        copies.append(remote(hw.at[:, them], hw_out.at[k], 2 * n, place.big_peer(k)))
        copies.append(remote(ho.at[them], ho_out.at[k], 2 * n + 1, place.big_peer(k)))
    for copy in copies:
        copy.start()
    for copy in copies:
        copy.wait()


def owner_body(place, meet, remote, local, ins, outs):
    piece, small = ins
    piece_out, small_out = outs
    meet([place.shard_peer(k) for k in ORDER])
    valid = place.yl == place.c
    own_small = local(small, small_out.at[place.s], 0)
    own_small.start()
    own_piece = local(piece.at[place.z], piece_out.at[place.s], 1)

    @pl.when(valid)
    def _():
        own_piece.start()

    smalls = [
        remote(small, small_out.at[place.s], n, place.shard_peer(k))
        for n, k in enumerate(ORDER)
    ]
    for copy in smalls:
        copy.start()
    pieces = []
    for n, k in enumerate(ORDER):
        them = place.shard_of(k)
        copy = remote(
            piece.at[lax.rem(them, 4)], piece_out.at[place.s], 7 + n, place.shard_peer(k)
        )
        goes = them // 4 == place.c
        pl.when(goes)(copy.start)
        pieces.append((copy, goes))
    own_small.wait()
    pl.when(valid)(own_piece.wait)
    for copy in smalls:
        copy.wait()
    for copy, goes in pieces:
        pl.when(goes)(copy.wait_send)
        pl.when(valid)(copy.wait_recv)


def spread_body(place, meet, remote, local, ins, outs):
    slab, go, small = ins
    slab_out, go_out, small_out = outs
    core = place.core_peer()
    everyone = [place.big_peer(k) for k in ORDER] + [core]
    everyone += [place.other_core_of(k) for k in ORDER]
    meet(everyone)
    valid = place.yl == place.c
    at = pl.multiple_of(place.c * 768, 128)

    def half(index):
        return go_out.at[index, :, pl.ds(at, 768)]

    other_at = pl.multiple_of((1 - place.c) * 768, 128)
    own_small = local(small, small_out.at[place.d], 0)
    own_go = local(go, half(place.big), 1)
    own_slab = local(slab, slab_out.at[place.big], 2)
    own_small.start()
    own_go.start()
    smalls = [
        remote(small, small_out.at[place.d], n, peer) for n, peer in enumerate(everyone)
    ]
    slabs = [
        remote(slab, slab_out.at[place.big], 15 + n, place.big_peer(k))
        for n, k in enumerate(ORDER)
    ]
    gos = [
        remote(go, half(place.big), 22 + n, place.big_peer(k)) for n, k in enumerate(ORDER)
    ]
    to_core_slab = remote(slab, slab_out.at[place.big], 29, core)
    to_core_go = remote(go, half(place.big), 30, core)

    @pl.when(valid)
    def _():
        own_slab.start()
        for copy in slabs:
            copy.start()
        to_core_slab.start()

    for copy in gos:
        copy.start()
    to_core_go.start()
    for copy in smalls:
        copy.start()
    forward_gos = []
    forward_slabs = []
    for n, k in enumerate(ORDER):
        origin = lax.rem(place.yh + k // 4, 2) * 4 + lax.rem(place.x + 4 - k % 4, 4)
        gos[n].wait_recv()
        go_copy = remote(half(origin), half(origin), 31 + n, core)
        go_copy.start()
        forward_gos.append(go_copy)
        slab_copy = remote(slab_out.at[origin], slab_out.at[origin], 38 + n, core)

        @pl.when(valid)
        def _(n=n, slab_copy=slab_copy):
            slabs[n].wait_recv()
            slab_copy.start()

        forward_slabs.append(slab_copy)
    own_small.wait()
    own_go.wait()
    for copy in smalls:
        copy.wait()
    for copy in gos:
        copy.wait_send()
    to_core_go.wait()
    for copy in forward_gos:
        copy.wait()

    @pl.when(valid)
    def _():
        own_slab.wait()
        for copy in slabs:
            copy.wait_send()
        to_core_slab.wait_send()
        for copy in forward_slabs:
            copy.wait_send()

    @pl.when(jnp.logical_not(valid))
    def _():
        to_core_slab.wait_recv()
        for copy in forward_slabs:
            copy.wait_recv()


def dot(a, b, ca, cb, precision=None):
    return lax.dot_general(
        a, b, (((ca,), (cb,)), ((), ())), precision=precision, preferred_element_type=f32
    )


def mm(a, b, ca=1, cb=0):
    return dot(a.astype(f32), b.astype(f32), ca, cb, highest)


def lanes(shape):
    return lax.broadcasted_iota(jnp.int32, shape, 1)


def rows_of(shape):
    return lax.broadcasted_iota(jnp.int32, shape, 0)


def widen(m):
    low = lanes((m.shape[0], 128)) < HD
    return jnp.concatenate(
        [jnp.where(low, m[:, 2 * i : 2 * i + 1], m[:, 2 * i + 1 : 2 * i + 2]) for i in range(3)],
        axis=1,
    )


def lower_ones():
    return (rows_of((BLOCK, BLOCK)) >= lanes((BLOCK, BLOCK))).astype(f32)


def head_ones():
    return (rows_of((OWN, BLOCK)) // HD == lanes((OWN, BLOCK))).astype(f32)


def split_pair(pair):
    low = lanes(pair.shape) < HD
    zero = jnp.zeros_like(pair)
    return jnp.concatenate([jnp.where(low, pair, zero), jnp.where(low, zero, pair)], axis=0)


def head_mixing(cumulative, turned, h):
    causal = rows_of((BLOCK, BLOCK)) >= lanes((BLOCK, BLOCK))
    differ = cumulative[:, h : h + 1] - turned[h : h + 1, :]
    return jnp.exp(jnp.where(causal, differ, -jnp.inf))


def softplus(v):
    return jnp.maximum(v, 0.0) + jnp.log1p(jnp.exp(-jnp.abs(v)))


TB = 256
HALF = DI // 8


def dot3(a, b, ca, cb):
    a_hi, b_hi = a.astype(bf16), b.astype(bf16)
    a_lo, b_lo = (a - a_hi.astype(f32)).astype(bf16), (b - b_hi.astype(f32)).astype(bf16)
    left = jnp.concatenate([a_hi, a_hi, a_lo], axis=ca)
    right = jnp.concatenate([b_hi, b_lo, b_hi], axis=cb)
    return dot(left, right, ca, cb)


def dot_exact(a, ones, ca, cb):
    a_hi = a.astype(bf16)
    a_lo = (a - a_hi.astype(f32)).astype(bf16)
    low = ones.astype(bf16)
    return dot(
        jnp.concatenate([a_hi, a_lo], axis=ca), jnp.concatenate([low, low], axis=cb), ca, cb
    )


def ones_dot(ones, a, ca, cb):
    a_hi = a.astype(bf16)
    a_lo = (a - a_hi.astype(f32)).astype(bf16)
    low = ones.astype(bf16)
    return dot(
        jnp.concatenate([low, low], axis=ca), jnp.concatenate([a_hi, a_lo], axis=cb), ca, cb
    )


def decay_parts(log_decay):
    cumulative = ones_dot(lower_ones(), log_decay, 1, 0)
    return cumulative, cumulative.T, widen(cumulative)


def forward_block(act, dt, log_decay, before):
    x, keys, query = act[:, :OWN], act[:, OWN : OWN + NS], act[:, OWN + NS :]
    cumulative, turned, wide = decay_parts(log_decay)
    contact = dot3(query, keys, 1, 1)
    scaled = x * widen(dt)
    within = []
    for p in range(3):
        pair = split_pair(scaled[:, 128 * p : 128 * p + 128])
        both = jnp.concatenate(
            [head_mixing(cumulative, turned, 2 * p + q) * contact for q in range(2)], axis=1
        )
        within.append(dot3(both, pair, 1, 0))
    last = wide[BLOCK - 1 : BLOCK, :]
    core = jnp.concatenate(within, axis=1) + dot3(query, before, 1, 0) * jnp.exp(wide)
    after = jnp.exp(last) * before + dot3(keys, scaled * jnp.exp(last - wide), 0, 0)
    return core, after


def whole_kernel(
    hid, cot, wide_ref, small, wo_ref, hd_ref, sk_ref,
    out_ref, n_ref, ct_ref, w_ref, dp_ref, mixed_ref, gn_out,
    dgain_ref, dskip_ref, dconv_ref, dhead_ref,
    sm_ref, gain_ref, conv_ref, z_ref, xbc_ref, cvo_ref, raw_ref, core_ref, y_ref, dm_ref,
    st_ref, sums_ref, got_sums, turned_sums, dcore_ref, po_ref, go_ref, own_out,
    state, halo, hid_v, send, recv, own,
):
    place = Place()
    me = place.s
    barrier = pltpu.get_barrier_semaphore()
    core_peer = place.core_peer()
    x_peers = [place.big_peer(k) for k in (1, 2, 3)]
    group = [place.shard_peer(k) for k in range(1, 8)]
    for peer in group + x_peers + [core_peer]:
        pl.semaphore_signal(barrier, inc=1, device_id=peer, device_id_type=MESH)
    pl.semaphore_wait(barrier, 11)

    def remote(src, dst, index, peer, other=None):
        return pltpu.make_async_remote_copy(
            src_ref=src,
            dst_ref=dst,
            send_sem=send.at[index],
            recv_sem=recv.at[index if other is None else other],
            device_id=peer,
            device_id_type=MESH,
        )

    quarter = pl.multiple_of(48 * place.x, 16)

    def weight_parts(them):
        at = pl.multiple_of(them * OWN, 128)
        rows = pl.ds(quarter, 48)
        return (
            (wide_ref.at[rows, pl.ds(at, OWN)], w_ref.at[me, rows, pl.ds(0, OWN)]),
            (wide_ref.at[rows, pl.ds(at + DI, OWN)], w_ref.at[me, rows, pl.ds(OWN, OWN)]),
            (wide_ref.at[rows, pl.ds(2 * DI, OWN)], w_ref.at[me, rows, pl.ds(2 * OWN, OWN)]),
        )

    locals_ = [
        pltpu.make_async_copy(small, sm_ref.at[me], own.at[0]),
        pltpu.make_async_copy(hid, n_ref.at[me], own.at[1]),
        pltpu.make_async_copy(cot, ct_ref.at[me], own.at[2]),
        pltpu.make_async_copy(hid, hid_v, own.at[3]),
    ]
    for copy in locals_:
        copy.start()
    mine = place.yl == place.c
    own_w = [
        pltpu.make_async_copy(src, dst, own.at[4 + i])
        for i, (src, dst) in enumerate(weight_parts(me))
    ]
    smalls = [remote(small, sm_ref.at[me], k, place.shard_peer(k)) for k in range(1, 8)]
    hids = [remote(hid, n_ref.at[me], 16 + k, place.shard_peer(k)) for k in range(1, 8)]
    cots = [remote(cot, ct_ref.at[me], 24 + k, place.shard_peer(k)) for k in range(1, 8)]
    weights = []
    for k in range(1, 8):
        weights.append(
            [
                remote(src, dst, 40 + 3 * k + i, place.shard_peer(k))
                for i, (src, dst) in enumerate(weight_parts(place.shard_of(k)))
            ]
        )

    @pl.when(mine)
    def _():
        for copy in own_w:
            copy.start()
        for parts in weights:
            for copy in parts:
                copy.start()

    for copy in smalls:
        copy.start()
    for copy in hids:
        copy.start()

    def from_offset(k):
        return lax.rem(place.yl + k // 4, 2)

    for k in range(1, 8):
        @pl.when(from_offset(k) == place.c)
        def _(k=k):
            for copy in weights[k - 1]:
                copy.wait_recv()

    @pl.when(mine)
    def _():
        for copy in own_w:
            copy.wait()

    def w_rows(x, c):
        return w_ref.at[pl.ds(4 * c, 4), pl.ds(pl.multiple_of(48 * x, 16), 48), :]

    w_x = [
        remote(w_rows(place.x, place.c), w_rows(place.x, place.c), 32 + k, x_peers[k - 1])
        for k in (1, 2, 3)
    ]
    for copy in w_x:
        copy.start()
    for copy in w_x:
        copy.wait_recv()
    w_half = w_ref.at[pl.ds(4 * place.c, 4)]
    w_core = remote(w_half, w_half, 36, core_peer)
    w_core.start()

    locals_[0].wait()
    for copy in smalls:
        copy.wait_recv()
    gain_ref[...] = jnp.concatenate([sm_ref[p, 5:6, :576] for p in range(8)], axis=1)
    conv_ref[...] = jnp.concatenate([sm_ref[p, :, :416] for p in range(8)], axis=1)
    gn_out[...] = gain_ref[:, :D]
    gg_at = pl.ds(pl.multiple_of(D + OWN * me, 128), OWN)
    cv_at = pl.ds(pl.multiple_of(OWN * me, 128), OWN)

    def conv_row(k):
        return jnp.concatenate([conv_ref[k : k + 1, cv_at], conv_ref[k : k + 1, DI:]], axis=1)

    locals_[1].wait()
    for copy in hids:
        copy.wait_recv()
    for copy in cots:
        copy.start()
    w_core.wait_recv()

    state[...] = jnp.zeros_like(state)
    halo[...] = jnp.zeros_like(halo)

    @pl.loop(0, LEN // TB)
    def _(i):
        two = pl.ds(2 * i, 2)
        u = n_ref[two].reshape(TB, D).astype(f32)
        scale = lax.rsqrt(jnp.mean(u * u, axis=1, keepdims=True) + epsilon)
        normed = (u * scale * gain_ref[:, :D]).astype(bf16)
        n_ref[two] = normed.reshape(2, BLOCK, D)
        project = dot(normed, w_ref[...].reshape(D, COLS), 1, 0)
        z = project[:, :OWN]
        xbc = project[:, OWN : OWN + 640]
        raw = pltpu.roll(project[:, 1024:1152], 128 - 6 * me, 1)
        z_ref[two] = z.reshape(2, BLOCK, OWN)
        xbc_ref[two] = xbc.reshape(2, BLOCK, 640)
        raw_ref[two] = raw.reshape(2, BLOCK, 128)
        extended = jnp.concatenate([halo[...], xbc], axis=0)
        halo[...] = xbc[TB - 8 :, :]
        conv = conv_row(KCONV)
        for k in range(KCONV):
            conv = conv + conv_row(k) * extended[5 + k : 5 + k + TB, :]
        cvo_ref[two] = conv.reshape(2, BLOCK, 640)
        act = conv * jax.nn.sigmoid(conv)
        dt = softplus(raw + hd_ref[0:1, :])
        log_decay = -jnp.exp(hd_ref[1:2, :]) * dt
        for j in range(TB // BLOCK):
            at = slice(j * BLOCK, (j + 1) * BLOCK)
            before = state[...]
            st_ref[2 * i + j] = before
            core, after = forward_block(act[at], dt[at], log_decay[at], before)
            state[...] = after
            core_ref[2 * i + j] = core
            y_ref[2 * i + j] = core + sk_ref[0:1, :] * act[at, :OWN]

    locals_[2].wait()
    for copy in cots:
        copy.wait_recv()

    @pl.loop(0, LEN // TB)
    def _(i):
        two = pl.ds(2 * i, 2)
        dm = dot(ct_ref[two].reshape(TB, D), wo_ref[...], 1, 1)
        dm_ref[two] = dm.reshape(2, BLOCK, OWN)
        z = z_ref[two].reshape(TB, OWN)
        gated = y_ref[two].reshape(TB, OWN) * (z * jax.nn.sigmoid(z))
        ones = jnp.ones((8, OWN), f32)
        first = ones_dot(ones, gated * gated, 1, 1)
        second = ones_dot(ones, gated * (gain_ref[:, gg_at] * dm), 1, 1)
        for j in range(2):
            sums_ref[pl.ds(2 * i + j, 1), :] = first[0:1, 128 * j : 128 * j + 128]
            sums_ref[pl.ds(2 * i + j + 8, 1), :] = second[0:1, 128 * j : 128 * j + 128]

    sums = [remote(sums_ref, got_sums.at[me], 64 + k, place.shard_peer(k)) for k in range(1, 8)]
    for copy in sums:
        copy.start()
    got_sums[me] = sums_ref[...]
    for copy in sums:
        copy.wait_recv()
    totals = got_sums[0]
    for j in range(1, 8):
        totals += got_sums[j]
    turned_sums[...] = jnp.concatenate([totals, jnp.zeros((112, 128), f32)], axis=0).T
    gain = gain_ref[:, gg_at]
    lane = lanes((BLOCK, 128))
    dgain_ref[...] = jnp.zeros_like(dgain_ref)
    dskip_ref[...] = jnp.zeros_like(dskip_ref)
    dconv_ref[...] = jnp.zeros_like(dconv_ref)
    dhead_ref[...] = jnp.zeros_like(dhead_ref)

    def out_copy(b):
        return remote(po_ref.at[b], go_ref.at[me], 72 + b, (place.d, b), 80 + me)

    @pl.loop(0, BLOCKS)
    def _(i):
        b = lax.rem(me + 1 + i, BLOCKS)
        column = turned_sums[...]
        first = jnp.sum(jnp.where(lane == b, column, 0.0), axis=1, keepdims=True)
        second = jnp.sum(jnp.where(lane == b + 8, column, 0.0), axis=1, keepdims=True)
        z, y, dm = z_ref[b], y_ref[b], dm_ref[b]
        sig_z = jax.nn.sigmoid(z)
        gate = z * sig_z
        scale = lax.rsqrt(first * (1.0 / DI) + epsilon)
        unit = y * gate * scale
        mixed = (unit * gain).astype(bf16)
        mixed_ref[b] = mixed
        dgain_ref[0:1, :] += jnp.sum(dm * unit, axis=0, keepdims=True)
        dgated = scale * (gain * dm) - unit * (scale * scale * (second * (1.0 / DI)))
        dz = dgated * y * (sig_z * (1.0 + z * (1.0 - sig_z)))
        dp_ref[b, :, :OWN] = dz.astype(bf16)
        dcore_ref[b] = dgated * gate
        part = dot(mixed, wo_ref[...], 1, 0)

        @pl.when(i < BLOCKS - 1)
        def _():
            po_ref[b] = part.astype(bf16)
            out_copy(b).start()

        @pl.when(i == BLOCKS - 1)
        def _():
            own_out[...] = part

    state[...] = jnp.zeros_like(state)
    halo[...] = jnp.zeros_like(halo)

    @pl.loop(0, BLOCKS)
    def _(i):
        b = BLOCKS - 1 - i
        conv, raw, core, dcore = cvo_ref[b], raw_ref[b], core_ref[b], dcore_ref[b]
        sig = jax.nn.sigmoid(conv)
        act = conv * sig
        x, keys, query = act[:, :OWN], act[:, OWN : OWN + NS], act[:, OWN + NS :]
        shifted = raw + hd_ref[0:1, :]
        dt = softplus(shifted)
        rate = jnp.exp(hd_ref[1:2, :])
        log_decay = -rate * dt
        dskip_ref[0:1, :] += jnp.sum(dcore * x, axis=0, keepdims=True)
        cumulative, turned, wide = decay_parts(log_decay)
        contact = dot3(query, keys, 1, 1)
        dt_wide = widen(dt)
        scaled = x * dt_wide
        dcontact = jnp.zeros((BLOCK, BLOCK), f32)
        dscaled = []
        for p in range(3):
            at = slice(128 * p, 128 * p + 128)
            mixing = [head_mixing(cumulative, turned, 2 * p + q) for q in range(2)]
            both = jnp.concatenate([m * contact for m in mixing], axis=0)
            pair = split_pair(dcore[:, at])
            dscaled.append(dot3(both, pair, 0, 0))
            dmix = dot3(pair, scaled[:, at], 1, 1)
            dcontact += dmix[:BLOCK] * mixing[0] + dmix[BLOCK:] * mixing[1]
        last = wide[BLOCK - 1 : BLOCK, :]
        before = st_ref[b]
        after_adj = state[...]
        left = jnp.exp(last - wide)
        from_core = dcore * jnp.exp(wide)
        dquery = dot3(from_core, before, 1, 1) + dot3(dcontact, keys, 1, 0)
        carried = dot3(keys, after_adj, 1, 0) * left
        dscaled = jnp.concatenate(dscaled, axis=1) + carried
        dkeys = dot3(scaled * left, after_adj, 1, 1) + dot3(dcontact, query, 0, 0)
        end = jnp.exp(last)
        state[...] = end * after_adj + dot3(query, from_core, 0, 0)
        heads = head_ones()
        last_add = dot_exact(
            jnp.sum(carried * scaled, axis=0, keepdims=True)
            + end * jnp.sum(after_adj * before, axis=0, keepdims=True),
            heads, 1, 0,
        )
        dcum = dot_exact(dcore * core - dscaled * scaled, heads, 1, 0)
        dlog = ones_dot(lower_ones(), dcum, 0, 0) + last_add
        ddt = dot_exact(dscaled * x, heads, 1, 0) - rate * dlog
        draw = ddt * jax.nn.sigmoid(shifted)
        dhead_ref[0:1, :] += jnp.sum(draw, axis=0, keepdims=True)
        dhead_ref[1:2, :] += jnp.sum(dlog * log_decay, axis=0, keepdims=True)
        dx = dscaled * dt_wide + sk_ref[0:1, :] * dcore
        dact = jnp.concatenate([dx, dkeys, dquery], axis=1)
        dconv = dact * (sig * (1.0 + conv * (1.0 - sig)))
        extended = jnp.concatenate([dconv, halo[...]], axis=0)
        halo[...] = dconv[:8, :]
        xbc = xbc_ref[b]
        dxbc = jnp.zeros_like(xbc)
        for k in range(KCONV):
            moved = extended[3 - k : 3 - k + BLOCK, :]
            dxbc += conv_row(k) * moved
            dconv_ref[k : k + 1, :] += jnp.sum(xbc * moved, axis=0, keepdims=True)
        dconv_ref[KCONV : KCONV + 1, :] += jnp.sum(dconv, axis=0, keepdims=True)
        dp_ref[b, :, OWN : OWN + 640] = dxbc.astype(bf16)
        draw_own = jnp.where(lane < 6, draw, 0.0)
        dp_ref[b, :, 1024:] = pltpu.roll(draw_own, 6 * me, 1).astype(bf16)

    locals_[3].wait()
    own_out[...] += hid_v[...].astype(f32)

    @pl.loop(1, BLOCKS)
    def _(k):
        j = lax.rem(me + k, BLOCKS)
        remote(po_ref.at[j], go_ref.at[j], 72 + j, (place.d, j), 80 + j).wait_recv()
        own_out[...] += go_ref[j].astype(f32)

    out_ref[...] = own_out[...].astype(bf16)

    for copy in smalls + hids + cots + sums + w_x + [w_core]:
        copy.wait_send()

    @pl.when(mine)
    def _():
        for parts in weights:
            for copy in parts:
                copy.wait_send()

    @pl.loop(1, BLOCKS)
    def _(k):
        out_copy(lax.rem(me + k, BLOCKS)).wait_send()


def sds(shape, dtype=f32):
    return jax.ShapeDtypeStruct(shape, dtype)


def run_whole(hid, cot, wide, small, wo, hd, sk):
    any_spec = pl.BlockSpec(memory_space=pl.ANY)
    vmem = pl.BlockSpec(memory_space=pltpu.VMEM)

    def v(*shape, dtype=f32):
        return pltpu.VMEM(shape, dtype)

    return pl.pallas_call(
        whole_kernel,
        in_specs=[any_spec] * 4 + [vmem] * 3,
        out_specs=tuple([vmem] * 11),
        out_shape=(
            sds((BLOCK, D), bf16), sds((8, BLOCK, D), bf16), sds((8, BLOCK, D), bf16),
            sds((8, 192, COLS), bf16), sds((8, BLOCK, COLS), bf16), sds((8, BLOCK, OWN), bf16),
            sds((1, D)), sds((8, OWN)), sds((8, OWN)), sds((8, 640)), sds((8, 128)),
        ),
        scratch_shapes=[
            v(8, 8, 640), v(1, 4608), v(8, CONVC), v(8, BLOCK, OWN), v(8, BLOCK, 640),
            v(8, BLOCK, 640), v(8, BLOCK, 128), v(8, BLOCK, OWN), v(8, BLOCK, OWN),
            v(8, BLOCK, OWN), v(8, NS, OWN), v(16, 128), v(8, 16, 128), v(BLOCK, 128),
            v(8, BLOCK, OWN), v(8, BLOCK, D, dtype=bf16), v(8, BLOCK, D, dtype=bf16),
            v(BLOCK, D), v(NS, OWN), v(8, 640), v(BLOCK, D, dtype=bf16),
            pltpu.SemaphoreType.DMA((88,)), pltpu.SemaphoreType.DMA((88,)),
            pltpu.SemaphoreType.DMA((7,)),
        ],
        compiler_params=pltpu.CompilerParams(
            collective_id=1, has_side_effects=True, vmem_limit_bytes=VMEM_LIMIT
        ),
    )(hid, cot, wide, small, wo, hd, sk)


def adam_update(master, first, second, gradient, rate, decay):
    first_new = beta_one * first + (1.0 - beta_one) * gradient
    second_new = beta_two * second + (1.0 - beta_two) * gradient * gradient
    scaled = (
        first_new
        / (1.0 - beta_one**STEP)
        / (jnp.sqrt(second_new / (1.0 - beta_two**STEP)) + adam_epsilon)
    )
    return (first_new, second_new, master - rate * (scaled + decay * master))


def on_device(
    hidden, cotangent, in_master, in_first, in_second, out_master, out_first, out_second,
    gain_master, gain_first, gain_second, conv_master, conv_first, conv_second,
    head_master, head_first, head_second,
):
    s = lax.axis_index("shard")
    c = lax.rem(lax.axis_index("dp"), 2)
    low = lambda v: lax.reduce_precision(v, 8, 7)
    wide = jnp.pad(in_master.astype(bf16), ((0, 0), (0, WIDE - PROJ)))
    wo = out_master.astype(bf16)
    small = jnp.concatenate(
        [
            jnp.pad(low(conv_master), ((0, 0), (0, 224))),
            jnp.pad(low(gain_master), (0, 64))[None],
            jnp.zeros((2, 640), f32),
        ],
        axis=0,
    )
    heads = low(head_master)
    hd = jnp.pad(heads, ((0, 5), (0, 122)))
    sk = jnp.repeat(heads[2], HD)[None]
    layer_out, normed, ct, w, dproj, mixed, gn, dgain, dskip, dconv, dhead = run_whole(
        hidden[0], cotangent[0], wide, small, wo, hd, sk
    )
    normed, ct, w = normed.reshape(LEN, D), ct.reshape(LEN, D), w.reshape(D, COLS)
    dproj, mixed = dproj.reshape(LEN, COLS), mixed.reshape(LEN, OWN)
    dgain, dskip, dconv, dhead = dgain[0], dskip[0], dconv[:5], dhead[:2, :6]
    grad_o = dot(mixed, ct, 0, 0)
    grad_w = dot(normed, dproj, 0, 0)
    part_in = dot(dproj, w, 1, 1).astype(bf16).reshape(8, BLOCK, D)
    (got_in,) = exchange(3, scatter_body, (part_in,), (sds((8, BLOCK, D), bf16),), 7, 1)
    inputs = hidden[0].astype(f32)
    d_normed = jnp.sum(got_in.astype(f32), axis=0)
    scale = lax.rsqrt(jnp.mean(inputs * inputs, axis=-1, keepdims=True) + epsilon)
    gained = gn * d_normed
    grad_inputs = scale * gained - inputs * scale**3 * jnp.mean(
        inputs * gained, axis=-1, keepdims=True
    )
    input_grad = (cotangent[0].astype(f32) + grad_inputs).astype(bf16)
    dnorm = jnp.sum(d_normed * inputs * scale, axis=0)
    small_grad = jnp.concatenate(
        [
            dnorm, dgain, dconv[:, :OWN].reshape(-1), dconv[:, OWN:].reshape(-1),
            dhead.reshape(-1), jnp.sum(dskip.reshape(6, HD), axis=1), jnp.zeros((1006,), f32),
        ]
    ).reshape(48, 128)

    grad_w = grad_w.reshape(8, 8, 24, COLS)
    grad_o = grad_o.reshape(8, 48, D)
    swap_w, swap_o = exchange(
        4, swap_body, (grad_w, grad_o), (sds((4, 8, 24, COLS), f32), sds((8, 48, 768), f32)), 2, 0
    )
    half_w = (
        lax.dynamic_slice_in_dim(grad_w, 4 * c, 4, 0).astype(f32) + swap_w.astype(f32)
    ).astype(bf16)
    half_o = (
        lax.dynamic_slice_in_dim(grad_o, 768 * c, 768, 2).astype(f32) + swap_o.astype(f32)
    ).astype(bf16)
    got_w, got_o = exchange(
        5, reduce_body, (half_w, half_o),
        (sds((8, 4, 24, COLS), bf16), sds((8, 48, 768), bf16)), 14, 2,
    )
    piece_w = jnp.sum(got_w.astype(f32), axis=0)
    piece_o = jnp.sum(got_o.astype(f32), axis=0)
    own_w, small_all = exchange(
        6, owner_body, (piece_w, small_grad), (sds((8, 24, COLS)), sds((8, 48, 128))), 14, 2
    )
    own_w = own_w.transpose(1, 0, 2)
    slab = jnp.concatenate(
        [
            own_w[:, :, :OWN].reshape(24, DI),
            own_w[:, :, OWN : 2 * OWN].reshape(24, DI),
            jnp.sum(own_w[:, :, 2 * OWN :], axis=1),
        ],
        axis=1,
    )
    flat = small_all.reshape(8, 6144)
    g_gain = jnp.concatenate([jnp.sum(flat[:, :D], axis=0), flat[:, D : D + OWN].reshape(-1)])
    g_conv = jnp.concatenate(
        [
            flat[:, 1920:3840].reshape(8, 5, OWN).transpose(1, 0, 2).reshape(5, DI),
            jnp.sum(flat[:, 3840:5120], axis=0).reshape(5, 256),
        ],
        axis=1,
    )
    own_small = jnp.concatenate(
        [
            lax.dynamic_slice(g_gain, (576 * s,), (576,)),
            lax.dynamic_slice(g_conv, (0, 416 * s), (5, 416)).reshape(-1),
            lax.dynamic_slice(flat, (s, 5120), (1, 18))[0],
            jnp.zeros((398,), f32),
        ]
    ).reshape(24, 128)
    total_w, total_o, total_small = exchange(
        7, spread_body, (slab, piece_o, own_small),
        (sds((8, 24, WIDE)), sds((8, 48, D)), sds((16, 24, 128))), 45, 3,
    )
    total_small = jnp.sum(total_small, axis=0).reshape(-1)
    totals = (
        total_w.reshape(192, WIDE)[:, :PROJ].astype(f32),
        total_o.reshape(OWN, D).astype(f32),
        total_small[:576],
        total_small[576:2656].reshape(5, 416),
        total_small[2656:2674].reshape(3, 6),
    )
    masters = (in_master, out_master, gain_master, conv_master, head_master)
    firsts = (in_first, out_first, gain_first, conv_first, head_first)
    seconds = (in_second, out_second, gain_second, conv_second, head_second)
    updated = [
        adam_update(masters[g], firsts[g], seconds[g], totals[g], rates[g], decays[g])
        for g in range(5)
    ]
    return (layer_out[None], input_grad[None]) + tuple(v for group in updated for v in group)


def solution(mesh):
    rows, columns = P("shard", None), P(None, "shard")
    tokens = P("dp", "shard", None)
    state = (rows,) * 6 + (P("shard"),) * 3 + (columns,) * 6
    return jax.shard_map(
        on_device,
        mesh=mesh,
        in_specs=(tokens, tokens) + state,
        out_specs=(tokens, tokens) + state,
        check_vma=False,
    )
```

```python
import functools

import jax
import jax.numpy as jnp
from jax import lax
from jax.experimental import pallas as pl
from jax.experimental.pallas import tpu as pltpu
from jax.sharding import PartitionSpec as P

D = 1536
DI = 3072
H = 48
HD = 64
NS = 128
KCONV = 4
STEP = 5
BLOCK = 128
CONVC = 3328
PROJ = 6448
LEN = 1024
OWN = 384
COLS = 1152
WIDE = 6528
BLOCKS = LEN // BLOCK

f32 = jnp.float32
bf16 = jnp.bfloat16
highest = lax.Precision.HIGHEST
MESH = pl.DeviceIdType.MESH
epsilon = 1e-05
beta_one = 0.9
beta_two = 0.95
adam_epsilon = 1e-08
rates = (0.05, 0.04, 0.25, 0.5, 0.5)
decays = (0.1, 0.1, 0.0, 0.0, 0.0)
VMEM_LIMIT = 60 * 2**20


class Place:
    def __init__(self):
        self.d = lax.axis_index("dp")
        self.s = lax.axis_index("shard")
        self.c = lax.rem(self.d, 2)
        self.x = lax.rem(self.d // 2, 4)
        self.yh = self.d // 8
        self.big = self.d // 2
        self.z = lax.rem(self.s, 4)
        self.yl = self.s // 4

    def shard_of(self, k):
        return lax.rem(self.yl + k // 4, 2) * 4 + lax.rem(self.z + k % 4, 4)

    def shard_peer(self, k):
        return (self.d, self.shard_of(k))

    def big_of(self, k):
        return lax.rem(self.yh + k // 4, 2) * 4 + lax.rem(self.x + k % 4, 4)

    def big_peer(self, k):
        return (self.big_of(k) * 2 + self.c, self.s)

    def core_peer(self):
        return (self.big * 2 + 1 - self.c, self.s)

    def other_core_of(self, k):
        return (self.big_of(k) * 2 + 1 - self.c, self.s)


ORDER = (6, 2, 5, 7, 1, 3, 4)


def exchange(cid, body, ins, outs, sems, locals_):
    def kernel(*refs):
        in_refs = refs[: len(ins)]
        out_refs = refs[len(ins) : len(ins) + len(outs)]
        send, recv, own = refs[len(ins) + len(outs) :]
        place = Place()

        def meet(peers):
            barrier = pltpu.get_barrier_semaphore()
            for peer in peers:
                pl.semaphore_signal(barrier, inc=1, device_id=peer, device_id_type=MESH)
            pl.semaphore_wait(barrier, len(peers))

        def remote(src, dst, index, peer):
            return pltpu.make_async_remote_copy(
                src_ref=src,
                dst_ref=dst,
                send_sem=send.at[index],
                recv_sem=recv.at[index],
                device_id=peer,
                device_id_type=MESH,
            )

        def local(src, dst, index):
            return pltpu.make_async_copy(src, dst, own.at[index])

        body(place, meet, remote, local, in_refs, out_refs)

    any_spec = pl.BlockSpec(memory_space=pl.ANY)
    return pl.pallas_call(
        kernel,
        out_shape=outs,
        in_specs=[any_spec] * len(ins),
        out_specs=tuple([any_spec] * len(outs)),
        scratch_shapes=[
            pltpu.SemaphoreType.DMA((sems,)),
            pltpu.SemaphoreType.DMA((sems,)),
            pltpu.SemaphoreType.DMA((max(locals_, 1),)),
        ],
        compiler_params=pltpu.CompilerParams(collective_id=cid, has_side_effects=True),
    )(*ins)


def spread_body(place, meet, remote, local, ins, outs):
    slab, go, small = ins
    slab_out, go_out, small_out = outs
    core = place.core_peer()
    everyone = [place.big_peer(k) for k in ORDER] + [core]
    everyone += [place.other_core_of(k) for k in ORDER]
    meet(everyone)
    valid = place.yl == place.c
    at = pl.multiple_of(place.c * 768, 128)

    def half(index):
        return go_out.at[index, :, pl.ds(at, 768)]

    other_at = pl.multiple_of((1 - place.c) * 768, 128)
    own_small = local(small, small_out.at[place.d], 0)
    own_go = local(go, half(place.big), 1)
    own_slab = local(slab, slab_out.at[place.big], 2)
    own_small.start()
    own_go.start()
    smalls = [
        remote(small, small_out.at[place.d], n, peer) for n, peer in enumerate(everyone)
    ]
    slabs = [
        remote(slab, slab_out.at[place.big], 15 + n, place.big_peer(k))
        for n, k in enumerate(ORDER)
    ]
    gos = [
        remote(go, half(place.big), 22 + n, place.big_peer(k)) for n, k in enumerate(ORDER)
    ]
    to_core_slab = remote(slab, slab_out.at[place.big], 29, core)
    to_core_go = remote(go, half(place.big), 30, core)

    @pl.when(valid)
    def _():
        own_slab.start()
        for copy in slabs:
            copy.start()
        to_core_slab.start()

    for copy in gos:
        copy.start()
    to_core_go.start()
    for copy in smalls:
        copy.start()
    forward_gos = []
    forward_slabs = []
    for n, k in enumerate(ORDER):
        origin = lax.rem(place.yh + k // 4, 2) * 4 + lax.rem(place.x + 4 - k % 4, 4)
        gos[n].wait_recv()
        go_copy = remote(half(origin), half(origin), 31 + n, core)
        go_copy.start()
        forward_gos.append(go_copy)
        slab_copy = remote(slab_out.at[origin], slab_out.at[origin], 38 + n, core)

        @pl.when(valid)
        def _(n=n, slab_copy=slab_copy):
            slabs[n].wait_recv()
            slab_copy.start()

        forward_slabs.append(slab_copy)
    own_small.wait()
    own_go.wait()
    for copy in smalls:
        copy.wait()
    for copy in gos:
        copy.wait_send()
    to_core_go.wait()
    for copy in forward_gos:
        copy.wait()

    @pl.when(valid)
    def _():
        own_slab.wait()
        for copy in slabs:
            copy.wait_send()
        to_core_slab.wait_send()
        for copy in forward_slabs:
            copy.wait_send()

    @pl.when(jnp.logical_not(valid))
    def _():
        to_core_slab.wait_recv()
        for copy in forward_slabs:
            copy.wait_recv()


def dot(a, b, ca, cb, precision=None):
    return lax.dot_general(
        a, b, (((ca,), (cb,)), ((), ())), precision=precision, preferred_element_type=f32
    )


def mm(a, b, ca=1, cb=0):
    return dot(a.astype(f32), b.astype(f32), ca, cb, highest)


def lanes(shape):
    return lax.broadcasted_iota(jnp.int32, shape, 1)


def rows_of(shape):
    return lax.broadcasted_iota(jnp.int32, shape, 0)


def widen(m):
    low = lanes((m.shape[0], 128)) < HD
    return jnp.concatenate(
        [jnp.where(low, m[:, 2 * i : 2 * i + 1], m[:, 2 * i + 1 : 2 * i + 2]) for i in range(3)],
        axis=1,
    )


def lower_ones():
    return (rows_of((BLOCK, BLOCK)) >= lanes((BLOCK, BLOCK))).astype(f32)


def head_ones():
    return (rows_of((OWN, BLOCK)) // HD == lanes((OWN, BLOCK))).astype(f32)


def split_pair(pair):
    low = lanes(pair.shape) < HD
    zero = jnp.zeros_like(pair)
    return jnp.concatenate([jnp.where(low, pair, zero), jnp.where(low, zero, pair)], axis=0)


def head_mixing(cumulative, turned, h):
    causal = rows_of((BLOCK, BLOCK)) >= lanes((BLOCK, BLOCK))
    differ = cumulative[:, h : h + 1] - turned[h : h + 1, :]
    return jnp.exp(jnp.where(causal, differ, -jnp.inf))


def softplus(v):
    return jnp.maximum(v, 0.0) + jnp.log1p(jnp.exp(-jnp.abs(v)))


TB = 256
HALF = DI // 8


def dot3(a, b, ca, cb):
    a_hi, b_hi = a.astype(bf16), b.astype(bf16)
    a_lo, b_lo = (a - a_hi.astype(f32)).astype(bf16), (b - b_hi.astype(f32)).astype(bf16)
    left = jnp.concatenate([a_hi, a_hi, a_lo], axis=ca)
    right = jnp.concatenate([b_hi, b_lo, b_hi], axis=cb)
    return dot(left, right, ca, cb)


def dot_exact(a, ones, ca, cb):
    a_hi = a.astype(bf16)
    a_lo = (a - a_hi.astype(f32)).astype(bf16)
    low = ones.astype(bf16)
    return dot(
        jnp.concatenate([a_hi, a_lo], axis=ca), jnp.concatenate([low, low], axis=cb), ca, cb
    )


def ones_dot(ones, a, ca, cb):
    a_hi = a.astype(bf16)
    a_lo = (a - a_hi.astype(f32)).astype(bf16)
    low = ones.astype(bf16)
    return dot(
        jnp.concatenate([low, low], axis=ca), jnp.concatenate([a_hi, a_lo], axis=cb), ca, cb
    )


def decay_parts(log_decay):
    cumulative = ones_dot(lower_ones(), log_decay, 1, 0)
    return cumulative, cumulative.T, widen(cumulative)


def two_blocks(ref, i, columns):
    return ref[i, :, :, :columns].reshape(TB, columns)


def block_of(ref, b, columns):
    four = pl.ds(4 * lax.rem(b, 2), 4)
    return ref[b // 2, four, :, :columns].reshape(BLOCK, columns)


def forward_block(act, dt, log_decay, before):
    x, keys, query = act[:, :OWN], act[:, OWN : OWN + NS], act[:, OWN + NS :]
    cumulative, turned, wide = decay_parts(log_decay)
    contact = dot3(query, keys, 1, 1)
    scaled = x * widen(dt)
    within = []
    for p in range(3):
        pair = split_pair(scaled[:, 128 * p : 128 * p + 128])
        both = jnp.concatenate(
            [head_mixing(cumulative, turned, 2 * p + q) * contact for q in range(2)], axis=1
        )
        within.append(dot3(both, pair, 1, 0))
    last = wide[BLOCK - 1 : BLOCK, :]
    core = jnp.concatenate(within, axis=1) + dot3(query, before, 1, 0) * jnp.exp(wide)
    after = jnp.exp(last) * before + dot3(keys, scaled * jnp.exp(last - wide), 0, 0)
    return core, after


def whole_kernel(
    hid, cot, in_ref, out_w, small, hd_ref,
    out_ref, igrad_ref, slab_ref, piece_o_ref, sg_all,
    n_ref, ct_ref, w_ref, z_ref, big_a, big_b, raw_ref, core_ref, y_ref, dm_ref, st_ref, dcore_ref,
    dp_ref, mixed_ref, po_ref, go_ref, own_out, wo_f, wq_f, wq, wo_ref, sm_ref, gain_ref, conv_ref,
    sums_ref, got_sums, turned_sums, rz, ro, own_o, gz, gro, rx, gx, gi_ref, own_dn,
    piece, ow, sg, dgain_ref, dskip_ref, dconv_ref, dhead_ref,
    state, halo, hid_v, cot_v, send, recv, own,
):
    place = Place()
    me = place.s
    wq_load = pltpu.make_async_copy(
        in_ref.at[pl.ds(pl.multiple_of(48 * place.x, 8), 48), :], wq_f, own.at[7]
    )
    wq_load.start()
    wq[:, WIDE - 128 :] = jnp.zeros((48, 128), bf16)
    barrier = pltpu.get_barrier_semaphore()
    core_peer = place.core_peer()
    bigs = [place.big_peer(k) for k in range(1, 8)]
    x_peers = bigs[:3]
    group = [place.shard_peer(k) for k in range(1, 8)]
    for peer in group + bigs + [core_peer]:
        pl.semaphore_signal(barrier, inc=1, device_id=peer, device_id_type=MESH)
    pl.semaphore_wait(barrier, 15)

    def remote(src, dst, index, peer, other=None):
        return pltpu.make_async_remote_copy(
            src_ref=src,
            dst_ref=dst,
            send_sem=send.at[index],
            recv_sem=recv.at[index if other is None else other],
            device_id=peer,
            device_id_type=MESH,
        )

    quarter = pl.multiple_of(48 * place.x, 16)

    def weight_parts(them):
        at = pl.multiple_of(them * OWN, 128)
        rows = pl.ds(quarter, 48)
        return (
            (wq.at[:, pl.ds(at, OWN)], w_ref.at[me, rows, pl.ds(0, OWN)]),
            (wq.at[:, pl.ds(at + DI, OWN)], w_ref.at[me, rows, pl.ds(OWN, OWN)]),
            (wq.at[:, pl.ds(2 * DI, OWN)], w_ref.at[me, rows, pl.ds(2 * OWN, OWN)]),
        )

    locals_ = [
        pltpu.make_async_copy(small, sm_ref.at[me], own.at[0]),
        pltpu.make_async_copy(hid, n_ref.at[me], own.at[1]),
        pltpu.make_async_copy(cot, ct_ref.at[me], own.at[2]),
        pltpu.make_async_copy(hid, hid_v, own.at[3]),
        pltpu.make_async_copy(cot, cot_v, own.at[14]),
    ]
    for copy in locals_:
        copy.start()
    mine = place.yl == place.c
    wo_parts = [
        pltpu.make_async_copy(
            out_w.at[pl.ds(BLOCK * (p % 3), BLOCK), pl.ds(768 * (p // 3), 768)],
            wo_f.at[p],
            own.at[8 + p],
        )
        for p in range(6)
    ]
    for copy in wo_parts:
        copy.start()
    wq_load.wait()
    wq[:, :PROJ] = wq_f[...].astype(bf16)
    own_w = [
        pltpu.make_async_copy(src, dst, own.at[4 + i])
        for i, (src, dst) in enumerate(weight_parts(me))
    ]
    smalls = [remote(small, sm_ref.at[me], k, place.shard_peer(k)) for k in range(1, 8)]
    hids = [remote(hid, n_ref.at[me], 16 + k, place.shard_peer(k)) for k in range(1, 8)]
    cots = [remote(cot, ct_ref.at[me], 24 + k, place.shard_peer(k)) for k in range(1, 8)]
    weights = []
    for k in range(1, 8):
        weights.append(
            [
                remote(src, dst, 40 + 3 * k + i, place.shard_peer(k))
                for i, (src, dst) in enumerate(weight_parts(place.shard_of(k)))
            ]
        )

    @pl.when(mine)
    def _():
        for copy in own_w:
            copy.start()
        for parts in weights:
            for copy in parts:
                copy.start()

    for copy in smalls:
        copy.start()
    for copy in hids:
        copy.start()

    def from_offset(k):
        return lax.rem(place.yl + k // 4, 2)

    for k in range(1, 8):
        @pl.when(from_offset(k) == place.c)
        def _(k=k):
            for copy in weights[k - 1]:
                copy.wait_recv()

    @pl.when(mine)
    def _():
        for copy in own_w:
            copy.wait()

    def w_rows(x, c):
        return w_ref.at[pl.ds(4 * c, 4), pl.ds(pl.multiple_of(48 * x, 16), 48), :]

    w_x = [
        remote(w_rows(place.x, place.c), w_rows(place.x, place.c), 32 + k, x_peers[k - 1])
        for k in (1, 2, 3)
    ]
    for copy in w_x:
        copy.start()
    for copy in w_x:
        copy.wait_recv()
    w_half = w_ref.at[pl.ds(4 * place.c, 4)]
    w_core = remote(w_half, w_half, 36, core_peer)
    w_core.start()

    locals_[0].wait()
    for copy in smalls:
        copy.wait_recv()
    gain_ref[...] = jnp.concatenate([sm_ref[p, 5:6, :576] for p in range(8)], axis=1)
    conv_ref[...] = jnp.concatenate([sm_ref[p, :, :416] for p in range(8)], axis=1)
    gg_at = pl.ds(pl.multiple_of(D + OWN * me, 128), OWN)
    cv_at = pl.ds(pl.multiple_of(OWN * me, 128), OWN)

    def conv_row(k):
        return jnp.concatenate([conv_ref[k : k + 1, cv_at], conv_ref[k : k + 1, DI:]], axis=1)

    locals_[1].wait()
    for copy in hids:
        copy.wait_recv()
    for copy in cots:
        copy.start()
    w_core.wait_recv()

    for copy in wo_parts:
        copy.wait()
    for p in range(6):
        at = 768 * (p // 3)
        wo_ref[BLOCK * (p % 3) : BLOCK * (p % 3 + 1), at : at + 768] = wo_f[p].astype(bf16)
    state[...] = jnp.zeros_like(state)
    halo[...] = jnp.zeros_like(halo)
    skip = hd_ref[3:4, :]

    @pl.loop(0, LEN // TB)
    def _(i):
        two = pl.ds(2 * i, 2)
        u = n_ref[two].reshape(TB, D).astype(f32)
        scale = lax.rsqrt(jnp.mean(u * u, axis=1, keepdims=True) + epsilon)
        normed = (u * scale * gain_ref[:, :D]).astype(bf16)
        n_ref[two] = normed.reshape(2, BLOCK, D)
        project = dot(normed, w_ref[...].reshape(D, COLS), 1, 0)
        z = project[:, :OWN]
        xbc = project[:, OWN : OWN + 640]
        raw = pltpu.roll(project[:, 1024:1152], 128 - 6 * me, 1)
        z_ref[i] = z.reshape(8, 32, OWN)
        big_a[i, :, :, :640] = xbc.reshape(8, 32, 640)
        raw_ref[two] = raw.reshape(2, BLOCK, 128)
        extended = jnp.concatenate([halo[...], xbc], axis=0)
        halo[...] = xbc[TB - 8 :, :]
        conv = conv_row(KCONV)
        for k in range(KCONV):
            conv = conv + conv_row(k) * extended[5 + k : 5 + k + TB, :]
        big_b[i, :, :, :640] = conv.reshape(8, 32, 640)
        act = conv * jax.nn.sigmoid(conv)
        dt = softplus(raw + hd_ref[0:1, :128])
        log_decay = -jnp.exp(hd_ref[1:2, :128]) * dt
        for j in range(TB // BLOCK):
            at = slice(j * BLOCK, (j + 1) * BLOCK)
            before = state[...]
            st_ref[2 * i + j] = before
            core, after = forward_block(act[at], dt[at], log_decay[at], before)
            state[...] = after
            core_ref[2 * i + j] = core
            y_ref[i, 4 * j : 4 * j + 4] = (core + skip * act[at, :OWN]).reshape(4, 32, OWN)

    locals_[2].wait()
    for copy in cots:
        copy.wait_recv()

    @pl.loop(0, LEN // TB)
    def _(i):
        two = pl.ds(2 * i, 2)
        dm = dot(ct_ref[two].reshape(TB, D), wo_ref[...], 1, 1)
        dm_ref[i] = dm.reshape(8, 32, OWN)
        z = two_blocks(z_ref, i, OWN)
        gated = two_blocks(y_ref, i, OWN) * (z * jax.nn.sigmoid(z))
        ones = jnp.ones((8, OWN), f32)
        first = ones_dot(ones, gated * gated, 1, 1)
        second = ones_dot(ones, gated * (gain_ref[:, gg_at] * dm), 1, 1)
        for j in range(2):
            sums_ref[pl.ds(2 * i + j, 1), :] = first[0:1, 128 * j : 128 * j + 128]
            sums_ref[pl.ds(2 * i + j + 8, 1), :] = second[0:1, 128 * j : 128 * j + 128]

    sums = [remote(sums_ref, got_sums.at[me], 64 + k, place.shard_peer(k)) for k in range(1, 8)]
    for copy in sums:
        copy.start()
    got_sums[me] = sums_ref[...]
    for copy in sums:
        copy.wait_recv()
    totals = got_sums[0]
    for j in range(1, 8):
        totals += got_sums[j]
    turned_sums[...] = jnp.concatenate([totals, jnp.zeros((112, 128), f32)], axis=0).T
    gain = gain_ref[:, gg_at]
    lane = lanes((BLOCK, 128))
    dgain_ref[...] = jnp.zeros_like(dgain_ref)
    dskip_ref[...] = jnp.zeros_like(dskip_ref)
    dconv_ref[...] = jnp.zeros_like(dconv_ref)
    dhead_ref[...] = jnp.zeros_like(dhead_ref)

    def out_copy(b):
        return remote(po_ref.at[b], go_ref.at[me], 72 + b, (place.d, b), 80 + me)

    @pl.loop(0, BLOCKS)
    def _(i):
        b = lax.rem(me + 1 + i, BLOCKS)
        column = turned_sums[...]
        first = jnp.sum(jnp.where(lane == b, column, 0.0), axis=1, keepdims=True)
        second = jnp.sum(jnp.where(lane == b + 8, column, 0.0), axis=1, keepdims=True)
        z, y, dm = block_of(z_ref, b, OWN), block_of(y_ref, b, OWN), block_of(dm_ref, b, OWN)
        sig_z = jax.nn.sigmoid(z)
        gate = z * sig_z
        scale = lax.rsqrt(first * (1.0 / DI) + epsilon)
        unit = y * gate * scale
        mixed = (unit * gain).astype(bf16)
        mixed_ref[b] = mixed
        dgain_ref[0:1, :] += jnp.sum(dm * unit, axis=0, keepdims=True)
        dgated = scale * (gain * dm) - unit * (scale * scale * (second * (1.0 / DI)))
        dz = dgated * y * (sig_z * (1.0 + z * (1.0 - sig_z)))
        dp_ref[b, :, :OWN] = dz.astype(bf16)
        dcore_ref[b] = dgated * gate
        part = dot(mixed, wo_ref[...], 1, 0)

        @pl.when(i < BLOCKS - 1)
        def _():
            po_ref[b] = part.astype(bf16)
            out_copy(b).start()

        @pl.when(i == BLOCKS - 1)
        def _():
            own_out[...] = part

    def weight_grad(q, columns):
        left = n_ref[:, :, pl.ds(pl.multiple_of(384 * q, 128), 384)].reshape(LEN, 384)
        return dot(left, dp_ref[:, :, columns].reshape(LEN, -1), 0, 0)

    def out_grad(h, q):
        at = pl.multiple_of(768 * h + 384 * q, 128)
        return dot(mixed_ref[...].reshape(LEN, OWN), ct_ref[:, :, pl.ds(at, 384)].reshape(LEN, 384), 0, 0)

    other = 1 - place.c
    zs = slice(0, OWN)
    late = slice(OWN, COLS)

    def rows24(ref):
        return ref.at[:, :, pl.ds(0, 24), :]

    @pl.loop(0, 2)
    def _(q):
        two = pl.ds(2 * q, 2)
        y_ref[two, :, :24, :] = weight_grad(2 * other + q, zs).reshape(2, 8, 24, OWN)
        z_ref[two, :, :24, :] = out_grad(other, q).reshape(2, 8, 24, OWN)

    swap_z = remote(rows24(y_ref), rz, 88, core_peer)
    swap_o = remote(rows24(z_ref), ro, 89, core_peer)
    swap_z.start()
    swap_o.start()

    @pl.loop(0, 2)
    def _(q):
        two = pl.ds(2 * q, 2)
        dm_ref[two, :, :24, :] = weight_grad(2 * place.c + q, zs).reshape(2, 8, 24, OWN)
        own_o[two] = out_grad(place.c, q).reshape(2, 8, 24, OWN)

    me_big = place.big
    g2z, g2o, g2x = [], [], []
    for k in range(1, 8):
        them, peer = place.big_of(k), bigs[k - 1]
        g2z.append(remote(dm_ref.at[:, them, pl.ds(0, 24), :], gz.at[me_big], 92 + k, peer))
        g2x.append(remote(big_b.at[:, them, pl.ds(0, 24), :], gx.at[me_big], 108 + k, peer))
        for q in range(2):
            rows = own_o.at[2 * q + them // 4, pl.ds(2 * lax.rem(them, 4), 2)]
            g2o.append(remote(rows, gro.at[me_big, q], (100 if q else 148) + k, peer))

    state[...] = jnp.zeros_like(state)
    halo[...] = jnp.zeros_like(halo)

    @pl.loop(0, BLOCKS)
    def _(i):
        b = BLOCKS - 1 - i

        @pl.when(i == 2)
        def _():
            swap_z.wait_recv()
            swap_o.wait_recv()
            for r in range(4):
                dm_ref[r, :, :24, :] += rz[r]
                own_o[r] += ro[r]
            for copy in g2z + g2o:
                copy.start()
            gz[me_big] = dm_ref[:, me_big, :24, :]
            for q in range(2):
                gro[me_big, q] = own_o[
                    2 * q + me_big // 4, pl.ds(2 * lax.rem(me_big, 4), 2)
                ]

        conv = block_of(big_b, b, 640)
        raw, core, dcore = raw_ref[b], core_ref[b], dcore_ref[b]
        sig = jax.nn.sigmoid(conv)
        act = conv * sig
        x, keys, query = act[:, :OWN], act[:, OWN : OWN + NS], act[:, OWN + NS :]
        shifted = raw + hd_ref[0:1, :128]
        dt = softplus(shifted)
        rate = jnp.exp(hd_ref[1:2, :128])
        log_decay = -rate * dt
        dskip_ref[0:1, :] += jnp.sum(dcore * x, axis=0, keepdims=True)
        cumulative, turned, wide = decay_parts(log_decay)
        contact = dot3(query, keys, 1, 1)
        dt_wide = widen(dt)
        scaled = x * dt_wide
        dcontact = jnp.zeros((BLOCK, BLOCK), f32)
        dscaled = []
        for p in range(3):
            at = slice(128 * p, 128 * p + 128)
            mixing = [head_mixing(cumulative, turned, 2 * p + q) for q in range(2)]
            both = jnp.concatenate([m * contact for m in mixing], axis=0)
            pair = split_pair(dcore[:, at])
            dscaled.append(dot3(both, pair, 0, 0))
            dmix = dot3(pair, scaled[:, at], 1, 1)
            dcontact += dmix[:BLOCK] * mixing[0] + dmix[BLOCK:] * mixing[1]
        last = wide[BLOCK - 1 : BLOCK, :]
        before = st_ref[b]
        after_adj = state[...]
        left = jnp.exp(last - wide)
        from_core = dcore * jnp.exp(wide)
        dquery = dot3(from_core, before, 1, 1) + dot3(dcontact, keys, 1, 0)
        carried = dot3(keys, after_adj, 1, 0) * left
        dscaled = jnp.concatenate(dscaled, axis=1) + carried
        dkeys = dot3(scaled * left, after_adj, 1, 1) + dot3(dcontact, query, 0, 0)
        end = jnp.exp(last)
        state[...] = end * after_adj + dot3(query, from_core, 0, 0)
        heads = head_ones()
        last_add = dot_exact(
            jnp.sum(carried * scaled, axis=0, keepdims=True)
            + end * jnp.sum(after_adj * before, axis=0, keepdims=True),
            heads, 1, 0,
        )
        dcum = dot_exact(dcore * core - dscaled * scaled, heads, 1, 0)
        dlog = ones_dot(lower_ones(), dcum, 0, 0) + last_add
        ddt = dot_exact(dscaled * x, heads, 1, 0) - rate * dlog
        draw = ddt * jax.nn.sigmoid(shifted)
        dhead_ref[0:1, :] += jnp.sum(draw, axis=0, keepdims=True)
        dhead_ref[1:2, :] += jnp.sum(dlog * log_decay, axis=0, keepdims=True)
        dx = dscaled * dt_wide + skip * dcore
        dact = jnp.concatenate([dx, dkeys, dquery], axis=1)
        dconv = dact * (sig * (1.0 + conv * (1.0 - sig)))
        extended = jnp.concatenate([dconv, halo[...]], axis=0)
        halo[...] = dconv[:8, :]
        xbc = block_of(big_a, b, 640)
        dxbc = jnp.zeros_like(xbc)
        for k in range(KCONV):
            moved = extended[3 - k : 3 - k + BLOCK, :]
            dxbc += conv_row(k) * moved
            dconv_ref[k : k + 1, :] += jnp.sum(xbc * moved, axis=0, keepdims=True)
        dconv_ref[KCONV : KCONV + 1, :] += jnp.sum(dconv, axis=0, keepdims=True)
        dp_ref[b, :, OWN : OWN + 640] = dxbc.astype(bf16)
        draw_own = jnp.where(lane < 6, draw, 0.0)
        dp_ref[b, :, 1024:] = pltpu.roll(draw_own, 6 * me, 1).astype(bf16)

    @pl.loop(0, 2)
    def _(q):
        two = pl.ds(2 * q, 2)
        big_a[two, :, :24, :] = weight_grad(2 * other + q, late).reshape(2, 8, 24, 768)

    swap_x = remote(rows24(big_a), rx, 90, core_peer)
    swap_x.start()

    @pl.loop(0, 2)
    def _(q):
        two = pl.ds(2 * q, 2)
        big_b[two, :, :24, :] = weight_grad(2 * place.c + q, late).reshape(2, 8, 24, 768)

    def in_copy(b):
        return remote(ct_ref.at[b], gi_ref.at[me], 116 + b, (place.d, b), 124 + me)

    @pl.loop(0, BLOCKS)
    def _(i):
        b = lax.rem(me + 1 + i, BLOCKS)
        part = dot(dp_ref[b], w_ref[...].reshape(D, COLS), 1, 1)

        @pl.when(i < BLOCKS - 1)
        def _():
            ct_ref[b] = part.astype(bf16)
            in_copy(b).start()

        @pl.when(i == BLOCKS - 1)
        def _():
            own_dn[...] = part

    swap_x.wait_recv()
    for r in range(4):
        big_b[r, :, :24, :] += rx[r]
    for copy in g2x:
        copy.start()
    gx[me_big] = big_b[:, me_big, :24, :]

    for copy in g2z + g2o:
        copy.wait_recv()
    total = gz[0]
    total_o = gro[0]
    for j in range(1, 8):
        total += gz[j]
        total_o += gro[j]
    piece[:, :, :OWN] = total
    for q in range(2):
        piece_o_ref[:, 384 * q : 384 * q + 384] = total_o[q].reshape(48, 384).astype(bf16)

    locals_[3].wait()
    own_out[...] += hid_v[...].astype(f32)

    @pl.loop(1, BLOCKS)
    def _(k):
        j = lax.rem(me + k, BLOCKS)
        remote(po_ref.at[j], go_ref.at[j], 72 + j, (place.d, j), 80 + j).wait_recv()
        own_out[...] += go_ref[j].astype(f32)

    out_ref[...] = own_out[...].astype(bf16)

    for copy in g2x:
        copy.wait_recv()
    total = gx[0]
    for j in range(1, 8):
        total += gx[j]
    piece[:, :, OWN:] = total
    owners = []
    for k in range(1, 8):
        them = place.shard_of(k)
        copy = remote(piece.at[lax.rem(them, 4)], ow.at[me], 132 + k, place.shard_peer(k))
        goes = them // 4 == place.c
        pl.when(goes)(copy.start)
        owners.append((copy, goes))

    @pl.when(mine)
    def _():
        ow[me] = piece[place.z]

    @pl.loop(1, BLOCKS)
    def _(k):
        j = lax.rem(me + k, BLOCKS)
        remote(ct_ref.at[j], gi_ref.at[j], 116 + j, (place.d, j), 124 + j).wait_recv()
        own_dn[...] += gi_ref[j].astype(f32)

    locals_[4].wait()
    u = hid_v[...].astype(f32)
    scale = lax.rsqrt(jnp.mean(u * u, axis=1, keepdims=True) + epsilon)
    d_normed = own_dn[...]
    gained = gain_ref[:, :D] * d_normed
    unit = u * scale
    grad = scale * gained - unit * (scale * scale * jnp.mean(u * gained, axis=1, keepdims=True))
    igrad_ref[...] = (cot_v[...].astype(f32) + grad).astype(bf16)

    sg[...] = jnp.zeros_like(sg)
    sg[0:1, :] = jnp.sum(d_normed * unit, axis=0, keepdims=True)
    sg[1:6, :640] = dconv_ref[0:5, :]
    sg[1:2, 640:1024] = dgain_ref[0:1, :]
    sg[2:3, 640:1024] = dskip_ref[0:1, :]
    sg[3:5, 640:768] = dhead_ref[0:2, :]
    sgs = [remote(sg, sg_all.at[me], 140 + k, place.shard_peer(k)) for k in range(1, 8)]
    for copy in sgs:
        copy.start()
    sg_all[me] = sg[...]

    for k in range(1, 8):
        @pl.when(mine)
        def _(k=k):
            owners[k - 1][0].wait_recv()

    @pl.when(mine)
    def _():
        common = ow[0, :, 2 * OWN :]
        for j in range(1, 8):
            common += ow[j, :, 2 * OWN :]
        for j in range(8):
            slab_ref[:, OWN * j : OWN * (j + 1)] = ow[j, :, :OWN].astype(bf16)
            slab_ref[:, DI + OWN * j : DI + OWN * (j + 1)] = ow[j, :, OWN : 2 * OWN].astype(bf16)
        slab_ref[:, 2 * DI :] = common.astype(bf16)

    @pl.when(jnp.logical_not(mine))
    def _():
        slab_ref[...] = jnp.zeros_like(slab_ref)

    for copy in sgs:
        copy.wait_recv()

    for copy in smalls + hids + cots + sums + w_x + [w_core, swap_z, swap_o, swap_x]:
        copy.wait_send()
    for copy in g2z + g2o + g2x + sgs:
        copy.wait_send()
    for copy, goes in owners:
        pl.when(goes)(copy.wait_send)

    @pl.when(mine)
    def _():
        for parts in weights:
            for copy in parts:
                copy.wait_send()

    @pl.loop(1, BLOCKS)
    def _(k):
        b = lax.rem(me + k, BLOCKS)
        out_copy(b).wait_send()
        in_copy(b).wait_send()


def sds(shape, dtype=f32):
    return jax.ShapeDtypeStruct(shape, dtype)


def run_whole(hid, cot, in_master, out_master, small, hd):
    any_spec = pl.BlockSpec(memory_space=pl.ANY)
    vmem = pl.BlockSpec(memory_space=pltpu.VMEM)

    def v(*shape, dtype=f32):
        return pltpu.VMEM(shape, dtype)

    tokens = (8, BLOCK, D)
    part = (8, BLOCK, OWN)
    split = (4, 8, 32, OWN)
    return pl.pallas_call(
        whole_kernel,
        in_specs=[any_spec] * 5 + [vmem],
        out_specs=tuple([vmem] * 5),
        out_shape=(
            sds((BLOCK, D), bf16), sds((BLOCK, D), bf16), sds((24, WIDE), bf16),
            sds((48, 768), bf16), sds((8, 8, D)),
        ),
        scratch_shapes=[
            v(*tokens, dtype=bf16), v(*tokens, dtype=bf16), v(8, 192, COLS, dtype=bf16), v(*split),
            v(4, 8, 32, 768), v(4, 8, 32, 768), v(8, BLOCK, 128), v(*part), v(*split), v(*split),
            v(8, NS, OWN), v(*part),
            v(8, BLOCK, COLS, dtype=bf16), v(*part, dtype=bf16), v(*tokens, dtype=bf16),
            v(*tokens, dtype=bf16), v(BLOCK, D), v(6, BLOCK, 768), v(48, PROJ),
            v(48, WIDE, dtype=bf16),
            v(OWN, D, dtype=bf16), v(8, 8, 640), v(1, 4608), v(8, CONVC),
            v(16, 128), v(8, 16, 128), v(BLOCK, 128), v(4, 8, 24, OWN), v(4, 8, 24, OWN),
            v(4, 8, 24, OWN), v(8, 4, 24, OWN), v(8, 2, 2, 24, OWN), v(4, 8, 24, 768),
            v(8, 4, 24, 768), v(*tokens, dtype=bf16),
            v(BLOCK, D), v(4, 24, COLS), v(8, 24, COLS), v(8, D), v(8, OWN), v(8, OWN), v(8, 640),
            v(8, 128), v(NS, OWN), v(8, 640), v(BLOCK, D, dtype=bf16), v(BLOCK, D, dtype=bf16),
            pltpu.SemaphoreType.DMA((156,)), pltpu.SemaphoreType.DMA((156,)),
            pltpu.SemaphoreType.DMA((15,)),
        ],
        compiler_params=pltpu.CompilerParams(
            collective_id=1, has_side_effects=True, vmem_limit_bytes=62 * 2**20
        ),
    )(hid, cot, in_master, out_master, small, hd)


def adam_update(master, first, second, gradient, rate, decay):
    first_new = beta_one * first + (1.0 - beta_one) * gradient
    second_new = beta_two * second + (1.0 - beta_two) * gradient * gradient
    scaled = (
        first_new
        / (1.0 - beta_one**STEP)
        / (jnp.sqrt(second_new / (1.0 - beta_two**STEP)) + adam_epsilon)
    )
    return (first_new, second_new, master - rate * (scaled + decay * master))


def on_device(
    hidden, cotangent, in_master, in_first, in_second, out_master, out_first, out_second,
    gain_master, gain_first, gain_second, conv_master, conv_first, conv_second,
    head_master, head_first, head_second,
):
    s = lax.axis_index("shard")
    low = lambda v: lax.reduce_precision(v, 8, 7)
    small = jnp.concatenate(
        [
            jnp.pad(low(conv_master), ((0, 0), (0, 224))),
            jnp.pad(low(gain_master), (0, 64))[None],
            jnp.zeros((2, 640), f32),
        ],
        axis=0,
    )
    heads = low(head_master)
    hd = jnp.concatenate(
        [
            jnp.pad(heads, ((0, 0), (0, OWN - 6))),
            jnp.repeat(heads[2], HD)[None],
            jnp.zeros((4, OWN), f32),
        ],
        axis=0,
    )
    layer_out, input_grad, slab, piece_o, sg = run_whole(
        hidden[0], cotangent[0], in_master, out_master, small, hd
    )
    g_gain = jnp.concatenate([jnp.sum(sg[:, 0], axis=0), sg[:, 1, 640:1024].reshape(-1)])
    g_conv = jnp.concatenate(
        [
            sg[:, 1:6, :OWN].transpose(1, 0, 2).reshape(5, DI),
            jnp.sum(sg[:, 1:6, OWN:640], axis=0),
        ],
        axis=1,
    )
    mine = lax.dynamic_index_in_dim(sg, s, 0, keepdims=False)
    own_small = jnp.concatenate(
        [
            lax.dynamic_slice(g_gain, (576 * s,), (576,)),
            lax.dynamic_slice(g_conv, (0, 416 * s), (5, 416)).reshape(-1),
            mine[3, 640:646], mine[4, 640:646],
            jnp.sum(mine[2, 640:1024].reshape(6, HD), axis=1),
            jnp.zeros((398,), f32),
        ]
    ).reshape(24, 128)
    total_w, total_o, total_small = exchange(
        7, spread_body, (slab, piece_o, own_small),
        (sds((8, 24, WIDE), bf16), sds((8, 48, D), bf16), sds((16, 24, 128))), 45, 3,
    )
    total_small = jnp.sum(total_small, axis=0).reshape(-1)
    totals = (
        total_w.reshape(192, WIDE)[:, :PROJ].astype(f32),
        total_o.reshape(OWN, D).astype(f32),
        total_small[:576],
        total_small[576:2656].reshape(5, 416),
        total_small[2656:2674].reshape(3, 6),
    )
    masters = (in_master, out_master, gain_master, conv_master, head_master)
    firsts = (in_first, out_first, gain_first, conv_first, head_first)
    seconds = (in_second, out_second, gain_second, conv_second, head_second)
    updated = [
        adam_update(masters[g], firsts[g], seconds[g], totals[g], rates[g], decays[g])
        for g in range(5)
    ]
    return (layer_out[None], input_grad[None]) + tuple(v for group in updated for v in group)


def solution(mesh):
    rows, columns = P("shard", None), P(None, "shard")
    tokens = P("dp", "shard", None)
    state = (rows,) * 6 + (P("shard"),) * 3 + (columns,) * 6
    return jax.shard_map(
        on_device,
        mesh=mesh,
        in_specs=(tokens, tokens) + state,
        out_specs=(tokens, tokens) + state,
        check_vma=False,
    )
```

```python
import functools

import jax
import jax.numpy as jnp
from jax import lax
from jax.experimental import pallas as pl
from jax.experimental.pallas import tpu as pltpu
from jax.sharding import PartitionSpec as P

D = 1536
DI = 3072
H = 48
HD = 64
NS = 128
KCONV = 4
STEP = 5
BLOCK = 128
CONVC = 3328
PROJ = 6448
LEN = 1024
OWN = 384
COLS = 1152
WIDE = 6528
BLOCKS = LEN // BLOCK

f32 = jnp.float32
bf16 = jnp.bfloat16
highest = lax.Precision.HIGHEST
MESH = pl.DeviceIdType.MESH
epsilon = 1e-05
beta_one = 0.9
beta_two = 0.95
adam_epsilon = 1e-08
rates = (0.05, 0.04, 0.25, 0.5, 0.5)
decays = (0.1, 0.1, 0.0, 0.0, 0.0)
VMEM_LIMIT = 60 * 2**20


class Place:
    def __init__(self):
        self.d = lax.axis_index("dp")
        self.s = lax.axis_index("shard")
        self.c = lax.rem(self.d, 2)
        self.x = lax.rem(self.d // 2, 4)
        self.yh = self.d // 8
        self.big = self.d // 2
        self.z = lax.rem(self.s, 4)
        self.yl = self.s // 4

    def shard_of(self, k):
        return lax.rem(self.yl + k // 4, 2) * 4 + lax.rem(self.z + k % 4, 4)

    def shard_peer(self, k):
        return (self.d, self.shard_of(k))

    def big_of(self, k):
        return lax.rem(self.yh + k // 4, 2) * 4 + lax.rem(self.x + k % 4, 4)

    def big_peer(self, k):
        return (self.big_of(k) * 2 + self.c, self.s)

    def z_peer(self, k):
        return (self.d, self.yl * 4 + lax.rem(self.z + k, 4))

    def y_partner(self):
        return (self.d, (1 - self.yl) * 4 + self.z)

    def core_peer(self):
        return (self.big * 2 + 1 - self.c, self.s)

    def other_core_of(self, k):
        return (self.big_of(k) * 2 + 1 - self.c, self.s)


ORDER = (6, 2, 5, 7, 1, 3, 4)


def exchange(cid, body, ins, outs, sems, locals_):
    def kernel(*refs):
        in_refs = refs[: len(ins)]
        out_refs = refs[len(ins) : len(ins) + len(outs)]
        send, recv, own = refs[len(ins) + len(outs) :]
        place = Place()

        def meet(peers):
            barrier = pltpu.get_barrier_semaphore()
            for peer in peers:
                pl.semaphore_signal(barrier, inc=1, device_id=peer, device_id_type=MESH)
            pl.semaphore_wait(barrier, len(peers))

        def remote(src, dst, index, peer):
            return pltpu.make_async_remote_copy(
                src_ref=src,
                dst_ref=dst,
                send_sem=send.at[index],
                recv_sem=recv.at[index],
                device_id=peer,
                device_id_type=MESH,
            )

        def local(src, dst, index):
            return pltpu.make_async_copy(src, dst, own.at[index])

        body(place, meet, remote, local, in_refs, out_refs)

    any_spec = pl.BlockSpec(memory_space=pl.ANY)
    return pl.pallas_call(
        kernel,
        out_shape=outs,
        in_specs=[any_spec] * len(ins),
        out_specs=tuple([any_spec] * len(outs)),
        scratch_shapes=[
            pltpu.SemaphoreType.DMA((sems,)),
            pltpu.SemaphoreType.DMA((sems,)),
            pltpu.SemaphoreType.DMA((max(locals_, 1),)),
        ],
        compiler_params=pltpu.CompilerParams(collective_id=cid, has_side_effects=True),
    )(*ins)


def spread_body(place, meet, remote, local, ins, outs):
    slab, go, small = ins
    slab_out, go_out, small_out = outs
    core = place.core_peer()
    everyone = [place.big_peer(k) for k in ORDER] + [core]
    everyone += [place.other_core_of(k) for k in ORDER]
    meet(everyone)
    valid = place.yl == place.c
    at = pl.multiple_of(place.c * 768, 128)

    def half(index):
        return go_out.at[index, :, pl.ds(at, 768)]

    other_at = pl.multiple_of((1 - place.c) * 768, 128)
    own_small = local(small, small_out.at[place.d], 0)
    own_go = local(go, half(place.big), 1)
    own_slab = local(slab, slab_out.at[place.big], 2)
    own_small.start()
    own_go.start()
    smalls = [
        remote(small, small_out.at[place.d], n, peer) for n, peer in enumerate(everyone)
    ]
    slabs = [
        remote(slab, slab_out.at[place.big], 15 + n, place.big_peer(k))
        for n, k in enumerate(ORDER)
    ]
    gos = [
        remote(go, half(place.big), 22 + n, place.big_peer(k)) for n, k in enumerate(ORDER)
    ]
    to_core_slab = remote(slab, slab_out.at[place.big], 29, core)
    to_core_go = remote(go, half(place.big), 30, core)

    @pl.when(valid)
    def _():
        own_slab.start()
        for copy in slabs:
            copy.start()
        to_core_slab.start()

    for copy in gos:
        copy.start()
    to_core_go.start()
    for copy in smalls:
        copy.start()
    forward_gos = []
    forward_slabs = []
    for n, k in enumerate(ORDER):
        origin = lax.rem(place.yh + k // 4, 2) * 4 + lax.rem(place.x + 4 - k % 4, 4)
        gos[n].wait_recv()
        go_copy = remote(half(origin), half(origin), 31 + n, core)
        go_copy.start()
        forward_gos.append(go_copy)
        slab_copy = remote(slab_out.at[origin], slab_out.at[origin], 38 + n, core)

        @pl.when(valid)
        def _(n=n, slab_copy=slab_copy):
            slabs[n].wait_recv()
            slab_copy.start()

        forward_slabs.append(slab_copy)
    own_small.wait()
    own_go.wait()
    for copy in smalls:
        copy.wait()
    for copy in gos:
        copy.wait_send()
    to_core_go.wait()
    for copy in forward_gos:
        copy.wait()

    @pl.when(valid)
    def _():
        own_slab.wait()
        for copy in slabs:
            copy.wait_send()
        to_core_slab.wait_send()
        for copy in forward_slabs:
            copy.wait_send()

    @pl.when(jnp.logical_not(valid))
    def _():
        to_core_slab.wait_recv()
        for copy in forward_slabs:
            copy.wait_recv()


class Gather:
    def __init__(self, place, remote, src, buf, base):
        def at(dy, dz, lo, hi):
            index = lax.rem(place.yl + dy, 2) * 4 + lax.rem(place.z + dz, 4)
            return buf.at[index, pl.ds(lo, hi - lo)]

        def onward(view, index, peer):
            return remote(view, view, base + index, peer)

        up, down, over = place.z_peer(1), place.z_peer(3), place.y_partner()
        self.copies = [
            remote(src, buf.at[place.s], base, up),
            remote(src, buf.at[place.s], base + 1, down),
            remote(src, buf.at[place.s], base + 2, over),
            onward(at(0, 3, 0, 64), 3, up),
            onward(at(0, 1, 64, 128), 4, down),
            onward(at(0, 3, 64, 128), 5, over),
            onward(at(0, 1, 64, 128), 6, over),
            onward(at(0, 2, 64, 128), 7, over),
            onward(at(1, 0, 0, 64), 8, up),
            onward(at(1, 0, 0, 64), 9, down),
            onward(at(1, 3, 0, 32), 10, up),
            onward(at(1, 1, 32, 64), 11, down),
        ]

    def after(self, arrived, *indices):
        self.copies[arrived].wait_recv()
        for index in indices:
            self.copies[index].start()

    def begin(self):
        for copy in (self.copies[2], self.copies[0], self.copies[1]):
            copy.start()

    def first(self):
        self.after(2, 8, 9)
        self.after(0, 3, 5)
        self.after(1, 4, 6)

    def second(self):
        self.after(8, 10)
        self.after(9, 11)
        self.after(4, 7)

    def last(self):
        for index in (3, 5, 6, 7, 10, 11):
            self.copies[index].wait_recv()

    def sent(self):
        for copy in self.copies:
            copy.wait_send()


class Scatter:
    def __init__(self, place, remote, part, ra, rb, ra2, rb2, total, base):
        self.place, self.remote, self.base = place, remote, base
        self.part, self.ra, self.rb, self.ra2, self.rb2, self.total = part, ra, rb, ra2, rb2, total
        self.top, self.low = pl.ds(0, 64), pl.ds(64, 64)

    def along_z(self, b, source):
        place = self.place
        return self.remote(
            self.part.at[b, self.top],
            self.ra.at[place.z, b // 4],
            self.base + b,
            (place.d, place.yl * 4 + lax.rem(b, 4)),
            self.base + source * 2 + b // 4,
        )

    def along_y(self, b):
        z = lax.rem(b, 4)
        return self.remote(
            self.part.at[b, self.low], self.rb.at[z], self.base + 8 + z, self.place.y_partner()
        )

    def send(self, b):
        pl.when(lax.rem(b, 4) != self.place.z)(self.along_z(b, self.place.z).start)
        pl.when(b // 4 != self.place.yl)(self.along_y(b).start)

    def other(self):
        return (1 - self.place.yl) * 4 + self.place.z

    def over(self):
        return self.remote(
            self.part.at[self.other(), self.top], self.ra2, self.base + 12, self.place.y_partner()
        )

    def back(self, z):
        place = self.place
        return self.remote(
            self.part.at[place.yl * 4 + z, self.low],
            self.rb2.at[place.z],
            self.base + 13 + z,
            (place.d, place.yl * 4 + z),
            self.base + 13 + place.z,
        )

    def others(self):
        return [lax.rem(self.place.z + k, 4) for k in (1, 2, 3)]

    def middle(self):
        place, part = self.place, self.part
        for z in self.others():
            for y in range(2):
                self.along_z(y * 4 + z, z).wait_recv()

        def sum_z(block, y):
            total = part[block, :64].astype(f32)
            for z in self.others():
                total += self.ra[z, y].astype(f32)
            return total

        part[self.other(), :64] = sum_z(self.other(), 1 - place.yl).astype(bf16)
        self.over().start()
        self.total[:64] = sum_z(place.s, place.yl)
        for z in range(4):
            self.along_y((1 - place.yl) * 4 + z).wait_recv()
        for z in self.others():
            block = place.yl * 4 + z
            part[block, 64:] = (part[block, 64:].astype(f32) + self.rb[z].astype(f32)).astype(bf16)
            self.back(z).start()
        self.total[64:] = part[place.s, 64:].astype(f32) + self.rb[place.z].astype(f32)

    def last(self):
        self.over().wait_recv()
        self.total[:64] += self.ra2[...].astype(f32)
        for z in self.others():
            self.remote(
                self.part.at[self.place.yl * 4 + z, self.low], self.rb2.at[z],
                self.base + 13 + z, (self.place.d, self.place.yl * 4 + z),
            ).wait_recv()
            self.total[64:] += self.rb2[z].astype(f32)

    def sent(self):
        place = self.place
        for z in self.others():
            for y in range(2):
                self.along_z(y * 4 + z, place.z).wait_send()
            self.back(z).wait_send()
        for z in range(4):
            self.along_y((1 - place.yl) * 4 + z).wait_send()
        self.over().wait_send()


class Reduce:
    def __init__(self, place, remote, view, read, write, gx, gy, base):
        self.place, self.view, self.read, self.write, self.gx, self.gy = place, view, read, write, gx, gy
        self.along = [
            remote(
                view(y * 4 + lax.rem(place.x + k, 4)), gx.at[k - 1, y], base + 2 * k + y,
                place.big_peer(k),
            )
            for k in (1, 2, 3)
            for y in range(2)
        ]
        self.other = (1 - place.yh) * 4 + place.x
        self.over = remote(view(self.other), gy, base + 8, place.big_peer(4))

    def begin(self):
        for copy in self.along:
            copy.start()

    def total(self, big, y):
        total = self.read(big)
        for k in range(3):
            total += self.gx[k, y]
        return total

    def middle(self):
        for copy in self.along:
            copy.wait_recv()
        self.write(self.other, self.total(self.other, 1 - self.place.yh))
        self.over.start()

    def last(self):
        total = self.total(self.place.big, self.place.yh)
        self.over.wait_recv()
        return total + self.gy[...]

    def sent(self):
        for copy in self.along + [self.over]:
            copy.wait_send()


def dot(a, b, ca, cb, precision=None):
    return lax.dot_general(
        a, b, (((ca,), (cb,)), ((), ())), precision=precision, preferred_element_type=f32
    )


def mm(a, b, ca=1, cb=0):
    return dot(a.astype(f32), b.astype(f32), ca, cb, highest)


def lanes(shape):
    return lax.broadcasted_iota(jnp.int32, shape, 1)


def rows_of(shape):
    return lax.broadcasted_iota(jnp.int32, shape, 0)


def widen(m):
    low = lanes((m.shape[0], 128)) < HD
    return jnp.concatenate(
        [jnp.where(low, m[:, 2 * i : 2 * i + 1], m[:, 2 * i + 1 : 2 * i + 2]) for i in range(3)],
        axis=1,
    )


def lower_ones():
    return (rows_of((BLOCK, BLOCK)) >= lanes((BLOCK, BLOCK))).astype(f32)


def head_ones():
    return (rows_of((OWN, BLOCK)) // HD == lanes((OWN, BLOCK))).astype(f32)


def split_pair(pair):
    low = lanes(pair.shape) < HD
    zero = jnp.zeros_like(pair)
    return jnp.concatenate([jnp.where(low, pair, zero), jnp.where(low, zero, pair)], axis=0)


def head_mixing(cumulative, turned, h):
    causal = rows_of((BLOCK, BLOCK)) >= lanes((BLOCK, BLOCK))
    differ = cumulative[:, h : h + 1] - turned[h : h + 1, :]
    return jnp.exp(jnp.where(causal, differ, -jnp.inf))


def softplus(v):
    return jnp.maximum(v, 0.0) + jnp.log1p(jnp.exp(-jnp.abs(v)))


TB = 256
HALF = DI // 8


def dot3(a, b, ca, cb):
    a_hi, b_hi = a.astype(bf16), b.astype(bf16)
    a_lo, b_lo = (a - a_hi.astype(f32)).astype(bf16), (b - b_hi.astype(f32)).astype(bf16)
    left = jnp.concatenate([a_hi, a_hi, a_lo], axis=ca)
    right = jnp.concatenate([b_hi, b_lo, b_hi], axis=cb)
    return dot(left, right, ca, cb)


def dot_exact(a, ones, ca, cb):
    a_hi = a.astype(bf16)
    a_lo = (a - a_hi.astype(f32)).astype(bf16)
    low = ones.astype(bf16)
    return dot(
        jnp.concatenate([a_hi, a_lo], axis=ca), jnp.concatenate([low, low], axis=cb), ca, cb
    )


def ones_dot(ones, a, ca, cb):
    a_hi = a.astype(bf16)
    a_lo = (a - a_hi.astype(f32)).astype(bf16)
    low = ones.astype(bf16)
    return dot(
        jnp.concatenate([low, low], axis=ca), jnp.concatenate([a_hi, a_lo], axis=cb), ca, cb
    )


def decay_parts(log_decay):
    cumulative = ones_dot(lower_ones(), log_decay, 1, 0)
    return cumulative, cumulative.T, widen(cumulative)


def two_blocks(ref, i, columns):
    return ref[i, :, :, :columns].reshape(TB, columns)


def block_of(ref, b, columns):
    four = pl.ds(4 * lax.rem(b, 2), 4)
    return ref[b // 2, four, :, :columns].reshape(BLOCK, columns)


def forward_block(act, dt, log_decay, before):
    x, keys, query = act[:, :OWN], act[:, OWN : OWN + NS], act[:, OWN + NS :]
    cumulative, turned, wide = decay_parts(log_decay)
    contact = dot3(query, keys, 1, 1)
    scaled = x * widen(dt)
    within = []
    for p in range(3):
        pair = split_pair(scaled[:, 128 * p : 128 * p + 128])
        both = jnp.concatenate(
            [head_mixing(cumulative, turned, 2 * p + q) * contact for q in range(2)], axis=1
        )
        within.append(dot3(both, pair, 1, 0))
    last = wide[BLOCK - 1 : BLOCK, :]
    core = jnp.concatenate(within, axis=1) + dot3(query, before, 1, 0) * jnp.exp(wide)
    after = jnp.exp(last) * before + dot3(keys, scaled * jnp.exp(last - wide), 0, 0)
    return core, after


def whole_kernel(
    hid, cot, in_ref, out_w, small, hd_ref,
    out_ref, igrad_ref, slab_ref, piece_o_ref, sg_all,
    n_ref, ct_ref, w_ref, z_ref, big_a, big_b, raw_ref, core_ref, y_ref, dm_ref, st_ref, dcore_ref,
    dp_ref, mixed_ref, po_ref, ra_ref, rb_ref, ra2_ref, rb2_ref, own_out, wo_f, wq_f, wq, wo_ref, sm_ref, gain_ref, conv_ref,
    sums_ref, got_sums, turned_sums, rz, ro, own_o, gz, gz2, go, go2, rx, gx, gx2, ia_ref, ib_ref, ia2_ref, ib2_ref, own_dn,
    piece, ow, sg, dgain_ref, dskip_ref, dconv_ref, dhead_ref,
    state, halo, hid_v, cot_v, send, recv, own,
):
    place = Place()
    me = place.s
    wq_load = pltpu.make_async_copy(
        in_ref.at[pl.ds(pl.multiple_of(48 * place.x, 8), 48), :], wq_f, own.at[7]
    )
    wq_load.start()
    wq[:, WIDE - 128 :] = jnp.zeros((48, 128), bf16)
    barrier = pltpu.get_barrier_semaphore()
    core_peer = place.core_peer()
    bigs = [place.big_peer(k) for k in range(1, 8)]
    x_peers = bigs[:3]
    group = [place.shard_peer(k) for k in range(1, 8)]
    for peer in group + bigs + [core_peer]:
        pl.semaphore_signal(barrier, inc=1, device_id=peer, device_id_type=MESH)
    pl.semaphore_wait(barrier, 15)

    def remote(src, dst, index, peer, other=None):
        return pltpu.make_async_remote_copy(
            src_ref=src,
            dst_ref=dst,
            send_sem=send.at[index],
            recv_sem=recv.at[index if other is None else other],
            device_id=peer,
            device_id_type=MESH,
        )

    quarter = pl.multiple_of(48 * place.x, 16)

    def weight_parts(them):
        at = pl.multiple_of(them * OWN, 128)
        rows = pl.ds(quarter, 48)
        return (
            (wq.at[:, pl.ds(at, OWN)], w_ref.at[me, rows, pl.ds(0, OWN)]),
            (wq.at[:, pl.ds(at + DI, OWN)], w_ref.at[me, rows, pl.ds(OWN, OWN)]),
            (wq.at[:, pl.ds(2 * DI, OWN)], w_ref.at[me, rows, pl.ds(2 * OWN, OWN)]),
        )

    locals_ = [
        pltpu.make_async_copy(small, sm_ref.at[me], own.at[0]),
        pltpu.make_async_copy(hid, n_ref.at[me], own.at[1]),
        pltpu.make_async_copy(cot, ct_ref.at[me], own.at[2]),
        pltpu.make_async_copy(hid, hid_v, own.at[3]),
        pltpu.make_async_copy(cot, cot_v, own.at[14]),
    ]
    for copy in locals_:
        copy.start()
    mine = place.yl == place.c
    wo_parts = [
        pltpu.make_async_copy(
            out_w.at[pl.ds(BLOCK * (p % 3), BLOCK), pl.ds(768 * (p // 3), 768)],
            wo_f.at[p],
            own.at[8 + p],
        )
        for p in range(6)
    ]
    for copy in wo_parts:
        copy.start()
    wq_load.wait()
    wq[:, :PROJ] = wq_f[...].astype(bf16)
    own_w = [
        pltpu.make_async_copy(src, dst, own.at[4 + i])
        for i, (src, dst) in enumerate(weight_parts(me))
    ]
    smalls = [remote(small, sm_ref.at[me], k, place.shard_peer(k)) for k in range(1, 8)]
    hids = Gather(place, remote, hid, n_ref, 8)
    cots = Gather(place, remote, cot, ct_ref, 20)
    weights = []
    for k in range(1, 8):
        weights.append(
            [
                remote(src, dst, 40 + 3 * k + i, place.shard_peer(k))
                for i, (src, dst) in enumerate(weight_parts(place.shard_of(k)))
            ]
        )

    @pl.when(mine)
    def _():
        for copy in own_w:
            copy.start()
        for parts in weights:
            for copy in parts:
                copy.start()

    for copy in smalls:
        copy.start()
    hids.begin()

    def from_offset(k):
        return lax.rem(place.yl + k // 4, 2)

    for k in range(1, 8):
        @pl.when(from_offset(k) == place.c)
        def _(k=k):
            for copy in weights[k - 1]:
                copy.wait_recv()

    @pl.when(mine)
    def _():
        for copy in own_w:
            copy.wait()

    w_up, w_down = place.big_peer(1), place.big_peer(3)

    def w_quarter(k, lo=0, n=4):
        rows = pl.ds(pl.multiple_of(48 * lax.rem(place.x + k, 4), 16), 48)
        return w_ref.at[pl.ds(4 * place.c + lo, n), rows, :]

    def w_on(view, index, peer):
        return remote(view, view, 32 + index, peer)

    w_copies = [
        w_on(w_quarter(0), 0, w_up),
        w_on(w_quarter(0), 1, w_down),
        w_on(w_quarter(0), 2, core_peer),
        w_on(w_quarter(3, 0, 2), 3, w_up),
        w_on(w_quarter(3), 4, core_peer),
        w_on(w_quarter(1, 2, 2), 5, w_down),
        w_on(w_quarter(1), 6, core_peer),
        w_on(w_quarter(2, 0, 2), 7, core_peer),
        w_on(w_quarter(2, 2, 2), 8, core_peer),
    ]
    for copy in w_copies[:3]:
        copy.start()

    def w_after(arrived, *indices):
        w_copies[arrived].wait_recv()
        for index in indices:
            w_copies[index].start()

    locals_[1].wait()
    hids.first()
    w_after(0, 3, 4)
    w_after(1, 5, 6)
    hids.second()
    cots.begin()
    w_after(3, 7)
    w_after(5, 8)

    locals_[0].wait()
    for copy in smalls:
        copy.wait_recv()
    gain_ref[...] = jnp.concatenate([sm_ref[p, 5:6, :576] for p in range(8)], axis=1)
    conv_ref[...] = jnp.concatenate([sm_ref[p, :, :416] for p in range(8)], axis=1)
    gg_at = pl.ds(pl.multiple_of(D + OWN * me, 128), OWN)
    cv_at = pl.ds(pl.multiple_of(OWN * me, 128), OWN)

    def conv_row(k):
        return jnp.concatenate([conv_ref[k : k + 1, cv_at], conv_ref[k : k + 1, DI:]], axis=1)

    hids.last()
    hids.sent()
    for index in (2, 4, 6, 7, 8):
        w_copies[index].wait_recv()

    for copy in wo_parts:
        copy.wait()
    for p in range(6):
        at = 768 * (p // 3)
        wo_ref[BLOCK * (p % 3) : BLOCK * (p % 3 + 1), at : at + 768] = wo_f[p].astype(bf16)
    state[...] = jnp.zeros_like(state)
    halo[...] = jnp.zeros_like(halo)
    skip = hd_ref[3:4, :]

    @pl.loop(0, LEN // TB)
    def _(i):
        two = pl.ds(2 * i, 2)
        u = n_ref[two].reshape(TB, D).astype(f32)
        scale = lax.rsqrt(jnp.mean(u * u, axis=1, keepdims=True) + epsilon)
        normed = (u * scale * gain_ref[:, :D]).astype(bf16)
        n_ref[two] = normed.reshape(2, BLOCK, D)
        project = dot(normed, w_ref[...].reshape(D, COLS), 1, 0)
        z = project[:, :OWN]
        xbc = project[:, OWN : OWN + 640]
        raw = pltpu.roll(project[:, 1024:1152], 128 - 6 * me, 1)
        z_ref[i] = z.reshape(8, 32, OWN)
        big_a[i, :, :, :640] = xbc.reshape(8, 32, 640)
        raw_ref[two] = raw.reshape(2, BLOCK, 128)
        extended = jnp.concatenate([halo[...], xbc], axis=0)
        halo[...] = xbc[TB - 8 :, :]
        conv = conv_row(KCONV)
        for k in range(KCONV):
            conv = conv + conv_row(k) * extended[5 + k : 5 + k + TB, :]
        big_b[i, :, :, :640] = conv.reshape(8, 32, 640)
        act = conv * jax.nn.sigmoid(conv)
        dt = softplus(raw + hd_ref[0:1, :128])
        log_decay = -jnp.exp(hd_ref[1:2, :128]) * dt
        for j in range(TB // BLOCK):
            at = slice(j * BLOCK, (j + 1) * BLOCK)
            before = state[...]
            st_ref[2 * i + j] = before
            core, after = forward_block(act[at], dt[at], log_decay[at], before)
            state[...] = after
            core_ref[2 * i + j] = core
            y_ref[i, 4 * j : 4 * j + 4] = (core + skip * act[at, :OWN]).reshape(4, 32, OWN)

    locals_[2].wait()
    cots.first()
    cots.second()
    cots.last()

    @pl.loop(0, LEN // TB)
    def _(i):
        two = pl.ds(2 * i, 2)
        dm = dot(ct_ref[two].reshape(TB, D), wo_ref[...], 1, 1)
        dm_ref[i] = dm.reshape(8, 32, OWN)
        z = two_blocks(z_ref, i, OWN)
        gated = two_blocks(y_ref, i, OWN) * (z * jax.nn.sigmoid(z))
        ones = jnp.ones((8, OWN), f32)
        first = ones_dot(ones, gated * gated, 1, 1)
        second = ones_dot(ones, gated * (gain_ref[:, gg_at] * dm), 1, 1)
        for j in range(2):
            sums_ref[pl.ds(2 * i + j, 1), :] = first[0:1, 128 * j : 128 * j + 128]
            sums_ref[pl.ds(2 * i + j + 8, 1), :] = second[0:1, 128 * j : 128 * j + 128]

    sums = [remote(sums_ref, got_sums.at[me], 64 + k, place.shard_peer(k)) for k in range(1, 8)]
    for copy in sums:
        copy.start()
    got_sums[me] = sums_ref[...]
    for copy in sums:
        copy.wait_recv()
    totals = got_sums[0]
    for j in range(1, 8):
        totals += got_sums[j]
    turned_sums[...] = jnp.concatenate([totals, jnp.zeros((112, 128), f32)], axis=0).T
    gain = gain_ref[:, gg_at]
    lane = lanes((BLOCK, 128))
    dgain_ref[...] = jnp.zeros_like(dgain_ref)
    dskip_ref[...] = jnp.zeros_like(dskip_ref)
    dconv_ref[...] = jnp.zeros_like(dconv_ref)
    dhead_ref[...] = jnp.zeros_like(dhead_ref)

    outs = Scatter(place, remote, po_ref, ra_ref, rb_ref, ra2_ref, rb2_ref, own_out, 72)

    @pl.loop(0, BLOCKS)
    def _(i):
        b = lax.rem(me + 1 + i, BLOCKS)
        column = turned_sums[...]
        first = jnp.sum(jnp.where(lane == b, column, 0.0), axis=1, keepdims=True)
        second = jnp.sum(jnp.where(lane == b + 8, column, 0.0), axis=1, keepdims=True)
        z, y, dm = block_of(z_ref, b, OWN), block_of(y_ref, b, OWN), block_of(dm_ref, b, OWN)
        sig_z = jax.nn.sigmoid(z)
        gate = z * sig_z
        scale = lax.rsqrt(first * (1.0 / DI) + epsilon)
        unit = y * gate * scale
        mixed = (unit * gain).astype(bf16)
        mixed_ref[b] = mixed
        dgain_ref[0:1, :] += jnp.sum(dm * unit, axis=0, keepdims=True)
        dgated = scale * (gain * dm) - unit * (scale * scale * (second * (1.0 / DI)))
        dz = dgated * y * (sig_z * (1.0 + z * (1.0 - sig_z)))
        dp_ref[b, :, :OWN] = dz.astype(bf16)
        dcore_ref[b] = dgated * gate
        po_ref[b] = dot(mixed, wo_ref[...], 1, 0).astype(bf16)
        outs.send(b)

    def weight_grad(q, columns):
        left = n_ref[:, :, pl.ds(pl.multiple_of(384 * q, 128), 384)].reshape(LEN, 384)
        return dot(left, dp_ref[:, :, columns].reshape(LEN, -1), 0, 0)

    def out_grad(h, q):
        at = pl.multiple_of(768 * h + 384 * q, 128)
        return dot(mixed_ref[...].reshape(LEN, OWN), ct_ref[:, :, pl.ds(at, 384)].reshape(LEN, 384), 0, 0)

    other = 1 - place.c
    zs = slice(0, OWN)
    late = slice(OWN, COLS)

    def rows24(ref):
        return ref.at[:, :, pl.ds(0, 24), :]

    @pl.loop(0, 2)
    def _(q):
        two = pl.ds(2 * q, 2)
        y_ref[two, :, :24, :] = weight_grad(2 * other + q, zs).reshape(2, 8, 24, OWN)
        z_ref[two, :, :24, :] = out_grad(other, q).reshape(2, 8, 24, OWN)

    swap_z = remote(rows24(y_ref), rz, 156, core_peer)
    swap_o = remote(rows24(z_ref), ro, 157, core_peer)
    swap_z.start()
    swap_o.start()

    @pl.loop(0, 2)
    def _(q):
        two = pl.ds(2 * q, 2)
        dm_ref[two, :, :24, :] = weight_grad(2 * place.c + q, zs).reshape(2, 8, 24, OWN)
        own_o[q] = out_grad(place.c, q).reshape(8, 2, 24, OWN)

    def reducer(ref, gx_ref, gy_ref, base):
        def write(big, total):
            ref[:, big, :24, :] = total

        return Reduce(
            place, remote, lambda big: ref.at[:, big, pl.ds(0, 24), :],
            lambda big: ref[:, big, :24, :], write, gx_ref, gy_ref, base,
        )

    def write_o(big, total):
        own_o[:, big] = total

    sum_z = reducer(dm_ref, gz, gz2, 92)
    sum_x = reducer(big_b, gx, gx2, 102)
    sum_o = Reduce(
        place, remote, lambda big: own_o.at[:, big], lambda big: own_o[:, big], write_o, go, go2, 112
    )

    state[...] = jnp.zeros_like(state)
    halo[...] = jnp.zeros_like(halo)

    @pl.loop(0, BLOCKS)
    def _(i):
        b = BLOCKS - 1 - i

        @pl.when(i == 1)
        def _():
            swap_z.wait_recv()
            swap_o.wait_recv()
            for r in range(4):
                dm_ref[r, :, :24, :] += rz[r]
            for q in range(2):
                own_o[q] += ro[2 * q : 2 * q + 2].reshape(8, 2, 24, OWN)
            sum_z.begin()
            sum_o.begin()

        pl.when(i == 5)(outs.middle)

        conv = block_of(big_b, b, 640)
        raw, core, dcore = raw_ref[b], core_ref[b], dcore_ref[b]
        sig = jax.nn.sigmoid(conv)
        act = conv * sig
        x, keys, query = act[:, :OWN], act[:, OWN : OWN + NS], act[:, OWN + NS :]
        shifted = raw + hd_ref[0:1, :128]
        dt = softplus(shifted)
        rate = jnp.exp(hd_ref[1:2, :128])
        log_decay = -rate * dt
        dskip_ref[0:1, :] += jnp.sum(dcore * x, axis=0, keepdims=True)
        cumulative, turned, wide = decay_parts(log_decay)
        contact = dot3(query, keys, 1, 1)
        dt_wide = widen(dt)
        scaled = x * dt_wide
        dcontact = jnp.zeros((BLOCK, BLOCK), f32)
        dscaled = []
        for p in range(3):
            at = slice(128 * p, 128 * p + 128)
            mixing = [head_mixing(cumulative, turned, 2 * p + q) for q in range(2)]
            both = jnp.concatenate([m * contact for m in mixing], axis=0)
            pair = split_pair(dcore[:, at])
            dscaled.append(dot3(both, pair, 0, 0))
            dmix = dot3(pair, scaled[:, at], 1, 1)
            dcontact += dmix[:BLOCK] * mixing[0] + dmix[BLOCK:] * mixing[1]
        last = wide[BLOCK - 1 : BLOCK, :]
        before = st_ref[b]
        after_adj = state[...]
        left = jnp.exp(last - wide)
        from_core = dcore * jnp.exp(wide)
        dquery = dot3(from_core, before, 1, 1) + dot3(dcontact, keys, 1, 0)
        carried = dot3(keys, after_adj, 1, 0) * left
        dscaled = jnp.concatenate(dscaled, axis=1) + carried
        dkeys = dot3(scaled * left, after_adj, 1, 1) + dot3(dcontact, query, 0, 0)
        end = jnp.exp(last)
        state[...] = end * after_adj + dot3(query, from_core, 0, 0)
        heads = head_ones()
        last_add = dot_exact(
            jnp.sum(carried * scaled, axis=0, keepdims=True)
            + end * jnp.sum(after_adj * before, axis=0, keepdims=True),
            heads, 1, 0,
        )
        dcum = dot_exact(dcore * core - dscaled * scaled, heads, 1, 0)
        dlog = ones_dot(lower_ones(), dcum, 0, 0) + last_add
        ddt = dot_exact(dscaled * x, heads, 1, 0) - rate * dlog
        draw = ddt * jax.nn.sigmoid(shifted)
        dhead_ref[0:1, :] += jnp.sum(draw, axis=0, keepdims=True)
        dhead_ref[1:2, :] += jnp.sum(dlog * log_decay, axis=0, keepdims=True)
        dx = dscaled * dt_wide + skip * dcore
        dact = jnp.concatenate([dx, dkeys, dquery], axis=1)
        dconv = dact * (sig * (1.0 + conv * (1.0 - sig)))
        extended = jnp.concatenate([dconv, halo[...]], axis=0)
        halo[...] = dconv[:8, :]
        xbc = block_of(big_a, b, 640)
        dxbc = jnp.zeros_like(xbc)
        for k in range(KCONV):
            moved = extended[3 - k : 3 - k + BLOCK, :]
            dxbc += conv_row(k) * moved
            dconv_ref[k : k + 1, :] += jnp.sum(xbc * moved, axis=0, keepdims=True)
        dconv_ref[KCONV : KCONV + 1, :] += jnp.sum(dconv, axis=0, keepdims=True)
        dp_ref[b, :, OWN : OWN + 640] = dxbc.astype(bf16)
        draw_own = jnp.where(lane < 6, draw, 0.0)
        dp_ref[b, :, 1024:] = pltpu.roll(draw_own, 6 * me, 1).astype(bf16)

    @pl.loop(0, 2)
    def _(q):
        two = pl.ds(2 * q, 2)
        big_a[two, :, :24, :] = weight_grad(2 * other + q, late).reshape(2, 8, 24, 768)

    swap_x = remote(rows24(big_a), rx, 158, core_peer)
    swap_x.start()

    @pl.loop(0, 2)
    def _(q):
        two = pl.ds(2 * q, 2)
        big_b[two, :, :24, :] = weight_grad(2 * place.c + q, late).reshape(2, 8, 24, 768)

    cots.sent()
    ins = Scatter(place, remote, ct_ref, ia_ref, ib_ref, ia2_ref, ib2_ref, own_dn, 122)

    @pl.loop(0, BLOCKS)
    def _(i):
        b = lax.rem(me + 1 + i, BLOCKS)
        ct_ref[b] = dot(dp_ref[b], w_ref[...].reshape(D, COLS), 1, 1).astype(bf16)
        ins.send(b)

    swap_x.wait_recv()
    for r in range(4):
        big_b[r, :, :24, :] += rx[r]
    sum_x.begin()
    sum_z.middle()
    sum_o.middle()

    outs.last()
    locals_[3].wait()
    out_ref[...] = (own_out[...] + hid_v[...].astype(f32)).astype(bf16)

    piece[:, :, :OWN] = sum_z.last()
    total_o = sum_o.last()
    for q in range(2):
        piece_o_ref[:, 384 * q : 384 * q + 384] = total_o[q].reshape(48, 384).astype(bf16)
    ins.middle()

    sum_x.middle()
    piece[:, :, OWN:] = sum_x.last()
    owners = []
    for k in range(1, 8):
        them = place.shard_of(k)
        copy = remote(piece.at[lax.rem(them, 4)], ow.at[me], 140 + k, place.shard_peer(k))
        goes = them // 4 == place.c
        pl.when(goes)(copy.start)
        owners.append((copy, goes))

    @pl.when(mine)
    def _():
        ow[me] = piece[place.z]

    ins.last()
    locals_[4].wait()
    u = hid_v[...].astype(f32)
    scale = lax.rsqrt(jnp.mean(u * u, axis=1, keepdims=True) + epsilon)
    d_normed = own_dn[...]
    gained = gain_ref[:, :D] * d_normed
    unit = u * scale
    grad = scale * gained - unit * (scale * scale * jnp.mean(u * gained, axis=1, keepdims=True))
    igrad_ref[...] = (cot_v[...].astype(f32) + grad).astype(bf16)

    sg[...] = jnp.zeros_like(sg)
    sg[0:1, :] = jnp.sum(d_normed * unit, axis=0, keepdims=True)
    sg[1:6, :640] = dconv_ref[0:5, :]
    sg[1:2, 640:1024] = dgain_ref[0:1, :]
    sg[2:3, 640:1024] = dskip_ref[0:1, :]
    sg[3:5, 640:768] = dhead_ref[0:2, :]
    sgs = [remote(sg, sg_all.at[me], 148 + k, place.shard_peer(k)) for k in range(1, 8)]
    for copy in sgs:
        copy.start()
    sg_all[me] = sg[...]

    for k in range(1, 8):
        @pl.when(mine)
        def _(k=k):
            owners[k - 1][0].wait_recv()

    @pl.when(mine)
    def _():
        common = ow[0, :, 2 * OWN :]
        for j in range(1, 8):
            common += ow[j, :, 2 * OWN :]
        for j in range(8):
            slab_ref[:, OWN * j : OWN * (j + 1)] = ow[j, :, :OWN].astype(bf16)
            slab_ref[:, DI + OWN * j : DI + OWN * (j + 1)] = ow[j, :, OWN : 2 * OWN].astype(bf16)
        slab_ref[:, 2 * DI :] = common.astype(bf16)

    @pl.when(jnp.logical_not(mine))
    def _():
        slab_ref[...] = jnp.zeros_like(slab_ref)

    for copy in sgs:
        copy.wait_recv()

    for copy in smalls + sums + w_copies + sgs + [swap_z, swap_o, swap_x]:
        copy.wait_send()
    for group_of in (outs, ins, sum_z, sum_o, sum_x):
        group_of.sent()
    for copy, goes in owners:
        pl.when(goes)(copy.wait_send)

    @pl.when(mine)
    def _():
        for parts in weights:
            for copy in parts:
                copy.wait_send()


def sds(shape, dtype=f32):
    return jax.ShapeDtypeStruct(shape, dtype)


def run_whole(hid, cot, in_master, out_master, small, hd):
    any_spec = pl.BlockSpec(memory_space=pl.ANY)
    vmem = pl.BlockSpec(memory_space=pltpu.VMEM)

    def v(*shape, dtype=f32):
        return pltpu.VMEM(shape, dtype)

    tokens = (8, BLOCK, D)
    part = (8, BLOCK, OWN)
    split = (4, 8, 32, OWN)
    landing = [
        v(4, 2, 64, D, dtype=bf16), v(4, 64, D, dtype=bf16), v(64, D, dtype=bf16),
        v(4, 64, D, dtype=bf16),
    ]
    return pl.pallas_call(
        whole_kernel,
        in_specs=[any_spec] * 5 + [vmem],
        out_specs=tuple([vmem] * 5),
        out_shape=(
            sds((BLOCK, D), bf16), sds((BLOCK, D), bf16), sds((24, WIDE), bf16),
            sds((48, 768), bf16), sds((8, 8, D)),
        ),
        scratch_shapes=[
            v(*tokens, dtype=bf16), v(*tokens, dtype=bf16), v(8, 192, COLS, dtype=bf16), v(*split),
            v(4, 8, 32, 768), v(4, 8, 32, 768), v(8, BLOCK, 128), v(*part), v(*split), v(*split),
            v(8, NS, OWN), v(*part),
            v(8, BLOCK, COLS, dtype=bf16), v(*part, dtype=bf16), v(*tokens, dtype=bf16),
            *landing, v(BLOCK, D), v(6, BLOCK, 768), v(48, PROJ),
            v(48, WIDE, dtype=bf16),
            v(OWN, D, dtype=bf16), v(8, 8, 640), v(1, 4608), v(8, CONVC),
            v(16, 128), v(8, 16, 128), v(BLOCK, 128), v(4, 8, 24, OWN), v(4, 8, 24, OWN),
            v(2, 8, 2, 24, OWN), v(3, 2, 4, 24, OWN), v(4, 24, OWN), v(3, 2, 2, 2, 24, OWN),
            v(2, 2, 24, OWN), v(4, 8, 24, 768), v(3, 2, 4, 24, 768), v(4, 24, 768), *landing,
            v(BLOCK, D), v(4, 24, COLS), v(8, 24, COLS), v(8, D), v(8, OWN), v(8, OWN), v(8, 640),
            v(8, 128), v(NS, OWN), v(8, 640), v(BLOCK, D, dtype=bf16), v(BLOCK, D, dtype=bf16),
            pltpu.SemaphoreType.DMA((160,)), pltpu.SemaphoreType.DMA((160,)),
            pltpu.SemaphoreType.DMA((15,)),
        ],
        compiler_params=pltpu.CompilerParams(
            collective_id=1, has_side_effects=True, vmem_limit_bytes=62 * 2**20
        ),
    )(hid, cot, in_master, out_master, small, hd)


def adam_update(master, first, second, gradient, rate, decay):
    first_new = beta_one * first + (1.0 - beta_one) * gradient
    second_new = beta_two * second + (1.0 - beta_two) * gradient * gradient
    scaled = (
        first_new
        / (1.0 - beta_one**STEP)
        / (jnp.sqrt(second_new / (1.0 - beta_two**STEP)) + adam_epsilon)
    )
    return (first_new, second_new, master - rate * (scaled + decay * master))


def on_device(
    hidden, cotangent, in_master, in_first, in_second, out_master, out_first, out_second,
    gain_master, gain_first, gain_second, conv_master, conv_first, conv_second,
    head_master, head_first, head_second,
):
    s = lax.axis_index("shard")
    low = lambda v: lax.reduce_precision(v, 8, 7)
    small = jnp.concatenate(
        [
            jnp.pad(low(conv_master), ((0, 0), (0, 224))),
            jnp.pad(low(gain_master), (0, 64))[None],
            jnp.zeros((2, 640), f32),
        ],
        axis=0,
    )
    heads = low(head_master)
    hd = jnp.concatenate(
        [
            jnp.pad(heads, ((0, 0), (0, OWN - 6))),
            jnp.repeat(heads[2], HD)[None],
            jnp.zeros((4, OWN), f32),
        ],
        axis=0,
    )
    layer_out, input_grad, slab, piece_o, sg = run_whole(
        hidden[0], cotangent[0], in_master, out_master, small, hd
    )
    g_gain = jnp.concatenate([jnp.sum(sg[:, 0], axis=0), sg[:, 1, 640:1024].reshape(-1)])
    g_conv = jnp.concatenate(
        [
            sg[:, 1:6, :OWN].transpose(1, 0, 2).reshape(5, DI),
            jnp.sum(sg[:, 1:6, OWN:640], axis=0),
        ],
        axis=1,
    )
    mine = lax.dynamic_index_in_dim(sg, s, 0, keepdims=False)
    own_small = jnp.concatenate(
        [
            lax.dynamic_slice(g_gain, (576 * s,), (576,)),
            lax.dynamic_slice(g_conv, (0, 416 * s), (5, 416)).reshape(-1),
            mine[3, 640:646], mine[4, 640:646],
            jnp.sum(mine[2, 640:1024].reshape(6, HD), axis=1),
            jnp.zeros((398,), f32),
        ]
    ).reshape(24, 128)
    total_w, total_o, total_small = exchange(
        7, spread_body, (slab, piece_o, own_small),
        (sds((8, 24, WIDE), bf16), sds((8, 48, D), bf16), sds((16, 24, 128))), 45, 3,
    )
    total_small = jnp.sum(total_small, axis=0).reshape(-1)
    totals = (
        total_w.reshape(192, WIDE)[:, :PROJ].astype(f32),
        total_o.reshape(OWN, D).astype(f32),
        total_small[:576],
        total_small[576:2656].reshape(5, 416),
        total_small[2656:2674].reshape(3, 6),
    )
    masters = (in_master, out_master, gain_master, conv_master, head_master)
    firsts = (in_first, out_first, gain_first, conv_first, head_first)
    seconds = (in_second, out_second, gain_second, conv_second, head_second)
    updated = [
        adam_update(masters[g], firsts[g], seconds[g], totals[g], rates[g], decays[g])
        for g in range(5)
    ]
    return (layer_out[None], input_grad[None]) + tuple(v for group in updated for v in group)


def solution(mesh):
    rows, columns = P("shard", None), P(None, "shard")
    tokens = P("dp", "shard", None)
    state = (rows,) * 6 + (P("shard"),) * 3 + (columns,) * 6
    return jax.shard_map(
        on_device,
        mesh=mesh,
        in_specs=(tokens, tokens) + state,
        out_specs=(tokens, tokens) + state,
        check_vma=False,
    )
```

```python
import functools

import jax
import jax.numpy as jnp
from jax import lax
from jax.experimental import pallas as pl
from jax.experimental.pallas import tpu as pltpu
from jax.sharding import PartitionSpec as P

D = 1536
DI = 3072
H = 48
HD = 64
NS = 128
KCONV = 4
STEP = 5
BLOCK = 128
CONVC = 3328
PROJ = 6448
LEN = 1024
OWN = 384
COLS = 1152
WIDE = 6528
BLOCKS = LEN // BLOCK

f32 = jnp.float32
bf16 = jnp.bfloat16
highest = lax.Precision.HIGHEST
MESH = pl.DeviceIdType.MESH
epsilon = 1e-05
beta_one = 0.9
beta_two = 0.95
adam_epsilon = 1e-08
rates = (0.05, 0.04, 0.25, 0.5, 0.5)
decays = (0.1, 0.1, 0.0, 0.0, 0.0)
TOP = 96


class Place:
    def __init__(self):
        self.d = lax.axis_index("dp")
        self.s = lax.axis_index("shard")
        self.c = lax.rem(self.d, 2)
        self.x = lax.rem(self.d // 2, 4)
        self.yh = self.d // 8
        self.big = self.d // 2
        self.z = lax.rem(self.s, 4)
        self.yl = self.s // 4

    def shard_of(self, k):
        return lax.rem(self.yl + k // 4, 2) * 4 + lax.rem(self.z + k % 4, 4)

    def shard_peer(self, k):
        return (self.d, self.shard_of(k))

    def big_of(self, k):
        return lax.rem(self.yh + k // 4, 2) * 4 + lax.rem(self.x + k % 4, 4)

    def big_peer(self, k):
        return (self.big_of(k) * 2 + self.c, self.s)

    def z_peer(self, k):
        return (self.d, self.yl * 4 + lax.rem(self.z + k, 4))

    def y_partner(self):
        return (self.d, (1 - self.yl) * 4 + self.z)

    def core_peer(self):
        return (self.big * 2 + 1 - self.c, self.s)

    def other_core_of(self, k):
        return (self.big_of(k) * 2 + 1 - self.c, self.s)


class Gather:
    def __init__(self, place, remote, src, buf, base):
        def at(dy, dz, lo, hi):
            index = lax.rem(place.yl + dy, 2) * 4 + lax.rem(place.z + dz, 4)
            return buf.at[index, pl.ds(lo, hi - lo)]

        def onward(view, index, peer):
            return remote(view, view, base + index, peer)

        up, down, over = place.z_peer(1), place.z_peer(3), place.y_partner()
        self.copies = [
            remote(src, buf.at[place.s], base, up),
            remote(src, buf.at[place.s], base + 1, down),
            remote(src, buf.at[place.s], base + 2, over),
            onward(at(0, 3, 0, 64), 3, up),
            onward(at(0, 1, 64, 128), 4, down),
            onward(at(0, 3, 64, 128), 5, over),
            onward(at(0, 1, 64, 128), 6, over),
            onward(at(0, 2, 64, 128), 7, over),
            onward(at(1, 0, 0, 64), 8, up),
            onward(at(1, 0, 0, 64), 9, down),
            onward(at(1, 3, 0, 32), 10, up),
            onward(at(1, 1, 32, 64), 11, down),
        ]

    def after(self, arrived, *indices):
        self.copies[arrived].wait_recv()
        for index in indices:
            self.copies[index].start()

    def begin(self):
        for copy in (self.copies[2], self.copies[0], self.copies[1]):
            copy.start()

    def first(self):
        self.after(2, 8, 9)
        self.after(0, 3, 5)
        self.after(1, 4, 6)

    def second(self):
        self.after(8, 10)
        self.after(9, 11)
        self.after(4, 7)

    def last(self):
        for index in (3, 5, 6, 7, 10, 11):
            self.copies[index].wait_recv()

    def sent(self):
        for copy in self.copies:
            copy.wait_send()


class Scatter:
    def __init__(self, place, remote, part, ra, rb, ra2, rb2, total, base):
        self.place, self.remote, self.base = place, remote, base
        self.part, self.ra, self.rb, self.ra2, self.rb2, self.total = part, ra, rb, ra2, rb2, total
        self.top, self.low = pl.ds(0, TOP), pl.ds(TOP, BLOCK - TOP)

    def along_z(self, b, source):
        place = self.place
        return self.remote(
            self.part.at[b, self.top],
            self.ra.at[place.z, b // 4],
            self.base + b,
            (place.d, place.yl * 4 + lax.rem(b, 4)),
            self.base + source * 2 + b // 4,
        )

    def along_y(self, b):
        z = lax.rem(b, 4)
        return self.remote(
            self.part.at[b, self.low], self.rb.at[z], self.base + 8 + z, self.place.y_partner()
        )

    def send(self, b):
        pl.when(lax.rem(b, 4) != self.place.z)(self.along_z(b, self.place.z).start)
        pl.when(b // 4 != self.place.yl)(self.along_y(b).start)

    def other(self):
        return (1 - self.place.yl) * 4 + self.place.z

    def over(self):
        return self.remote(
            self.part.at[self.other(), self.top], self.ra2, self.base + 12, self.place.y_partner()
        )

    def back(self, z):
        place = self.place
        return self.remote(
            self.part.at[place.yl * 4 + z, self.low],
            self.rb2.at[place.z],
            self.base + 13 + z,
            (place.d, place.yl * 4 + z),
            self.base + 13 + place.z,
        )

    def others(self):
        return [lax.rem(self.place.z + k, 4) for k in (1, 2, 3)]

    def middle(self):
        place, part = self.place, self.part
        for z in self.others():
            for y in range(2):
                self.along_z(y * 4 + z, z).wait_recv()

        def sum_z(block, y):
            total = part[block, :TOP].astype(f32)
            for z in self.others():
                total += self.ra[z, y].astype(f32)
            return total

        part[self.other(), :TOP] = sum_z(self.other(), 1 - place.yl).astype(bf16)
        self.over().start()
        self.total[:TOP] = sum_z(place.s, place.yl)
        for z in range(4):
            self.along_y((1 - place.yl) * 4 + z).wait_recv()
        for z in self.others():
            block = place.yl * 4 + z
            part[block, TOP:] = (part[block, TOP:].astype(f32) + self.rb[z].astype(f32)).astype(bf16)
            self.back(z).start()
        self.total[TOP:] = part[place.s, TOP:].astype(f32) + self.rb[place.z].astype(f32)

    def last(self):
        self.over().wait_recv()
        self.total[:TOP] += self.ra2[...].astype(f32)
        for z in self.others():
            self.remote(
                self.part.at[self.place.yl * 4 + z, self.low], self.rb2.at[z],
                self.base + 13 + z, (self.place.d, self.place.yl * 4 + z),
            ).wait_recv()
            self.total[TOP:] += self.rb2[z].astype(f32)

    def sent(self):
        place = self.place
        for z in self.others():
            for y in range(2):
                self.along_z(y * 4 + z, place.z).wait_send()
            self.back(z).wait_send()
        for z in range(4):
            self.along_y((1 - place.yl) * 4 + z).wait_send()
        self.over().wait_send()


class Reduce:
    def __init__(self, place, remote, view, read, write, gx, gy, base):
        self.place, self.view, self.read, self.write, self.gx, self.gy = place, view, read, write, gx, gy
        self.along = [
            remote(
                view(y * 4 + lax.rem(place.x + k, 4)), gx.at[k - 1, y], base + 2 * k + y,
                place.big_peer(k),
            )
            for k in (1, 2, 3)
            for y in range(2)
        ]
        self.other = (1 - place.yh) * 4 + place.x
        self.over = remote(view(self.other), gy, base + 8, place.big_peer(4))

    def begin(self):
        for copy in self.along:
            copy.start()

    def total(self, big, y):
        total = self.read(big)
        for k in range(3):
            total += self.gx[k, y]
        return total

    def middle(self):
        for copy in self.along:
            copy.wait_recv()
        self.write(self.other, self.total(self.other, 1 - self.place.yh))
        self.over.start()

    def last(self):
        total = self.total(self.place.big, self.place.yh)
        self.over.wait_recv()
        return total + self.gy[...]

    def sent(self):
        for copy in self.along + [self.over]:
            copy.wait_send()


class Direct:
    def __init__(self, place, remote, src, view, base):
        own, core = view(place.big), place.core_peer()
        self.copies = [remote(src, own, base + k, place.big_peer(k)) for k in range(1, 8)]
        self.cores = [remote(src, own, base + 8, core)]
        for k in range(1, 8):
            block = view(lax.rem(place.yh + k // 4, 2) * 4 + lax.rem(place.x + 4 - k % 4, 4))
            self.cores.append(remote(block, block, base + 8 + k, core))

    def begin(self):
        for copy in self.copies + self.cores[:1]:
            copy.start()

    def forward(self):
        for k in range(1, 8):
            self.copies[k - 1].wait_recv()
            self.cores[k].start()

    def sent(self):
        for copy in self.copies + self.cores:
            copy.wait_send()


def dot(a, b, ca, cb, precision=None):
    return lax.dot_general(
        a, b, (((ca,), (cb,)), ((), ())), precision=precision, preferred_element_type=f32
    )


def mm(a, b, ca=1, cb=0):
    return dot(a.astype(f32), b.astype(f32), ca, cb, highest)


def lanes(shape):
    return lax.broadcasted_iota(jnp.int32, shape, 1)


def rows_of(shape):
    return lax.broadcasted_iota(jnp.int32, shape, 0)


def widen(m):
    low = lanes((m.shape[0], 128)) < HD
    return jnp.concatenate(
        [jnp.where(low, m[:, 2 * i : 2 * i + 1], m[:, 2 * i + 1 : 2 * i + 2]) for i in range(3)],
        axis=1,
    )


def lower_ones():
    return (rows_of((BLOCK, BLOCK)) >= lanes((BLOCK, BLOCK))).astype(f32)


def head_ones():
    return (rows_of((OWN, BLOCK)) // HD == lanes((OWN, BLOCK))).astype(f32)


def split_pair(pair):
    low = lanes(pair.shape) < HD
    zero = jnp.zeros_like(pair)
    return jnp.concatenate([jnp.where(low, pair, zero), jnp.where(low, zero, pair)], axis=0)


def head_mixing(cumulative, turned, h):
    causal = rows_of((BLOCK, BLOCK)) >= lanes((BLOCK, BLOCK))
    differ = cumulative[:, h : h + 1] - turned[h : h + 1, :]
    return jnp.exp(jnp.where(causal, differ, -jnp.inf))


def softplus(v):
    return jnp.maximum(v, 0.0) + jnp.log1p(jnp.exp(-jnp.abs(v)))


TB = 256
HALF = DI // 8


def dot3(a, b, ca, cb):
    a_hi, b_hi = a.astype(bf16), b.astype(bf16)
    a_lo, b_lo = (a - a_hi.astype(f32)).astype(bf16), (b - b_hi.astype(f32)).astype(bf16)
    left = jnp.concatenate([a_hi, a_hi, a_lo], axis=ca)
    right = jnp.concatenate([b_hi, b_lo, b_hi], axis=cb)
    return dot(left, right, ca, cb)


def dot_exact(a, ones, ca, cb):
    a_hi = a.astype(bf16)
    a_lo = (a - a_hi.astype(f32)).astype(bf16)
    low = ones.astype(bf16)
    return dot(
        jnp.concatenate([a_hi, a_lo], axis=ca), jnp.concatenate([low, low], axis=cb), ca, cb
    )


def ones_dot(ones, a, ca, cb):
    a_hi = a.astype(bf16)
    a_lo = (a - a_hi.astype(f32)).astype(bf16)
    low = ones.astype(bf16)
    return dot(
        jnp.concatenate([low, low], axis=ca), jnp.concatenate([a_hi, a_lo], axis=cb), ca, cb
    )


def decay_parts(log_decay):
    cumulative = ones_dot(lower_ones(), log_decay, 1, 0)
    return cumulative, cumulative.T, widen(cumulative)


def two_blocks(ref, i, columns):
    return ref[i, :, :, :columns].reshape(TB, columns)


def block_of(ref, b, columns):
    four = pl.ds(4 * lax.rem(b, 2), 4)
    return ref[b // 2, four, :, :columns].reshape(BLOCK, columns)


def forward_block(act, dt, log_decay, before):
    x, keys, query = act[:, :OWN], act[:, OWN : OWN + NS], act[:, OWN + NS :]
    cumulative, turned, wide = decay_parts(log_decay)
    contact = dot3(query, keys, 1, 1)
    scaled = x * widen(dt)
    within = []
    for p in range(3):
        pair = split_pair(scaled[:, 128 * p : 128 * p + 128])
        both = jnp.concatenate(
            [head_mixing(cumulative, turned, 2 * p + q) * contact for q in range(2)], axis=1
        )
        within.append(dot3(both, pair, 1, 0))
    last = wide[BLOCK - 1 : BLOCK, :]
    core = jnp.concatenate(within, axis=1) + dot3(query, before, 1, 0) * jnp.exp(wide)
    after = jnp.exp(last) * before + dot3(keys, scaled * jnp.exp(last - wide), 0, 0)
    return core, after


def whole_kernel(
    hid, cot, in_ref, out_w, conv_in, gain_in, head_in,
    out_ref, igrad_ref, slabs, gos, total_small,
    n_ref, ct_ref, w_ref, z_ref, big_a, big_b, raw_ref, core_ref, y_ref, dm_ref, st_ref, dcore_ref,
    dp_ref, mixed_ref, po_ref, ra_ref, rb_ref, ra2_ref, rb2_ref, own_out, wq_f, wq, wo_ref, sm_ref, gain_ref, conv_ref,
    sums_ref, got_sums, turned_sums, rz, ro, own_o, gz, gz2, go, go2, rx, gx, gx2, ia_ref, ib_ref, ia2_ref, ib2_ref,
    piece_z, piece_x, ow_z, ow_x, slab_ref, piece_o_ref, small_out, smalls_dp, sg, sg_all, small, hd_ref, gvec, cvec, dgain_ref, dskip_ref, dconv_ref, dhead_ref,
    state, halo, hid_v, cot_v, send, recv, own,
):
    place = Place()
    me = place.s
    wq_load = pltpu.make_async_copy(
        in_ref.at[pl.ds(pl.multiple_of(48 * place.x, 8), 48), :], wq_f, own.at[7]
    )
    wq_load.start()
    wq[:, WIDE - 128 :] = jnp.zeros((48, 128), bf16)
    small[...] = jnp.zeros_like(small)
    small[:5, :416] = conv_in[...].astype(bf16).astype(f32)
    small[5:6, :576] = gain_in[...].astype(bf16).astype(f32)
    hd_ref[...] = jnp.zeros_like(hd_ref)
    hd_ref[:3, :6] = head_in[...].astype(bf16).astype(f32)
    hd_ref[3:4, :] = widen(hd_ref[:, :128])[2:3]
    barrier = pltpu.get_barrier_semaphore()
    core_peer = place.core_peer()
    bigs = [place.big_peer(k) for k in range(1, 8)]
    x_peers = bigs[:3]
    group = [place.shard_peer(k) for k in range(1, 8)]
    everyone = bigs + [core_peer] + [place.other_core_of(k) for k in range(1, 8)]
    for peer in group + everyone:
        pl.semaphore_signal(barrier, inc=1, device_id=peer, device_id_type=MESH)
    pl.semaphore_wait(barrier, 22)

    def remote(src, dst, index, peer, other=None):
        return pltpu.make_async_remote_copy(
            src_ref=src,
            dst_ref=dst,
            send_sem=send.at[index],
            recv_sem=recv.at[index if other is None else other],
            device_id=peer,
            device_id_type=MESH,
        )

    quarter = pl.multiple_of(48 * place.x, 16)

    def weight_parts(them):
        at = pl.multiple_of(them * OWN, 128)
        rows = pl.ds(quarter, 48)
        return (
            (wq.at[:, pl.ds(at, OWN)], w_ref.at[me, rows, pl.ds(0, OWN)]),
            (wq.at[:, pl.ds(at + DI, OWN)], w_ref.at[me, rows, pl.ds(OWN, OWN)]),
            (wq.at[:, pl.ds(2 * DI, OWN)], w_ref.at[me, rows, pl.ds(2 * OWN, OWN)]),
        )

    locals_ = [
        pltpu.make_async_copy(hid, n_ref.at[me], own.at[1]),
        pltpu.make_async_copy(cot, ct_ref.at[me], own.at[2]),
        pltpu.make_async_copy(hid, hid_v, own.at[3]),
        pltpu.make_async_copy(cot, cot_v, own.at[14]),
    ]
    for copy in locals_:
        copy.start()
    mine = place.yl == place.c
    wo_parts = [
        pltpu.make_async_copy(
            out_w.at[pl.ds(32 * (p % 12), 32), pl.ds(768 * (p // 12), 768)],
            big_a.at[p // 8, p % 8],
            own.at[17 + p],
        )
        for p in range(24)
    ]
    for copy in wo_parts:
        copy.start()
    wq_load.wait()
    wq[:, :PROJ] = wq_f[...].astype(bf16)
    own_w = [
        pltpu.make_async_copy(src, dst, own.at[4 + i])
        for i, (src, dst) in enumerate(weight_parts(me))
    ]
    smalls = [remote(small, sm_ref.at[me], k, place.shard_peer(k)) for k in range(1, 8)]
    hids = Gather(place, remote, hid, n_ref, 8)
    cots = Gather(place, remote, cot, ct_ref, 20)
    weights = []
    for k in range(1, 8):
        weights.append(
            [
                remote(src, dst, 40 + 3 * k + i, place.shard_peer(k))
                for i, (src, dst) in enumerate(weight_parts(place.shard_of(k)))
            ]
        )

    def w_begin(some):
        @pl.when(mine)
        def _():
            for i in some:
                own_w[i].start()
            for parts in weights:
                for i in some:
                    parts[i].start()

    w_begin((1, 2))
    for copy in smalls:
        copy.start()
    hids.begin()
    w_begin((0,))

    def w_arrived(some):
        for k in range(1, 8):
            @pl.when(lax.rem(place.yl + k // 4, 2) == place.c)
            def _(k=k):
                for i in some:
                    weights[k - 1][i].wait_recv()

        @pl.when(mine)
        def _():
            for i in some:
                own_w[i].wait()

    w_up, w_down = place.big_peer(1), place.big_peer(3)

    class Quarters:
        def __init__(self, columns, base):
            def quarter(k, lo=0, n=4):
                rows = pl.ds(pl.multiple_of(48 * lax.rem(place.x + k, 4), 16), 48)
                return w_ref.at[pl.ds(4 * place.c + lo, n), rows, columns]

            def on(view, index, peer):
                return remote(view, view, base + index, peer)

            self.copies = [
                on(quarter(0), 0, w_up),
                on(quarter(0), 1, w_down),
                on(quarter(0), 2, core_peer),
                on(quarter(3, 0, 2), 3, w_up),
                on(quarter(3), 4, core_peer),
                on(quarter(1, 2, 2), 5, w_down),
                on(quarter(1), 6, core_peer),
                on(quarter(2, 0, 2), 7, core_peer),
                on(quarter(2, 2, 2), 8, core_peer),
            ]

        def begin(self):
            for copy in self.copies[:3]:
                copy.start()

        def after(self, arrived, *indices):
            self.copies[arrived].wait_recv()
            for index in indices:
                self.copies[index].start()

        def first(self):
            self.after(0, 3, 4)
            self.after(1, 5, 6)

        def second(self):
            self.after(3, 7)
            self.after(5, 8)

        def last(self):
            for index in (2, 4, 6, 7, 8):
                self.copies[index].wait_recv()

    w_scan = Quarters(pl.ds(OWN, 768), 32)
    w_gate = Quarters(pl.ds(0, OWN), 240)
    w_arrived((1, 2))
    w_scan.begin()
    locals_[0].wait()
    hids.first()
    w_scan.first()
    hids.second()
    w_arrived((0,))
    w_gate.begin()
    cots.begin()
    w_scan.second()

    sm_ref[me] = small[...]
    for copy in smalls:
        copy.wait_recv()
    gain_ref[...] = jnp.concatenate([sm_ref[p, 5:6, :576] for p in range(8)], axis=1)
    conv_ref[...] = jnp.concatenate([sm_ref[p, :, :416] for p in range(8)], axis=1)
    gg_at = pl.ds(pl.multiple_of(D + OWN * me, 128), OWN)
    cv_at = pl.ds(pl.multiple_of(OWN * me, 128), OWN)

    def conv_row(k):
        return jnp.concatenate([conv_ref[k : k + 1, cv_at], conv_ref[k : k + 1, DI:]], axis=1)

    hids.last()
    hids.sent()
    w_scan.last()

    for copy in wo_parts:
        copy.wait()
    for p in range(24):
        at = 768 * (p // 12)
        rows = slice(32 * (p % 12), 32 * (p % 12) + 32)
        wo_ref[rows, at : at + 768] = big_a[p // 8, p % 8].astype(bf16)
    state[...] = jnp.zeros_like(state)
    halo[...] = jnp.zeros_like(halo)
    skip = hd_ref[3:4, :]

    @pl.loop(0, LEN // TB)
    def _(i):
        two = pl.ds(2 * i, 2)

        @pl.when(i == 1)
        def _():
            w_gate.first()

        @pl.when(i == 2)
        def _():
            w_gate.second()

        @pl.when(i == 3)
        def _():
            cots.first()

        u = n_ref[two].reshape(TB, D).astype(f32)
        scale = lax.rsqrt(jnp.mean(u * u, axis=1, keepdims=True) + epsilon)
        normed = (u * scale * gain_ref[:, :D]).astype(bf16)
        n_ref[two] = normed.reshape(2, BLOCK, D)
        project = dot(normed, w_ref[:, :, OWN:].reshape(D, 768), 1, 0)
        xbc = project[:, :640]
        raw = pltpu.roll(project[:, 640:], 128 - 6 * me, 1)
        big_a[i, :, :, :640] = xbc.reshape(8, 32, 640)
        raw_ref[two] = raw.reshape(2, BLOCK, 128)
        extended = jnp.concatenate([halo[...], xbc], axis=0)
        halo[...] = xbc[TB - 8 :, :]
        conv = conv_row(KCONV)
        for k in range(KCONV):
            conv = conv + conv_row(k) * extended[5 + k : 5 + k + TB, :]
        big_b[i, :, :, :640] = conv.reshape(8, 32, 640)
        act = conv * jax.nn.sigmoid(conv)
        dt = softplus(raw + hd_ref[0:1, :128])
        log_decay = -jnp.exp(hd_ref[1:2, :128]) * dt
        for j in range(TB // BLOCK):
            at = slice(j * BLOCK, (j + 1) * BLOCK)
            before = state[...]
            st_ref[2 * i + j] = before
            core, after = forward_block(act[at], dt[at], log_decay[at], before)
            state[...] = after
            core_ref[2 * i + j] = core
            y_ref[i, 4 * j : 4 * j + 4] = (core + skip * act[at, :OWN]).reshape(4, 32, OWN)

    cots.second()
    w_gate.last()

    @pl.loop(0, LEN // TB)
    def _(i):
        normed = n_ref[pl.ds(2 * i, 2)].reshape(TB, D)
        z = dot(normed, w_ref[:, :, :OWN].reshape(D, OWN), 1, 0)
        z_ref[i] = z.reshape(8, 32, OWN)

    locals_[1].wait()
    cots.last()

    @pl.loop(0, LEN // TB)
    def _(i):
        two = pl.ds(2 * i, 2)
        dm = dot(ct_ref[two].reshape(TB, D), wo_ref[...], 1, 1)
        dm_ref[i] = dm.reshape(8, 32, OWN)
        z = two_blocks(z_ref, i, OWN)
        gated = two_blocks(y_ref, i, OWN) * (z * jax.nn.sigmoid(z))
        ones = jnp.ones((8, OWN), f32)
        first = ones_dot(ones, gated * gated, 1, 1)
        second = ones_dot(ones, gated * (gain_ref[:, gg_at] * dm), 1, 1)
        for j in range(2):
            sums_ref[pl.ds(2 * i + j, 1), :] = first[0:1, 128 * j : 128 * j + 128]
            sums_ref[pl.ds(2 * i + j + 8, 1), :] = second[0:1, 128 * j : 128 * j + 128]

    sums = [remote(sums_ref, got_sums.at[me], 64 + k, place.shard_peer(k)) for k in range(1, 8)]
    for copy in sums:
        copy.start()
    got_sums[me] = sums_ref[...]
    for copy in sums:
        copy.wait_recv()
    totals = got_sums[0]
    for j in range(1, 8):
        totals += got_sums[j]
    turned_sums[...] = jnp.concatenate([totals, jnp.zeros((112, 128), f32)], axis=0).T
    gain = gain_ref[:, gg_at]
    lane = lanes((BLOCK, 128))
    dgain_ref[...] = jnp.zeros_like(dgain_ref)
    dskip_ref[...] = jnp.zeros_like(dskip_ref)
    dconv_ref[...] = jnp.zeros_like(dconv_ref)
    dhead_ref[...] = jnp.zeros_like(dhead_ref)

    outs = Scatter(place, remote, po_ref, ra_ref, rb_ref, ra2_ref, rb2_ref, own_out, 72)

    @pl.loop(0, BLOCKS)
    def _(i):
        b = lax.rem(me + 1 + i, BLOCKS)
        column = turned_sums[...]
        first = jnp.sum(jnp.where(lane == b, column, 0.0), axis=1, keepdims=True)
        second = jnp.sum(jnp.where(lane == b + 8, column, 0.0), axis=1, keepdims=True)
        z, y, dm = block_of(z_ref, b, OWN), block_of(y_ref, b, OWN), block_of(dm_ref, b, OWN)
        sig_z = jax.nn.sigmoid(z)
        gate = z * sig_z
        scale = lax.rsqrt(first * (1.0 / DI) + epsilon)
        unit = y * gate * scale
        mixed = (unit * gain).astype(bf16)
        mixed_ref[b] = mixed
        dgain_ref[0:1, :] += jnp.sum(dm * unit, axis=0, keepdims=True)
        dgated = scale * (gain * dm) - unit * (scale * scale * (second * (1.0 / DI)))
        dz = dgated * y * (sig_z * (1.0 + z * (1.0 - sig_z)))
        dp_ref[b, :, :OWN] = dz.astype(bf16)
        dcore_ref[b] = dgated * gate
        po_ref[b] = dot(mixed, wo_ref[...], 1, 0).astype(bf16)
        outs.send(b)

    def weight_grad(q, columns):
        left = n_ref[:, :, pl.ds(pl.multiple_of(384 * q, 128), 384)].reshape(LEN, 384)
        return dot(left, dp_ref[:, :, columns].reshape(LEN, -1), 0, 0)

    def out_grad(h, q):
        at = pl.multiple_of(768 * h + 384 * q, 128)
        return dot(mixed_ref[...].reshape(LEN, OWN), ct_ref[:, :, pl.ds(at, 384)].reshape(LEN, 384), 0, 0)

    other = 1 - place.c
    zs = slice(0, OWN)
    late = slice(OWN, COLS)

    def rows24(ref):
        return ref.at[:, :, pl.ds(0, 24), :]

    @pl.loop(0, 2)
    def _(q):
        two = pl.ds(2 * q, 2)
        y_ref[two, :, :24, :] = weight_grad(2 * other + q, zs).reshape(2, 8, 24, OWN)
        z_ref[two, :, :24, :] = out_grad(other, q).reshape(2, 8, 24, OWN)

    swap_z = remote(rows24(y_ref), rz, 156, core_peer)
    swap_o = remote(rows24(z_ref), ro, 157, core_peer)
    swap_z.start()
    swap_o.start()

    @pl.loop(0, 2)
    def _(q):
        two = pl.ds(2 * q, 2)
        dm_ref[two, :, :24, :] = weight_grad(2 * place.c + q, zs).reshape(2, 8, 24, OWN)
        own_o[q] = out_grad(place.c, q).reshape(8, 2, 24, OWN)

    def rows_fns(ref, first, n):
        some = pl.ds(first, n)

        def view(big):
            return ref.at[some, big, pl.ds(0, 24), :]

        def read(big):
            return ref[some, big, :24, :]

        def write(big, total):
            ref[some, big, :24, :] = total

        return view, read, write

    def write_o(big, total):
        own_o[:, big] = total

    sum_z = Reduce(place, remote, *rows_fns(dm_ref, 0, 4), gz, gz2, 92)
    sum_x = Reduce(place, remote, *rows_fns(big_b, 0, 4), gx, gx2, 102)
    sum_o = Reduce(
        place, remote, lambda big: own_o.at[:, big], lambda big: own_o[:, big], write_o, go, go2, 112
    )

    state[...] = jnp.zeros_like(state)
    halo[...] = jnp.zeros_like(halo)

    @pl.loop(0, BLOCKS)
    def _(i):
        b = BLOCKS - 1 - i

        @pl.when(i == 1)
        def _():
            swap_z.wait_recv()
            swap_o.wait_recv()
            for r in range(4):
                dm_ref[r, :, :24, :] += rz[r]
            for q in range(2):
                own_o[q] += ro[2 * q : 2 * q + 2].reshape(8, 2, 24, OWN)
            sum_z.begin()
            sum_o.begin()

        pl.when(i == 5)(outs.middle)

        conv = block_of(big_b, b, 640)
        raw, core, dcore = raw_ref[b], core_ref[b], dcore_ref[b]
        sig = jax.nn.sigmoid(conv)
        act = conv * sig
        x, keys, query = act[:, :OWN], act[:, OWN : OWN + NS], act[:, OWN + NS :]
        shifted = raw + hd_ref[0:1, :128]
        dt = softplus(shifted)
        rate = jnp.exp(hd_ref[1:2, :128])
        log_decay = -rate * dt
        dskip_ref[0:1, :] += jnp.sum(dcore * x, axis=0, keepdims=True)
        cumulative, turned, wide = decay_parts(log_decay)
        contact = dot3(query, keys, 1, 1)
        dt_wide = widen(dt)
        scaled = x * dt_wide
        dcontact = jnp.zeros((BLOCK, BLOCK), f32)
        dscaled = []
        for p in range(3):
            at = slice(128 * p, 128 * p + 128)
            mixing = [head_mixing(cumulative, turned, 2 * p + q) for q in range(2)]
            both = jnp.concatenate([m * contact for m in mixing], axis=0)
            pair = split_pair(dcore[:, at])
            dscaled.append(dot3(both, pair, 0, 0))
            dmix = dot3(pair, scaled[:, at], 1, 1)
            dcontact += dmix[:BLOCK] * mixing[0] + dmix[BLOCK:] * mixing[1]
        last = wide[BLOCK - 1 : BLOCK, :]
        before = st_ref[b]
        after_adj = state[...]
        left = jnp.exp(last - wide)
        from_core = dcore * jnp.exp(wide)
        dquery = dot3(from_core, before, 1, 1) + dot3(dcontact, keys, 1, 0)
        carried = dot3(keys, after_adj, 1, 0) * left
        dscaled = jnp.concatenate(dscaled, axis=1) + carried
        dkeys = dot3(scaled * left, after_adj, 1, 1) + dot3(dcontact, query, 0, 0)
        end = jnp.exp(last)
        state[...] = end * after_adj + dot3(query, from_core, 0, 0)
        heads = head_ones()
        last_add = dot_exact(
            jnp.sum(carried * scaled, axis=0, keepdims=True)
            + end * jnp.sum(after_adj * before, axis=0, keepdims=True),
            heads, 1, 0,
        )
        dcum = dot_exact(dcore * core - dscaled * scaled, heads, 1, 0)
        dlog = ones_dot(lower_ones(), dcum, 0, 0) + last_add
        ddt = dot_exact(dscaled * x, heads, 1, 0) - rate * dlog
        draw = ddt * jax.nn.sigmoid(shifted)
        dhead_ref[0:1, :] += jnp.sum(draw, axis=0, keepdims=True)
        dhead_ref[1:2, :] += jnp.sum(dlog * log_decay, axis=0, keepdims=True)
        dx = dscaled * dt_wide + skip * dcore
        dact = jnp.concatenate([dx, dkeys, dquery], axis=1)
        dconv = dact * (sig * (1.0 + conv * (1.0 - sig)))
        extended = jnp.concatenate([dconv, halo[...]], axis=0)
        halo[...] = dconv[:8, :]
        xbc = block_of(big_a, b, 640)
        dxbc = jnp.zeros_like(xbc)
        for k in range(KCONV):
            moved = extended[3 - k : 3 - k + BLOCK, :]
            dxbc += conv_row(k) * moved
            dconv_ref[k : k + 1, :] += jnp.sum(xbc * moved, axis=0, keepdims=True)
        dconv_ref[KCONV : KCONV + 1, :] += jnp.sum(dconv, axis=0, keepdims=True)
        dp_ref[b, :, OWN : OWN + 640] = dxbc.astype(bf16)
        draw_own = jnp.where(lane < 6, draw, 0.0)
        dp_ref[b, :, 1024:] = pltpu.roll(draw_own, 6 * me, 1).astype(bf16)

    @pl.loop(0, 2)
    def _(q):
        two = pl.ds(2 * q, 2)
        big_a[two, :, :24, :] = weight_grad(2 * other + q, late).reshape(2, 8, 24, 768)

    swap_x = remote(rows24(big_a), rx, 158, core_peer)
    swap_x.start()

    @pl.loop(0, 2)
    def _(q):
        two = pl.ds(2 * q, 2)
        big_b[two, :, :24, :] = weight_grad(2 * place.c + q, late).reshape(2, 8, 24, 768)

    cots.sent()
    ins = Scatter(place, remote, ct_ref, ia_ref, ib_ref, ia2_ref, ib2_ref, own_out, 122)

    @pl.loop(0, BLOCKS)
    def _(i):
        b = lax.rem(me + 1 + i, BLOCKS)
        ct_ref[b] = dot(dp_ref[b], w_ref[...].reshape(D, COLS), 1, 1).astype(bf16)
        ins.send(b)

        @pl.when(i == 3)
        def _():
            swap_x.wait_recv()
            for r in range(4):
                big_b[r, :, :24, :] += rx[r]
            sum_x.begin()

    sum_z.middle()
    sum_o.middle()

    at_o = pl.multiple_of(768 * place.c, 128)
    o_all = Spread(
        place, remote, piece_o_ref,
        lambda big, lo, hi: gos.at[big, :, pl.ds(pl.multiple_of(at_o + lo, 128), hi - lo)],
        (256, 384, 768), 160,
    )
    z_all = Spread(
        place, remote, slab_ref.at[:, pl.ds(0, DI)],
        lambda big, lo, hi: slabs.at[big, :, pl.ds(lo, hi - lo)], (768, 1536, DI), 180,
    )
    x_all = Direct(
        place, remote, slab_ref.at[:, pl.ds(DI, WIDE - DI)],
        lambda big: slabs.at[big, :, pl.ds(DI, WIDE - DI)], 200,
    )

    def to_owners(piece, ow, base):
        copies = []
        for k in range(1, 8):
            them = place.shard_of(k)
            copy = remote(piece.at[lax.rem(them, 4)], ow.at[me], base + k, place.shard_peer(k))
            goes = them // 4 == place.c
            pl.when(goes)(copy.start)
            copies.append((copy, goes))

        @pl.when(mine)
        def _():
            ow[me] = piece[place.z]

        return copies

    piece_z[...] = sum_z.last()
    owners_z = to_owners(piece_z, ow_z, 140)
    total_o = sum_o.last()
    for q in range(2):
        piece_o_ref[:, 384 * q : 384 * q + 384] = total_o[q].reshape(48, 384).astype(bf16)
    o_all.begin()
    own_go = pltpu.make_async_copy(
        piece_o_ref, gos.at[place.big, :, pl.ds(at_o, 768)], own.at[15]
    )
    own_go.start()

    outs.last()
    locals_[2].wait()
    out_ref[...] = (own_out[...] + hid_v[...].astype(f32)).astype(bf16)

    @pl.when(mine)
    def _():
        for copy, _ in owners_z:
            copy.wait_recv()
        for j in range(8):
            slab_ref[:, OWN * j : OWN * (j + 1)] = ow_z[j].astype(bf16)
        z_all.begin()

    ins.middle()
    for n in range(4):
        o_all.step(n)
        pl.when(mine)(functools.partial(z_all.step, n))
    sum_x.middle()
    for n in range(4, 8):
        o_all.step(n)
        pl.when(mine)(functools.partial(z_all.step, n))
    piece_x[...] = sum_x.last()
    owners_x = to_owners(piece_x, ow_x, 232)
    ins.last()
    locals_[3].wait()
    u = hid_v[...].astype(f32)
    scale = lax.rsqrt(jnp.mean(u * u, axis=1, keepdims=True) + epsilon)
    d_normed = own_out[...]
    gained = gain_ref[:, :D] * d_normed
    unit = u * scale
    grad = scale * gained - unit * (scale * scale * jnp.mean(u * gained, axis=1, keepdims=True))
    igrad_ref[...] = (cot_v[...].astype(f32) + grad).astype(bf16)

    sg[...] = jnp.zeros_like(sg)
    sg[0:1, :] = jnp.sum(d_normed * unit, axis=0, keepdims=True)
    sg[1:6, :640] = dconv_ref[0:5, :]
    sg[1:2, 640:1024] = dgain_ref[0:1, :]
    sgs = [remote(sg, sg_all.at[me], 148 + k, place.shard_peer(k)) for k in range(1, 8)]
    for copy in sgs:
        copy.start()
    sg_all[me] = sg[...]

    @pl.when(mine)
    def _():
        for copy, _ in owners_x:
            copy.wait_recv()
        common = ow_x[0, :, OWN:]
        for j in range(1, 8):
            common += ow_x[j, :, OWN:]
        for j in range(8):
            slab_ref[:, DI + OWN * j : DI + OWN * (j + 1)] = ow_x[j, :, :OWN].astype(bf16)
        slab_ref[:, 2 * DI :] = common.astype(bf16)
        x_all.begin()

    own_slab = pltpu.make_async_copy(slab_ref, slabs.at[place.big], own.at[16])
    pl.when(mine)(own_slab.start)
    for copy in sgs:
        copy.wait_recv()
    small_out[...] = jnp.zeros_like(small_out)
    gvec[:, :D] = sg_all[0, 0:1, :]
    cvec[...] = jnp.zeros_like(cvec)
    cvec[:5, DI:CONVC] = sg_all[0, 1:6, OWN:640]
    for j in range(1, 8):
        gvec[:, :D] += sg_all[j, 0:1, :]
        cvec[:5, DI:CONVC] += sg_all[j, 1:6, OWN:640]
    for j in range(8):
        gvec[:, D + OWN * j : D + OWN * (j + 1)] = sg_all[j, 1:2, 640:1024]
        cvec[:5, OWN * j : OWN * (j + 1)] = sg_all[j, 1:6, :OWN]
    near = gvec[:, pl.ds(pl.multiple_of(128 * (9 * me // 2), 128), 640)]
    small_out[5:6, :576] = jnp.where(lax.rem(me, 2) == 1, near[:, 64:640], near[:, :576])
    near = cvec[:, pl.ds(pl.multiple_of(128 * (13 * me // 4), 128), 640)]
    shift = lax.rem(13 * me, 4)
    taps = near[:, :416]
    for k in range(1, 4):
        taps = jnp.where(shift == k, near[:, 32 * k : 32 * k + 416], taps)
    small_out[:5, :416] = taps[:5]
    small_out[6:7, :128] = dhead_ref[0:1, :]
    small_out[6:7, 128:256] = dhead_ref[1:2, :]
    small_out[6:7, 256:384] = dot_exact(dskip_ref[0:1, :], head_ones(), 1, 0)
    dps = [remote(small_out, smalls_dp.at[place.d], 216 + n, peer) for n, peer in enumerate(everyone)]
    for copy in dps:
        copy.start()
    smalls_dp[place.d] = small_out[...]

    @pl.when(mine)
    def _():
        x_all.forward()
        own_slab.wait()

    @pl.when(jnp.logical_not(mine))
    def _():
        for copy in z_all.cores + x_all.cores:
            copy.wait_recv()

    for copy in o_all.cores:
        copy.wait_recv()
    own_go.wait()
    for copy in dps:
        copy.wait_recv()
    total = smalls_dp[0]
    for j in range(1, 16):
        total += smalls_dp[j]
    total_small[...] = total

    for copy in smalls + sums + w_scan.copies + w_gate.copies + sgs + dps + [swap_z, swap_o, swap_x]:
        copy.wait_send()
    for group_of in (outs, ins, sum_z, sum_o, sum_x, o_all):
        group_of.sent()
    for copy, goes in owners_z + owners_x:
        pl.when(goes)(copy.wait_send)

    @pl.when(mine)
    def _():
        z_all.sent()
        x_all.sent()
        for parts in weights:
            for copy in parts:
                copy.wait_send()


def sds(shape, dtype=f32):
    return jax.ShapeDtypeStruct(shape, dtype)


def run_whole(hid, cot, in_master, out_master, conv, gain, head):
    any_spec = pl.BlockSpec(memory_space=pl.ANY)
    vmem = pl.BlockSpec(memory_space=pltpu.VMEM)

    def v(*shape, dtype=f32):
        return pltpu.VMEM(shape, dtype)

    tokens = (8, BLOCK, D)
    part = (8, BLOCK, OWN)
    split = (4, 8, 32, OWN)
    landing = [
        v(4, 2, TOP, D, dtype=bf16), v(4, BLOCK - TOP, D, dtype=bf16), v(TOP, D, dtype=bf16),
        v(4, BLOCK - TOP, D, dtype=bf16),
    ]
    return pl.pallas_call(
        whole_kernel,
        in_specs=[any_spec] * 4 + [vmem] * 3,
        out_specs=(vmem, vmem, any_spec, any_spec, vmem),
        out_shape=(
            sds((BLOCK, D), bf16), sds((BLOCK, D), bf16), sds((8, 24, WIDE), bf16),
            sds((8, 48, D), bf16), sds((8, 640)),
        ),
        scratch_shapes=[
            v(*tokens, dtype=bf16), v(*tokens, dtype=bf16), v(8, 192, COLS, dtype=bf16), v(*split),
            v(4, 8, 32, 768), v(4, 8, 32, 768), v(8, BLOCK, 128), v(*part), v(*split), v(*split),
            v(8, NS, OWN), v(*part),
            v(8, BLOCK, COLS, dtype=bf16), v(*part, dtype=bf16), v(*tokens, dtype=bf16),
            *landing, v(BLOCK, D), v(48, PROJ),
            v(48, WIDE, dtype=bf16),
            v(OWN, D, dtype=bf16), v(8, 8, 640), v(1, 4608), v(8, CONVC),
            v(16, 128), v(8, 16, 128), v(BLOCK, 128), v(4, 8, 24, OWN), v(4, 8, 24, OWN),
            v(2, 8, 2, 24, OWN), v(3, 2, 4, 24, OWN), v(4, 24, OWN), v(3, 2, 2, 2, 24, OWN),
            v(2, 2, 24, OWN), v(4, 8, 24, 768), v(3, 2, 4, 24, 768), v(4, 24, 768), *landing,
            v(4, 24, OWN), v(4, 24, 768), v(8, 24, OWN), v(8, 24, 768),
            v(24, WIDE, dtype=bf16), v(48, 768, dtype=bf16), v(8, 640), v(16, 8, 640), v(8, D), v(8, 8, D), v(8, 640), v(8, OWN), v(1, 4736),
            v(8, 3456), v(8, OWN), v(8, OWN), v(8, 640), v(8, 128), v(NS, OWN), v(8, 640), v(BLOCK, D, dtype=bf16), v(BLOCK, D, dtype=bf16),
            pltpu.SemaphoreType.DMA((250,)), pltpu.SemaphoreType.DMA((250,)),
            pltpu.SemaphoreType.DMA((41,)),
        ],
        compiler_params=pltpu.CompilerParams(
            collective_id=1, has_side_effects=True, vmem_limit_bytes=62 * 2**20
        ),
    )(hid, cot, in_master, out_master, conv, gain, head)


class Spread:
    def __init__(self, place, remote, src, view, cuts, base):
        one, two, end = cuts

        def at(dy, dx, lo, hi):
            return view(lax.rem(place.yh + dy, 2) * 4 + lax.rem(place.x + dx, 4), lo, hi)

        def onward(part, index, peer):
            return remote(part, part, base + index, peer)

        up, down, over = place.big_peer(1), place.big_peer(3), place.big_peer(4)
        own = view(place.big, 0, end)
        self.copies = [
            remote(src, own, base, up),
            remote(src, own, base + 1, down),
            remote(src, own, base + 2, over),
            onward(at(0, 3, 0, two), 3, up),
            onward(at(0, 1, two, end), 4, down),
            onward(at(0, 3, two, end), 5, over),
            onward(at(0, 1, two, end), 6, over),
            onward(at(0, 2, two, end), 7, over),
            onward(at(1, 0, 0, two), 8, up),
            onward(at(1, 0, 0, two), 9, down),
            onward(at(1, 3, 0, one), 10, up),
            onward(at(1, 1, one, two), 11, down),
        ]
        core = place.core_peer()
        self.cores = [remote(src, own, base + 12, core)]
        for n, (dy, dx, _, _) in enumerate(ARRIVALS[1:]):
            block = at(dy, dx, 0, end)
            self.cores.append(remote(block, block, base + 13 + n, core))

    def begin(self):
        for index in (2, 0, 1):
            self.copies[index].start()
        self.cores[0].start()

    def step(self, n):
        _, _, needs, sends = ARRIVALS[n]
        for index in needs:
            self.copies[index].wait_recv()
        for index in sends:
            self.copies[index].start()
        if n:
            self.cores[n].start()

    def sent(self):
        for copy in self.copies + self.cores:
            copy.wait_send()


ARRIVALS = (
    (0, 0, (), ()),
    (1, 0, (2,), (8, 9)),
    (0, 3, (0,), (3, 5)),
    (0, 1, (1,), (4, 6)),
    (0, 2, (3, 4), (7,)),
    (1, 3, (8, 5), (10,)),
    (1, 1, (9, 6), (11,)),
    (1, 2, (10, 11, 7), ()),
)


def adam_update(master, first, second, gradient, rate, decay):
    first_new = beta_one * first + (1.0 - beta_one) * gradient
    second_new = beta_two * second + (1.0 - beta_two) * gradient * gradient
    scaled = (
        first_new
        / (1.0 - beta_one**STEP)
        / (jnp.sqrt(second_new / (1.0 - beta_two**STEP)) + adam_epsilon)
    )
    return (first_new, second_new, master - rate * (scaled + decay * master))


def on_device(
    hidden, cotangent, in_master, in_first, in_second, out_master, out_first, out_second,
    gain_master, gain_first, gain_second, conv_master, conv_first, conv_second,
    head_master, head_first, head_second,
):
    layer_out, input_grad, total_w, total_o, total = run_whole(
        hidden[0], cotangent[0], in_master, out_master, conv_master, gain_master[None], head_master
    )
    gradients = (
        total_w.reshape(192, WIDE)[:, :PROJ].astype(f32), total_o.reshape(OWN, D).astype(f32),
        total[5, :576], total[:5, :416],
        jnp.stack([total[6, :6], total[6, 128:134], total[6, 256:262]]),
    )
    masters = (in_master, out_master, gain_master, conv_master, head_master)
    firsts = (in_first, out_first, gain_first, conv_first, head_first)
    seconds = (in_second, out_second, gain_second, conv_second, head_second)
    updated = [
        adam_update(masters[g], firsts[g], seconds[g], gradients[g], rates[g], decays[g])
        for g in range(5)
    ]
    return (layer_out[None], input_grad[None]) + tuple(v for group in updated for v in group)


def solution(mesh):
    rows, columns = P("shard", None), P(None, "shard")
    tokens = P("dp", "shard", None)
    state = (rows,) * 6 + (P("shard"),) * 3 + (columns,) * 6
    return jax.shard_map(
        on_device,
        mesh=mesh,
        in_specs=(tokens, tokens) + state,
        out_specs=(tokens, tokens) + state,
        check_vma=False,
    )
```

```python
import functools

import jax
import jax.numpy as jnp
from jax import lax
from jax.experimental import pallas as pl
from jax.experimental.pallas import tpu as pltpu
from jax.sharding import PartitionSpec as P

D = 1536
DI = 3072
H = 48
HD = 64
NS = 128
KCONV = 4
STEP = 5
BLOCK = 128
CONVC = 3328
PROJ = 6448
LEN = 1024
OWN = 384
COLS = 1152
WIDE = 6528
BLOCKS = LEN // BLOCK

f32 = jnp.float32
bf16 = jnp.bfloat16
highest = lax.Precision.HIGHEST
MESH = pl.DeviceIdType.MESH
epsilon = 1e-05
beta_one = 0.9
beta_two = 0.95
adam_epsilon = 1e-08
rates = (0.05, 0.04, 0.25, 0.5, 0.5)
decays = (0.1, 0.1, 0.0, 0.0, 0.0)
TOP = 80


class Place:
    def __init__(self):
        self.d = lax.axis_index("dp")
        self.s = lax.axis_index("shard")
        self.c = lax.rem(self.d, 2)
        self.x = lax.rem(self.d // 2, 4)
        self.yh = self.d // 8
        self.big = self.d // 2
        self.z = lax.rem(self.s, 4)
        self.yl = self.s // 4

    def shard_of(self, k):
        return lax.rem(self.yl + k // 4, 2) * 4 + lax.rem(self.z + k % 4, 4)

    def shard_peer(self, k):
        return (self.d, self.shard_of(k))

    def big_of(self, k):
        return lax.rem(self.yh + k // 4, 2) * 4 + lax.rem(self.x + k % 4, 4)

    def big_peer(self, k):
        return (self.big_of(k) * 2 + self.c, self.s)

    def z_peer(self, k):
        return (self.d, self.yl * 4 + lax.rem(self.z + k, 4))

    def y_partner(self):
        return (self.d, (1 - self.yl) * 4 + self.z)

    def core_peer(self):
        return (self.big * 2 + 1 - self.c, self.s)

    def other_core_of(self, k):
        return (self.big_of(k) * 2 + 1 - self.c, self.s)


class Gather:
    def __init__(self, place, remote, src, buf, base):
        def at(dy, dz, lo, hi):
            index = lax.rem(place.yl + dy, 2) * 4 + lax.rem(place.z + dz, 4)
            return buf.at[index, pl.ds(lo, hi - lo)]

        def onward(view, index, peer):
            return remote(view, view, base + index, peer)

        up, down, over = place.z_peer(1), place.z_peer(3), place.y_partner()
        self.copies = [
            remote(src, buf.at[place.s], base, up),
            remote(src, buf.at[place.s], base + 1, down),
            remote(src, buf.at[place.s], base + 2, over),
            onward(at(0, 3, 0, 64), 3, up),
            onward(at(0, 1, 64, 128), 4, down),
            onward(at(0, 3, 64, 128), 5, over),
            onward(at(0, 1, 64, 128), 6, over),
            onward(at(0, 2, 64, 128), 7, over),
            onward(at(1, 0, 0, 64), 8, up),
            onward(at(1, 0, 0, 64), 9, down),
            onward(at(1, 3, 0, 32), 10, up),
            onward(at(1, 1, 32, 64), 11, down),
        ]

    def after(self, arrived, *indices):
        self.copies[arrived].wait_recv()
        for index in indices:
            self.copies[index].start()

    def begin(self):
        for copy in (self.copies[2], self.copies[0], self.copies[1]):
            copy.start()

    def first(self):
        self.after(2, 8, 9)
        self.after(0, 3, 5)
        self.after(1, 4, 6)

    def second(self):
        self.after(8, 10)
        self.after(9, 11)
        self.after(4, 7)

    def last(self):
        for index in (3, 5, 6, 7, 10, 11):
            self.copies[index].wait_recv()

    def sent(self):
        for copy in self.copies:
            copy.wait_send()


class Scatter:
    def __init__(self, place, remote, part, ra, rb, ra2, rb2, total, base):
        self.place, self.remote, self.base = place, remote, base
        self.part, self.ra, self.rb, self.ra2, self.rb2, self.total = part, ra, rb, ra2, rb2, total
        self.top, self.low = pl.ds(0, TOP), pl.ds(TOP, BLOCK - TOP)

    def along_z(self, b, source):
        place = self.place
        return self.remote(
            self.part.at[b, self.top],
            self.ra.at[place.z, b // 4],
            self.base + b,
            (place.d, place.yl * 4 + lax.rem(b, 4)),
            self.base + source * 2 + b // 4,
        )

    def along_y(self, b):
        z = lax.rem(b, 4)
        return self.remote(
            self.part.at[b, self.low], self.rb.at[z], self.base + 8 + z, self.place.y_partner()
        )

    def send(self, b):
        pl.when(lax.rem(b, 4) != self.place.z)(self.along_z(b, self.place.z).start)
        pl.when(b // 4 != self.place.yl)(self.along_y(b).start)

    def other(self):
        return (1 - self.place.yl) * 4 + self.place.z

    def over(self):
        return self.remote(
            self.part.at[self.other(), self.top], self.ra2, self.base + 12, self.place.y_partner()
        )

    def back(self, z):
        place = self.place
        return self.remote(
            self.part.at[place.yl * 4 + z, self.low],
            self.rb2.at[place.z],
            self.base + 13 + z,
            (place.d, place.yl * 4 + z),
            self.base + 13 + place.z,
        )

    def others(self):
        return [lax.rem(self.place.z + k, 4) for k in (1, 2, 3)]

    def middle(self):
        place, part = self.place, self.part
        for z in self.others():
            for y in range(2):
                self.along_z(y * 4 + z, z).wait_recv()

        def sum_z(block, y):
            total = part[block, :TOP].astype(f32)
            for z in self.others():
                total += self.ra[z, y].astype(f32)
            return total

        part[self.other(), :TOP] = sum_z(self.other(), 1 - place.yl).astype(bf16)
        self.over().start()
        self.total[:TOP] = sum_z(place.s, place.yl)
        for z in range(4):
            self.along_y((1 - place.yl) * 4 + z).wait_recv()
        for z in self.others():
            block = place.yl * 4 + z
            part[block, TOP:] = (part[block, TOP:].astype(f32) + self.rb[z].astype(f32)).astype(bf16)
            self.back(z).start()
        self.total[TOP:] = part[place.s, TOP:].astype(f32) + self.rb[place.z].astype(f32)

    def last(self):
        self.over().wait_recv()
        self.total[:TOP] += self.ra2[...].astype(f32)
        for z in self.others():
            self.remote(
                self.part.at[self.place.yl * 4 + z, self.low], self.rb2.at[z],
                self.base + 13 + z, (self.place.d, self.place.yl * 4 + z),
            ).wait_recv()
            self.total[TOP:] += self.rb2[z].astype(f32)

    def sent(self):
        place = self.place
        for z in self.others():
            for y in range(2):
                self.along_z(y * 4 + z, place.z).wait_send()
            self.back(z).wait_send()
        for z in range(4):
            self.along_y((1 - place.yl) * 4 + z).wait_send()
        self.over().wait_send()


class Reduce:
    def __init__(self, place, remote, view, read, write, gx, gy, base):
        self.place, self.view, self.read, self.write, self.gx, self.gy = place, view, read, write, gx, gy
        self.along = [
            remote(
                view(y * 4 + lax.rem(place.x + k, 4)), gx.at[k - 1, y], base + 2 * k + y,
                place.big_peer(k),
            )
            for k in (1, 2, 3)
            for y in range(2)
        ]
        self.other = (1 - place.yh) * 4 + place.x
        self.over = remote(view(self.other), gy, base + 8, place.big_peer(4))

    def begin(self):
        for copy in self.along:
            copy.start()

    def total(self, big, y):
        total = self.read(big)
        for k in range(3):
            total += self.gx[k, y]
        return total

    def middle(self):
        for copy in self.along:
            copy.wait_recv()
        self.write(self.other, self.total(self.other, 1 - self.place.yh))
        self.over.start()

    def last(self):
        total = self.total(self.place.big, self.place.yh)
        self.over.wait_recv()
        return total + self.gy[...]

    def sent(self):
        for copy in self.along + [self.over]:
            copy.wait_send()


class Direct:
    def __init__(self, place, remote, src, view, base):
        own, core = view(place.big), place.core_peer()
        self.copies = [remote(src, own, base + k, place.big_peer(k)) for k in range(1, 8)]
        self.cores = [remote(src, own, base + 8, core)]
        for k in range(1, 8):
            block = view(lax.rem(place.yh + k // 4, 2) * 4 + lax.rem(place.x + 4 - k % 4, 4))
            self.cores.append(remote(block, block, base + 8 + k, core))

    def begin(self):
        for copy in self.copies + self.cores[:1]:
            copy.start()

    def forward(self):
        for k in range(1, 8):
            self.copies[k - 1].wait_recv()
            self.cores[k].start()

    def sent(self):
        for copy in self.copies + self.cores:
            copy.wait_send()


def dot(a, b, ca, cb, precision=None):
    return lax.dot_general(
        a, b, (((ca,), (cb,)), ((), ())), precision=precision, preferred_element_type=f32
    )


def mm(a, b, ca=1, cb=0):
    return dot(a.astype(f32), b.astype(f32), ca, cb, highest)


def lanes(shape):
    return lax.broadcasted_iota(jnp.int32, shape, 1)


def rows_of(shape):
    return lax.broadcasted_iota(jnp.int32, shape, 0)


def widen(m):
    low = lanes((m.shape[0], 128)) < HD
    return jnp.concatenate(
        [jnp.where(low, m[:, 2 * i : 2 * i + 1], m[:, 2 * i + 1 : 2 * i + 2]) for i in range(3)],
        axis=1,
    )


def lower_ones():
    return (rows_of((BLOCK, BLOCK)) >= lanes((BLOCK, BLOCK))).astype(f32)


def head_ones():
    return (rows_of((OWN, BLOCK)) // HD == lanes((OWN, BLOCK))).astype(f32)


def split_pair(pair):
    low = lanes(pair.shape) < HD
    zero = jnp.zeros_like(pair)
    return jnp.concatenate([jnp.where(low, pair, zero), jnp.where(low, zero, pair)], axis=0)


def head_mixing(cumulative, turned, h):
    causal = rows_of((BLOCK, BLOCK)) >= lanes((BLOCK, BLOCK))
    differ = cumulative[:, h : h + 1] - turned[h : h + 1, :]
    return jnp.exp(jnp.where(causal, differ, -jnp.inf))


def softplus(v):
    return jnp.maximum(v, 0.0) + jnp.log1p(jnp.exp(-jnp.abs(v)))


TB = 256
HALF = DI // 8


def dot3(a, b, ca, cb):
    a_hi, b_hi = a.astype(bf16), b.astype(bf16)
    a_lo, b_lo = (a - a_hi.astype(f32)).astype(bf16), (b - b_hi.astype(f32)).astype(bf16)
    left = jnp.concatenate([a_hi, a_hi, a_lo], axis=ca)
    right = jnp.concatenate([b_hi, b_lo, b_hi], axis=cb)
    return dot(left, right, ca, cb)


def dot_exact(a, ones, ca, cb):
    a_hi = a.astype(bf16)
    a_lo = (a - a_hi.astype(f32)).astype(bf16)
    low = ones.astype(bf16)
    return dot(
        jnp.concatenate([a_hi, a_lo], axis=ca), jnp.concatenate([low, low], axis=cb), ca, cb
    )


def ones_dot(ones, a, ca, cb):
    a_hi = a.astype(bf16)
    a_lo = (a - a_hi.astype(f32)).astype(bf16)
    low = ones.astype(bf16)
    return dot(
        jnp.concatenate([low, low], axis=ca), jnp.concatenate([a_hi, a_lo], axis=cb), ca, cb
    )


def decay_parts(log_decay):
    cumulative = ones_dot(lower_ones(), log_decay, 1, 0)
    return cumulative, cumulative.T, widen(cumulative)


def two_blocks(ref, i, columns):
    return ref[i, :, :, :columns].reshape(TB, columns)


def block_of(ref, b, columns):
    four = pl.ds(4 * lax.rem(b, 2), 4)
    return ref[b // 2, four, :, :columns].reshape(BLOCK, columns)


def forward_block(act, dt, log_decay, before):
    x, keys, query = act[:, :OWN], act[:, OWN : OWN + NS], act[:, OWN + NS :]
    cumulative, turned, wide = decay_parts(log_decay)
    contact = dot3(query, keys, 1, 1)
    scaled = x * widen(dt)
    within = []
    for p in range(3):
        pair = split_pair(scaled[:, 128 * p : 128 * p + 128])
        both = jnp.concatenate(
            [head_mixing(cumulative, turned, 2 * p + q) * contact for q in range(2)], axis=1
        )
        within.append(dot3(both, pair, 1, 0))
    last = wide[BLOCK - 1 : BLOCK, :]
    core = jnp.concatenate(within, axis=1) + dot3(query, before, 1, 0) * jnp.exp(wide)
    after = jnp.exp(last) * before + dot3(keys, scaled * jnp.exp(last - wide), 0, 0)
    return core, after


def whole_kernel(
    hid, cot, in_ref, out_w, conv_in, gain_in, head_in,
    out_ref, igrad_ref, slabs, gos, total_small,
    n_ref, ct_ref, w_ref, z_ref, big_a, big_b, raw_ref, core_ref, y_ref, dm_ref, st_ref, dcore_ref,
    dp_ref, mixed_ref, po_ref, ra_ref, rb_ref, ra2_ref, rb2_ref, own_out, wq_f, wq, wo_ref, sm_ref, gain_ref, conv_ref,
    sums_ref, got_sums, turned_sums, rz, ro, own_o, gz, gz2, go, go2, rx, gx, gx2, ia_ref, ib_ref, ia2_ref, ib2_ref,
    piece_z, piece_x, ow_z, ow_x, slab_ref, piece_o_ref, small_out, smalls_dp, sg, sg_all, small, hd_ref, gvec, cvec, dgain_ref, dskip_ref, dconv_ref, dhead_ref,
    state, halo, hid_v, cot_v, send, recv, own,
):
    place = Place()
    me = place.s
    wq_load = pltpu.make_async_copy(
        in_ref.at[pl.ds(pl.multiple_of(48 * place.x, 8), 48), :], wq_f, own.at[7]
    )
    wq_load.start()
    wq[:, WIDE - 128 :] = jnp.zeros((48, 128), bf16)
    small[...] = jnp.zeros_like(small)
    small[:5, :416] = conv_in[...].astype(bf16).astype(f32)
    small[5, :576] = gain_in[...].astype(bf16).astype(f32)
    hd_ref[...] = jnp.zeros_like(hd_ref)
    hd_ref[:3, :6] = head_in[...].astype(bf16).astype(f32)
    hd_ref[3:4, :] = widen(hd_ref[:, :128])[2:3]
    barrier = pltpu.get_barrier_semaphore()
    core_peer = place.core_peer()
    bigs = [place.big_peer(k) for k in range(1, 8)]
    x_peers = bigs[:3]
    group = [place.shard_peer(k) for k in range(1, 8)]
    everyone = bigs + [core_peer] + [place.other_core_of(k) for k in range(1, 8)]
    for peer in group + everyone:
        pl.semaphore_signal(barrier, inc=1, device_id=peer, device_id_type=MESH)
    pl.semaphore_wait(barrier, 22)

    def remote(src, dst, index, peer, other=None):
        return pltpu.make_async_remote_copy(
            src_ref=src,
            dst_ref=dst,
            send_sem=send.at[index],
            recv_sem=recv.at[index if other is None else other],
            device_id=peer,
            device_id_type=MESH,
        )

    quarter = pl.multiple_of(48 * place.x, 16)

    def weight_parts(them):
        at = pl.multiple_of(them * OWN, 128)
        rows = pl.ds(quarter, 48)
        return (
            (wq.at[:, pl.ds(at, OWN)], w_ref.at[me, rows, pl.ds(0, OWN)]),
            (wq.at[:, pl.ds(at + DI, OWN)], w_ref.at[me, rows, pl.ds(OWN, OWN)]),
            (wq.at[:, pl.ds(2 * DI, OWN)], w_ref.at[me, rows, pl.ds(2 * OWN, OWN)]),
        )

    locals_ = [
        pltpu.make_async_copy(hid, n_ref.at[me], own.at[1]),
        pltpu.make_async_copy(cot, ct_ref.at[me], own.at[2]),
        pltpu.make_async_copy(hid, hid_v, own.at[3]),
        pltpu.make_async_copy(cot, cot_v, own.at[14]),
    ]
    for copy in locals_:
        copy.start()
    mine = place.yl == place.c
    wo_parts = [
        pltpu.make_async_copy(
            out_w.at[pl.ds(32 * (p % 12), 32), pl.ds(768 * (p // 12), 768)],
            big_a.at[p // 8, p % 8],
            own.at[17 + p],
        )
        for p in range(24)
    ]
    for copy in wo_parts:
        copy.start()
    wq_load.wait()
    wq[:, :PROJ] = wq_f[...].astype(bf16)
    own_w = [
        pltpu.make_async_copy(src, dst, own.at[4 + i])
        for i, (src, dst) in enumerate(weight_parts(me))
    ]
    smalls = [remote(small, sm_ref.at[me], k, place.shard_peer(k)) for k in range(1, 8)]
    hids = Gather(place, remote, hid, n_ref, 8)
    cots = Gather(place, remote, cot, ct_ref, 20)
    weights = []
    for k in range(1, 8):
        weights.append(
            [
                remote(src, dst, 40 + 3 * k + i, place.shard_peer(k))
                for i, (src, dst) in enumerate(weight_parts(place.shard_of(k)))
            ]
        )

    def w_begin(some):
        @pl.when(mine)
        def _():
            for i in some:
                own_w[i].start()
            for parts in weights:
                for i in some:
                    parts[i].start()

    w_begin((1, 2))
    for copy in smalls:
        copy.start()
    hids.begin()
    w_begin((0,))

    def w_arrived(some):
        for k in range(1, 8):
            @pl.when(lax.rem(place.yl + k // 4, 2) == place.c)
            def _(k=k):
                for i in some:
                    weights[k - 1][i].wait_recv()

        @pl.when(mine)
        def _():
            for i in some:
                own_w[i].wait()

    w_up, w_down = place.big_peer(1), place.big_peer(3)

    class Quarters:
        def __init__(self, columns, base):
            def quarter(k, lo=0, n=4):
                rows = pl.ds(pl.multiple_of(48 * lax.rem(place.x + k, 4), 16), 48)
                return w_ref.at[pl.ds(4 * place.c + lo, n), rows, columns]

            def on(view, index, peer):
                return remote(view, view, base + index, peer)

            self.copies = [
                on(quarter(0), 0, w_up),
                on(quarter(0), 1, w_down),
                on(quarter(0), 2, core_peer),
                on(quarter(3, 0, 2), 3, w_up),
                on(quarter(3), 4, core_peer),
                on(quarter(1, 2, 2), 5, w_down),
                on(quarter(1), 6, core_peer),
                on(quarter(2, 0, 2), 7, core_peer),
                on(quarter(2, 2, 2), 8, core_peer),
            ]

        def begin(self):
            for copy in self.copies[:3]:
                copy.start()

        def after(self, arrived, *indices):
            self.copies[arrived].wait_recv()
            for index in indices:
                self.copies[index].start()

        def first(self):
            self.after(0, 3, 4)
            self.after(1, 5, 6)

        def second(self):
            self.after(3, 7)
            self.after(5, 8)

        def last(self):
            for index in (2, 4, 6, 7, 8):
                self.copies[index].wait_recv()

    w_scan = Quarters(pl.ds(OWN, 768), 32)
    w_gate = Quarters(pl.ds(0, OWN), 240)
    w_arrived((1, 2))
    w_scan.begin()
    locals_[0].wait()
    hids.first()
    w_scan.first()
    hids.second()
    w_arrived((0,))
    w_gate.begin()
    cots.begin()
    w_scan.second()

    sm_ref[me] = small[...]
    for copy in smalls:
        copy.wait_recv()
    gain_ref[...] = jnp.concatenate([sm_ref[p, 5:6, :576] for p in range(8)], axis=1)
    conv_ref[...] = jnp.concatenate([sm_ref[p, :, :416] for p in range(8)], axis=1)
    gg_at = pl.ds(pl.multiple_of(D + OWN * me, 128), OWN)
    cv_at = pl.ds(pl.multiple_of(OWN * me, 128), OWN)

    def conv_row(k):
        return jnp.concatenate([conv_ref[k : k + 1, cv_at], conv_ref[k : k + 1, DI:]], axis=1)

    hids.last()
    hids.sent()
    w_scan.last()

    for copy in wo_parts:
        copy.wait()
    for p in range(24):
        at = 768 * (p // 12)
        rows = slice(32 * (p % 12), 32 * (p % 12) + 32)
        wo_ref[rows, at : at + 768] = big_a[p // 8, p % 8].astype(bf16)
    state[...] = jnp.zeros_like(state)
    halo[...] = jnp.zeros_like(halo)
    skip = hd_ref[3:4, :]

    @pl.loop(0, LEN // TB)
    def _(i):
        two = pl.ds(2 * i, 2)

        @pl.when(i == 1)
        def _():
            w_gate.first()

        @pl.when(i == 2)
        def _():
            w_gate.second()

        @pl.when(i == 3)
        def _():
            cots.first()

        u = n_ref[two].reshape(TB, D).astype(f32)
        scale = lax.rsqrt(jnp.mean(u * u, axis=1, keepdims=True) + epsilon)
        normed = (u * scale * gain_ref[:, :D]).astype(bf16)
        n_ref[two] = normed.reshape(2, BLOCK, D)
        project = dot(normed, w_ref[:, :, OWN:].reshape(D, 768), 1, 0)
        xbc = project[:, :640]
        raw = pltpu.roll(project[:, 640:], 128 - 6 * me, 1)
        big_a[i, :, :, :640] = xbc.reshape(8, 32, 640)
        raw_ref[two] = raw.reshape(2, BLOCK, 128)
        extended = jnp.concatenate([halo[...], xbc], axis=0)
        halo[...] = xbc[TB - 8 :, :]
        conv = conv_row(KCONV)
        for k in range(KCONV):
            conv = conv + conv_row(k) * extended[5 + k : 5 + k + TB, :]
        big_b[i, :, :, :640] = conv.reshape(8, 32, 640)
        act = conv * jax.nn.sigmoid(conv)
        dt = softplus(raw + hd_ref[0:1, :128])
        log_decay = -jnp.exp(hd_ref[1:2, :128]) * dt
        for j in range(TB // BLOCK):
            at = slice(j * BLOCK, (j + 1) * BLOCK)
            before = state[...]
            st_ref[2 * i + j] = before
            core, after = forward_block(act[at], dt[at], log_decay[at], before)
            state[...] = after
            core_ref[2 * i + j] = core
            y_ref[i, 4 * j : 4 * j + 4] = (core + skip * act[at, :OWN]).reshape(4, 32, OWN)

    cots.second()
    w_gate.last()

    @pl.loop(0, LEN // TB)
    def _(i):
        normed = n_ref[pl.ds(2 * i, 2)].reshape(TB, D)
        z = dot(normed, w_ref[:, :, :OWN].reshape(D, OWN), 1, 0)
        z_ref[i] = z.reshape(8, 32, OWN)

    locals_[1].wait()
    cots.last()

    @pl.loop(0, LEN // TB)
    def _(i):
        two = pl.ds(2 * i, 2)
        dm = dot(ct_ref[two].reshape(TB, D), wo_ref[...], 1, 1)
        dm_ref[i] = dm.reshape(8, 32, OWN)
        z = two_blocks(z_ref, i, OWN)
        gated = two_blocks(y_ref, i, OWN) * (z * jax.nn.sigmoid(z))
        ones = jnp.ones((8, OWN), f32)
        first = ones_dot(ones, gated * gated, 1, 1)
        second = ones_dot(ones, gated * (gain_ref[:, gg_at] * dm), 1, 1)
        for j in range(2):
            sums_ref[pl.ds(2 * i + j, 1), :] = first[0:1, 128 * j : 128 * j + 128]
            sums_ref[pl.ds(2 * i + j + 8, 1), :] = second[0:1, 128 * j : 128 * j + 128]

    sums = [remote(sums_ref, got_sums.at[me], 64 + k, place.shard_peer(k)) for k in range(1, 8)]
    for copy in sums:
        copy.start()
    got_sums[me] = sums_ref[...]
    for copy in sums:
        copy.wait_recv()
    totals = got_sums[0]
    for j in range(1, 8):
        totals += got_sums[j]
    turned_sums[...] = jnp.concatenate([totals, jnp.zeros((112, 128), f32)], axis=0).T
    gain = gain_ref[:, gg_at]
    lane = lanes((BLOCK, 128))
    dgain_ref[...] = jnp.zeros_like(dgain_ref)
    dskip_ref[...] = jnp.zeros_like(dskip_ref)
    dconv_ref[...] = jnp.zeros_like(dconv_ref)
    dhead_ref[...] = jnp.zeros_like(dhead_ref)

    outs = Scatter(place, remote, po_ref, ra_ref, rb_ref, ra2_ref, rb2_ref, own_out, 72)

    @pl.loop(0, BLOCKS // 2)
    def _(i):
        pair = lax.rem(me // 2 + 1 + i, BLOCKS // 2)
        column = turned_sums[...]
        for j in range(2):
            b = 2 * pair + j
            first = jnp.sum(jnp.where(lane == b, column, 0.0), axis=1, keepdims=True)
            second = jnp.sum(jnp.where(lane == b + 8, column, 0.0), axis=1, keepdims=True)
            z, y, dm = block_of(z_ref, b, OWN), block_of(y_ref, b, OWN), block_of(dm_ref, b, OWN)
            sig_z = jax.nn.sigmoid(z)
            gate = z * sig_z
            scale = lax.rsqrt(first * (1.0 / DI) + epsilon)
            unit = y * gate * scale
            mixed_ref[b] = (unit * gain).astype(bf16)
            dgain_ref[0:1, :] += jnp.sum(dm * unit, axis=0, keepdims=True)
            dgated = scale * (gain * dm) - unit * (scale * scale * (second * (1.0 / DI)))
            dz = dgated * y * (sig_z * (1.0 + z * (1.0 - sig_z)))
            dp_ref[b, :, :OWN] = dz.astype(bf16)
            dcore_ref[b] = dgated * gate
        two = pl.ds(2 * pair, 2)
        part = dot(mixed_ref[two].reshape(TB, OWN), wo_ref[...], 1, 0)
        po_ref[two] = part.astype(bf16).reshape(2, BLOCK, D)
        outs.send(2 * pair)
        outs.send(2 * pair + 1)

    def weight_grad(q, columns):
        left = n_ref[:, :, pl.ds(pl.multiple_of(384 * q, 128), 384)].reshape(LEN, 384)
        return dot(left, dp_ref[:, :, columns].reshape(LEN, -1), 0, 0)

    def out_grad(h, q):
        at = pl.multiple_of(768 * h + 384 * q, 128)
        return dot(mixed_ref[...].reshape(LEN, OWN), ct_ref[:, :, pl.ds(at, 384)].reshape(LEN, 384), 0, 0)

    other = 1 - place.c
    zs = slice(0, OWN)
    late = slice(OWN, COLS)

    def rows24(ref):
        return ref.at[:, :, pl.ds(0, 24), :]

    @pl.loop(0, 2)
    def _(q):
        two = pl.ds(2 * q, 2)
        y_ref[two, :, :24, :] = weight_grad(2 * other + q, zs).reshape(2, 8, 24, OWN)
        z_ref[two, :, :24, :] = out_grad(other, q).reshape(2, 8, 24, OWN)

    swap_z = remote(rows24(y_ref), rz, 156, core_peer)
    swap_o = remote(rows24(z_ref), ro, 157, core_peer)
    swap_z.start()
    swap_o.start()

    @pl.loop(0, 2)
    def _(q):
        two = pl.ds(2 * q, 2)
        dm_ref[two, :, :24, :] = weight_grad(2 * place.c + q, zs).reshape(2, 8, 24, OWN)
        own_o[q] = out_grad(place.c, q).reshape(8, 2, 24, OWN)

    def rows_fns(ref, first, n):
        some = pl.ds(first, n)

        def view(big):
            return ref.at[some, big, pl.ds(0, 24), :]

        def read(big):
            return ref[some, big, :24, :]

        def write(big, total):
            ref[some, big, :24, :] = total

        return view, read, write

    def write_o(big, total):
        own_o[:, big] = total

    sum_z = Reduce(place, remote, *rows_fns(dm_ref, 0, 4), gz, gz2, 92)
    sum_x = Reduce(place, remote, *rows_fns(big_b, 0, 4), gx, gx2, 102)
    sum_o = Reduce(
        place, remote, lambda big: own_o.at[:, big], lambda big: own_o[:, big], write_o, go, go2, 112
    )

    state[...] = jnp.zeros_like(state)
    halo[...] = jnp.zeros_like(halo)

    @pl.loop(0, BLOCKS)
    def _(i):
        b = BLOCKS - 1 - i

        @pl.when(i == 1)
        def _():
            swap_z.wait_recv()
            swap_o.wait_recv()
            for r in range(4):
                dm_ref[r, :, :24, :] += rz[r]
            for q in range(2):
                own_o[q] += ro[2 * q : 2 * q + 2].reshape(8, 2, 24, OWN)
            sum_z.begin()
            sum_o.begin()

        pl.when(i == 7)(outs.middle)

        conv = block_of(big_b, b, 640)
        raw, core, dcore = raw_ref[b], core_ref[b], dcore_ref[b]
        sig = jax.nn.sigmoid(conv)
        act = conv * sig
        x, keys, query = act[:, :OWN], act[:, OWN : OWN + NS], act[:, OWN + NS :]
        shifted = raw + hd_ref[0:1, :128]
        dt = softplus(shifted)
        rate = jnp.exp(hd_ref[1:2, :128])
        log_decay = -rate * dt
        dskip_ref[0:1, :] += jnp.sum(dcore * x, axis=0, keepdims=True)
        cumulative, turned, wide = decay_parts(log_decay)
        contact = dot3(query, keys, 1, 1)
        dt_wide = widen(dt)
        scaled = x * dt_wide
        dcontact = jnp.zeros((BLOCK, BLOCK), f32)
        dscaled = []
        for p in range(3):
            at = slice(128 * p, 128 * p + 128)
            mixing = [head_mixing(cumulative, turned, 2 * p + q) for q in range(2)]
            both = jnp.concatenate([m * contact for m in mixing], axis=0)
            pair = split_pair(dcore[:, at])
            dscaled.append(dot3(both, pair, 0, 0))
            dmix = dot3(pair, scaled[:, at], 1, 1)
            dcontact += dmix[:BLOCK] * mixing[0] + dmix[BLOCK:] * mixing[1]
        last = wide[BLOCK - 1 : BLOCK, :]
        before = st_ref[b]
        after_adj = state[...]
        left = jnp.exp(last - wide)
        from_core = dcore * jnp.exp(wide)
        dquery = dot3(from_core, before, 1, 1) + dot3(dcontact, keys, 1, 0)
        carried = dot3(keys, after_adj, 1, 0) * left
        dscaled = jnp.concatenate(dscaled, axis=1) + carried
        dkeys = dot3(scaled * left, after_adj, 1, 1) + dot3(dcontact, query, 0, 0)
        end = jnp.exp(last)
        state[...] = end * after_adj + dot3(query, from_core, 0, 0)
        heads = head_ones()
        last_add = dot_exact(
            jnp.sum(carried * scaled, axis=0, keepdims=True)
            + end * jnp.sum(after_adj * before, axis=0, keepdims=True),
            heads, 1, 0,
        )
        dcum = dot_exact(dcore * core - dscaled * scaled, heads, 1, 0)
        dlog = ones_dot(lower_ones(), dcum, 0, 0) + last_add
        ddt = dot_exact(dscaled * x, heads, 1, 0) - rate * dlog
        draw = ddt * jax.nn.sigmoid(shifted)
        dhead_ref[0:1, :] += jnp.sum(draw, axis=0, keepdims=True)
        dhead_ref[1:2, :] += jnp.sum(dlog * log_decay, axis=0, keepdims=True)
        dx = dscaled * dt_wide + skip * dcore
        dact = jnp.concatenate([dx, dkeys, dquery], axis=1)
        dconv = dact * (sig * (1.0 + conv * (1.0 - sig)))
        extended = jnp.concatenate([dconv, halo[...]], axis=0)
        halo[...] = dconv[:8, :]
        xbc = block_of(big_a, b, 640)
        dxbc = jnp.zeros_like(xbc)
        for k in range(KCONV):
            moved = extended[3 - k : 3 - k + BLOCK, :]
            dxbc += conv_row(k) * moved
            dconv_ref[k : k + 1, :] += jnp.sum(xbc * moved, axis=0, keepdims=True)
        dconv_ref[KCONV : KCONV + 1, :] += jnp.sum(dconv, axis=0, keepdims=True)
        dp_ref[b, :, OWN : OWN + 640] = dxbc.astype(bf16)
        draw_own = jnp.where(lane < 6, draw, 0.0)
        dp_ref[b, :, 1024:] = pltpu.roll(draw_own, 6 * me, 1).astype(bf16)

    @pl.loop(0, 2)
    def _(q):
        two = pl.ds(2 * q, 2)
        big_a[two, :, :24, :] = weight_grad(2 * other + q, late).reshape(2, 8, 24, 768)

    swap_x = remote(rows24(big_a), rx, 158, core_peer)
    swap_x.start()

    @pl.loop(0, 2)
    def _(q):
        two = pl.ds(2 * q, 2)
        big_b[two, :, :24, :] = weight_grad(2 * place.c + q, late).reshape(2, 8, 24, 768)

    cots.sent()
    ins = Scatter(place, remote, ct_ref, ia_ref, ib_ref, ia2_ref, ib2_ref, own_out, 122)

    @pl.loop(0, BLOCKS // 2)
    def _(i):
        pair = lax.rem(me // 2 + 1 + i, BLOCKS // 2)
        two = pl.ds(2 * pair, 2)
        part = dot(dp_ref[two].reshape(TB, COLS), w_ref[...].reshape(D, COLS), 1, 1)
        ct_ref[two] = part.astype(bf16).reshape(2, BLOCK, D)
        ins.send(2 * pair)
        ins.send(2 * pair + 1)

        @pl.when(i == 1)
        def _():
            swap_x.wait_recv()
            for r in range(4):
                big_b[r, :, :24, :] += rx[r]
            sum_x.begin()

    sum_z.middle()
    sum_o.middle()

    at_o = pl.multiple_of(768 * place.c, 128)
    o_all = Spread(
        place, remote, piece_o_ref,
        lambda big, lo, hi: gos.at[big, :, pl.ds(pl.multiple_of(at_o + lo, 128), hi - lo)],
        (256, 384, 768), 160,
    )
    z_all = Spread(
        place, remote, slab_ref.at[:, pl.ds(0, DI)],
        lambda big, lo, hi: slabs.at[big, :, pl.ds(lo, hi - lo)], (768, 1536, DI), 180,
    )
    x_all = Direct(
        place, remote, slab_ref.at[:, pl.ds(DI, WIDE - DI)],
        lambda big: slabs.at[big, :, pl.ds(DI, WIDE - DI)], 200,
    )

    def to_owners(piece, ow, base):
        copies = []
        for k in range(1, 8):
            them = place.shard_of(k)
            copy = remote(piece.at[lax.rem(them, 4)], ow.at[me], base + k, place.shard_peer(k))
            goes = them // 4 == place.c
            pl.when(goes)(copy.start)
            copies.append((copy, goes))

        @pl.when(mine)
        def _():
            ow[me] = piece[place.z]

        return copies

    piece_z[...] = sum_z.last()
    owners_z = to_owners(piece_z, ow_z, 140)
    total_o = sum_o.last()
    for q in range(2):
        piece_o_ref[:, 384 * q : 384 * q + 384] = total_o[q].reshape(48, 384).astype(bf16)
    o_all.begin()
    own_go = pltpu.make_async_copy(
        piece_o_ref, gos.at[place.big, :, pl.ds(at_o, 768)], own.at[15]
    )
    own_go.start()

    outs.last()
    locals_[2].wait()
    out_ref[...] = (own_out[...] + hid_v[...].astype(f32)).astype(bf16)

    @pl.when(mine)
    def _():
        for copy, _ in owners_z:
            copy.wait_recv()
        for j in range(8):
            slab_ref[:, OWN * j : OWN * (j + 1)] = ow_z[j].astype(bf16)
        z_all.begin()

    ins.middle()
    for n in range(4):
        o_all.step(n)
        pl.when(mine)(functools.partial(z_all.step, n))
    sum_x.middle()
    for n in range(4, 8):
        o_all.step(n)
        pl.when(mine)(functools.partial(z_all.step, n))
    piece_x[...] = sum_x.last()
    owners_x = to_owners(piece_x, ow_x, 232)
    ins.last()
    locals_[3].wait()
    u = hid_v[...].astype(f32)
    scale = lax.rsqrt(jnp.mean(u * u, axis=1, keepdims=True) + epsilon)
    d_normed = own_out[...]
    gained = gain_ref[:, :D] * d_normed
    unit = u * scale
    grad = scale * gained - unit * (scale * scale * jnp.mean(u * gained, axis=1, keepdims=True))
    igrad_ref[...] = (cot_v[...].astype(f32) + grad).astype(bf16)

    sg[...] = jnp.zeros_like(sg)
    sg[0:1, :] = jnp.sum(d_normed * unit, axis=0, keepdims=True)
    sg[1:6, :640] = dconv_ref[0:5, :]
    sg[1:2, 640:1024] = dgain_ref[0:1, :]
    sgs = [remote(sg, sg_all.at[me], 148 + k, place.shard_peer(k)) for k in range(1, 8)]
    for copy in sgs:
        copy.start()
    sg_all[me] = sg[...]

    @pl.when(mine)
    def _():
        for copy, _ in owners_x:
            copy.wait_recv()
        common = ow_x[0, :, OWN:]
        for j in range(1, 8):
            common += ow_x[j, :, OWN:]
        for j in range(8):
            slab_ref[:, DI + OWN * j : DI + OWN * (j + 1)] = ow_x[j, :, :OWN].astype(bf16)
        slab_ref[:, 2 * DI :] = common.astype(bf16)
        x_all.begin()

    own_slab = pltpu.make_async_copy(slab_ref, slabs.at[place.big], own.at[16])
    pl.when(mine)(own_slab.start)
    for copy in sgs:
        copy.wait_recv()
    small_out[...] = jnp.zeros_like(small_out)
    gvec[:, :D] = sg_all[0, 0:1, :]
    cvec[...] = jnp.zeros_like(cvec)
    cvec[:5, DI:CONVC] = sg_all[0, 1:6, OWN:640]
    for j in range(1, 8):
        gvec[:, :D] += sg_all[j, 0:1, :]
        cvec[:5, DI:CONVC] += sg_all[j, 1:6, OWN:640]
    for j in range(8):
        gvec[:, D + OWN * j : D + OWN * (j + 1)] = sg_all[j, 1:2, 640:1024]
        cvec[:5, OWN * j : OWN * (j + 1)] = sg_all[j, 1:6, :OWN]
    near = gvec[:, pl.ds(pl.multiple_of(128 * (9 * me // 2), 128), 640)]
    small_out[5:6, :576] = jnp.where(lax.rem(me, 2) == 1, near[:, 64:640], near[:, :576])
    near = cvec[:, pl.ds(pl.multiple_of(128 * (13 * me // 4), 128), 640)]
    shift = lax.rem(13 * me, 4)
    taps = near[:, :416]
    for k in range(1, 4):
        taps = jnp.where(shift == k, near[:, 32 * k : 32 * k + 416], taps)
    small_out[:5, :416] = taps[:5]
    small_out[6:7, :128] = dhead_ref[0:1, :]
    small_out[6:7, 128:256] = dhead_ref[1:2, :]
    small_out[6:7, 256:384] = dot_exact(dskip_ref[0:1, :], head_ones(), 1, 0)
    dps = [remote(small_out, smalls_dp.at[place.d], 216 + n, peer) for n, peer in enumerate(everyone)]
    for copy in dps:
        copy.start()
    smalls_dp[place.d] = small_out[...]

    @pl.when(mine)
    def _():
        x_all.forward()
        own_slab.wait()

    @pl.when(jnp.logical_not(mine))
    def _():
        for copy in z_all.cores + x_all.cores:
            copy.wait_recv()

    for copy in o_all.cores:
        copy.wait_recv()
    own_go.wait()
    for copy in dps:
        copy.wait_recv()
    total = smalls_dp[0]
    for j in range(1, 16):
        total += smalls_dp[j]
    total_small[...] = total

    for copy in smalls + sums + w_scan.copies + w_gate.copies + sgs + dps + [swap_z, swap_o, swap_x]:
        copy.wait_send()
    for group_of in (outs, ins, sum_z, sum_o, sum_x, o_all):
        group_of.sent()
    for copy, goes in owners_z + owners_x:
        pl.when(goes)(copy.wait_send)

    @pl.when(mine)
    def _():
        z_all.sent()
        x_all.sent()
        for parts in weights:
            for copy in parts:
                copy.wait_send()


def sds(shape, dtype=f32):
    return jax.ShapeDtypeStruct(shape, dtype)


def run_whole(hid, cot, in_master, out_master, conv, gain, head):
    any_spec = pl.BlockSpec(memory_space=pl.ANY)
    vmem = pl.BlockSpec(memory_space=pltpu.VMEM)

    def v(*shape, dtype=f32):
        return pltpu.VMEM(shape, dtype)

    tokens = (8, BLOCK, D)
    part = (8, BLOCK, OWN)
    split = (4, 8, 32, OWN)
    landing = [
        v(4, 2, TOP, D, dtype=bf16), v(4, BLOCK - TOP, D, dtype=bf16), v(TOP, D, dtype=bf16),
        v(4, BLOCK - TOP, D, dtype=bf16),
    ]
    return pl.pallas_call(
        whole_kernel,
        in_specs=[any_spec] * 4 + [vmem] * 3,
        out_specs=(vmem, vmem, any_spec, any_spec, vmem),
        out_shape=(
            sds((BLOCK, D), bf16), sds((BLOCK, D), bf16), sds((8, 24, WIDE), bf16),
            sds((8, 48, D), bf16), sds((8, 640)),
        ),
        scratch_shapes=[
            v(*tokens, dtype=bf16), v(*tokens, dtype=bf16), v(8, 192, COLS, dtype=bf16), v(*split),
            v(4, 8, 32, 768), v(4, 8, 32, 768), v(8, BLOCK, 128), v(*part), v(*split), v(*split),
            v(8, NS, OWN), v(*part),
            v(8, BLOCK, COLS, dtype=bf16), v(*part, dtype=bf16), v(*tokens, dtype=bf16),
            *landing, v(BLOCK, D), v(48, PROJ),
            v(48, WIDE, dtype=bf16),
            v(OWN, D, dtype=bf16), v(8, 8, 640), v(1, 4608), v(8, CONVC),
            v(16, 128), v(8, 16, 128), v(BLOCK, 128), v(4, 8, 24, OWN), v(4, 8, 24, OWN),
            v(2, 8, 2, 24, OWN), v(3, 2, 4, 24, OWN), v(4, 24, OWN), v(3, 2, 2, 2, 24, OWN),
            v(2, 2, 24, OWN), v(4, 8, 24, 768), v(3, 2, 4, 24, 768), v(4, 24, 768), *landing,
            v(4, 24, OWN), v(4, 24, 768), v(8, 24, OWN), v(8, 24, 768),
            v(24, WIDE, dtype=bf16), v(48, 768, dtype=bf16), v(8, 640), v(16, 8, 640), v(8, D), v(8, 8, D), v(8, 640), v(8, OWN), v(1, 4736),
            v(8, 3456), v(8, OWN), v(8, OWN), v(8, 640), v(8, 128), v(NS, OWN), v(8, 640), v(BLOCK, D, dtype=bf16), v(BLOCK, D, dtype=bf16),
            pltpu.SemaphoreType.DMA((250,)), pltpu.SemaphoreType.DMA((250,)),
            pltpu.SemaphoreType.DMA((41,)),
        ],
        compiler_params=pltpu.CompilerParams(
            collective_id=1, has_side_effects=True, vmem_limit_bytes=62 * 2**20
        ),
    )(hid, cot, in_master, out_master, conv, gain, head)


class Spread:
    def __init__(self, place, remote, src, view, cuts, base):
        one, two, end = cuts

        def at(dy, dx, lo, hi):
            return view(lax.rem(place.yh + dy, 2) * 4 + lax.rem(place.x + dx, 4), lo, hi)

        def onward(part, index, peer):
            return remote(part, part, base + index, peer)

        up, down, over = place.big_peer(1), place.big_peer(3), place.big_peer(4)
        own = view(place.big, 0, end)
        self.copies = [
            remote(src, own, base, up),
            remote(src, own, base + 1, down),
            remote(src, own, base + 2, over),
            onward(at(0, 3, 0, two), 3, up),
            onward(at(0, 1, two, end), 4, down),
            onward(at(0, 3, two, end), 5, over),
            onward(at(0, 1, two, end), 6, over),
            onward(at(0, 2, two, end), 7, over),
            onward(at(1, 0, 0, two), 8, up),
            onward(at(1, 0, 0, two), 9, down),
            onward(at(1, 3, 0, one), 10, up),
            onward(at(1, 1, one, two), 11, down),
        ]
        core = place.core_peer()
        self.cores = [remote(src, own, base + 12, core)]
        for n, (dy, dx, _, _) in enumerate(ARRIVALS[1:]):
            block = at(dy, dx, 0, end)
            self.cores.append(remote(block, block, base + 13 + n, core))

    def begin(self):
        for index in (2, 0, 1):
            self.copies[index].start()
        self.cores[0].start()

    def step(self, n):
        _, _, needs, sends = ARRIVALS[n]
        for index in needs:
            self.copies[index].wait_recv()
        for index in sends:
            self.copies[index].start()
        if n:
            self.cores[n].start()

    def sent(self):
        for copy in self.copies + self.cores:
            copy.wait_send()


ARRIVALS = (
    (0, 0, (), ()),
    (1, 0, (2,), (8, 9)),
    (0, 3, (0,), (3, 5)),
    (0, 1, (1,), (4, 6)),
    (0, 2, (3, 4), (7,)),
    (1, 3, (8, 5), (10,)),
    (1, 1, (9, 6), (11,)),
    (1, 2, (10, 11, 7), ()),
)


def adam_update(master, first, second, gradient, rate, decay):
    first_new = beta_one * first + (1.0 - beta_one) * gradient
    second_new = beta_two * second + (1.0 - beta_two) * gradient * gradient
    scaled = (
        first_new
        / (1.0 - beta_one**STEP)
        / (jnp.sqrt(second_new / (1.0 - beta_two**STEP)) + adam_epsilon)
    )
    return (first_new, second_new, master - rate * (scaled + decay * master))


def on_device(
    hidden, cotangent, in_master, in_first, in_second, out_master, out_first, out_second,
    gain_master, gain_first, gain_second, conv_master, conv_first, conv_second,
    head_master, head_first, head_second,
):
    layer_out, input_grad, total_w, total_o, total = run_whole(
        hidden[0], cotangent[0], in_master, out_master, conv_master, gain_master, head_master
    )
    gradients = (
        total_w.reshape(192, WIDE)[:, :PROJ].astype(f32), total_o.reshape(OWN, D).astype(f32),
        total[5, :576], total[:5, :416],
        jnp.stack([total[6, :6], total[6, 128:134], total[6, 256:262]]),
    )
    masters = (in_master, out_master, gain_master, conv_master, head_master)
    firsts = (in_first, out_first, gain_first, conv_first, head_first)
    seconds = (in_second, out_second, gain_second, conv_second, head_second)
    updated = [
        adam_update(masters[g], firsts[g], seconds[g], gradients[g], rates[g], decays[g])
        for g in range(5)
    ]
    return (layer_out[None], input_grad[None]) + tuple(v for group in updated for v in group)


def solution(mesh):
    rows, columns = P("shard", None), P(None, "shard")
    tokens = P("dp", "shard", None)
    state = (rows,) * 6 + (P("shard"),) * 3 + (columns,) * 6
    return jax.shard_map(
        on_device,
        mesh=mesh,
        in_specs=(tokens, tokens) + state,
        out_specs=(tokens, tokens) + state,
        check_vma=False,
    )
```

```python
import functools

import jax
import jax.numpy as jnp
from jax import lax
from jax.experimental import pallas as pl
from jax.experimental.pallas import tpu as pltpu
from jax.sharding import PartitionSpec as P

D = 1536
DI = 3072
H = 48
HD = 64
NS = 128
KCONV = 4
STEP = 5
BLOCK = 128
CONVC = 3328
PROJ = 6448
LEN = 1024
OWN = 384
COLS = 1152
WIDE = 6528
BLOCKS = LEN // BLOCK

f32 = jnp.float32
bf16 = jnp.bfloat16
highest = lax.Precision.HIGHEST
MESH = pl.DeviceIdType.MESH
epsilon = 1e-05
beta_one = 0.9
beta_two = 0.95
adam_epsilon = 1e-08
rates = (0.05, 0.04, 0.25, 0.5, 0.5)
decays = (0.1, 0.1, 0.0, 0.0, 0.0)
TOP = 80


class Place:
    def __init__(self):
        self.d = lax.axis_index("dp")
        self.s = lax.axis_index("shard")
        self.c = lax.rem(self.d, 2)
        self.x = lax.rem(self.d // 2, 4)
        self.yh = self.d // 8
        self.big = self.d // 2
        self.z = lax.rem(self.s, 4)
        self.yl = self.s // 4

    def shard_of(self, k):
        return lax.rem(self.yl + k // 4, 2) * 4 + lax.rem(self.z + k % 4, 4)

    def shard_peer(self, k):
        return (self.d, self.shard_of(k))

    def big_of(self, k):
        return lax.rem(self.yh + k // 4, 2) * 4 + lax.rem(self.x + k % 4, 4)

    def big_peer(self, k):
        return (self.big_of(k) * 2 + self.c, self.s)

    def z_peer(self, k):
        return (self.d, self.yl * 4 + lax.rem(self.z + k, 4))

    def y_partner(self):
        return (self.d, (1 - self.yl) * 4 + self.z)

    def core_peer(self):
        return (self.big * 2 + 1 - self.c, self.s)

    def other_core_of(self, k):
        return (self.big_of(k) * 2 + 1 - self.c, self.s)


class Gather:
    def __init__(self, place, remote, src, buf, base):
        def at(dy, dz, lo, hi):
            index = lax.rem(place.yl + dy, 2) * 4 + lax.rem(place.z + dz, 4)
            return buf.at[index, pl.ds(lo, hi - lo)]

        def onward(view, index, peer):
            return remote(view, view, base + index, peer)

        up, down, over = place.z_peer(1), place.z_peer(3), place.y_partner()
        self.copies = [
            remote(src, buf.at[place.s], base, up),
            remote(src, buf.at[place.s], base + 1, down),
            remote(src, buf.at[place.s], base + 2, over),
            onward(at(0, 3, 0, 64), 3, up),
            onward(at(0, 1, 64, 128), 4, down),
            onward(at(0, 3, 64, 128), 5, over),
            onward(at(0, 1, 64, 128), 6, over),
            onward(at(0, 2, 64, 128), 7, over),
            onward(at(1, 0, 0, 64), 8, up),
            onward(at(1, 0, 0, 64), 9, down),
            onward(at(1, 3, 0, 32), 10, up),
            onward(at(1, 1, 32, 64), 11, down),
        ]

    def after(self, arrived, *indices):
        self.copies[arrived].wait_recv()
        for index in indices:
            self.copies[index].start()

    def begin(self):
        for copy in (self.copies[2], self.copies[0], self.copies[1]):
            copy.start()

    def first(self):
        self.after(2, 8, 9)
        self.after(0, 3, 5)
        self.after(1, 4, 6)

    def second(self):
        self.after(8, 10)
        self.after(9, 11)
        self.after(4, 7)

    def last(self):
        for index in (3, 5, 6, 7, 10, 11):
            self.copies[index].wait_recv()

    def sent(self):
        for copy in self.copies:
            copy.wait_send()


class Scatter:
    def __init__(self, place, remote, part, ra, rb, ra2, rb2, total, base):
        self.place, self.remote, self.base = place, remote, base
        self.part, self.ra, self.rb, self.ra2, self.rb2, self.total = part, ra, rb, ra2, rb2, total
        self.top, self.low = pl.ds(0, TOP), pl.ds(TOP, BLOCK - TOP)

    def along_z(self, b, source):
        place = self.place
        return self.remote(
            self.part.at[b, self.top],
            self.ra.at[place.z, b // 4],
            self.base + b,
            (place.d, place.yl * 4 + lax.rem(b, 4)),
            self.base + source * 2 + b // 4,
        )

    def along_y(self, b):
        z = lax.rem(b, 4)
        return self.remote(
            self.part.at[b, self.low], self.rb.at[z], self.base + 8 + z, self.place.y_partner()
        )

    def send(self, b):
        pl.when(lax.rem(b, 4) != self.place.z)(self.along_z(b, self.place.z).start)
        pl.when(b // 4 != self.place.yl)(self.along_y(b).start)

    def other(self):
        return (1 - self.place.yl) * 4 + self.place.z

    def over(self):
        return self.remote(
            self.part.at[self.other(), self.top], self.ra2, self.base + 12, self.place.y_partner()
        )

    def back(self, z):
        place = self.place
        return self.remote(
            self.part.at[place.yl * 4 + z, self.low],
            self.rb2.at[place.z],
            self.base + 13 + z,
            (place.d, place.yl * 4 + z),
            self.base + 13 + place.z,
        )

    def others(self):
        return [lax.rem(self.place.z + k, 4) for k in (1, 2, 3)]

    def middle(self):
        place, part = self.place, self.part
        for z in self.others():
            for y in range(2):
                self.along_z(y * 4 + z, z).wait_recv()

        def sum_z(block, y):
            total = part[block, :TOP].astype(f32)
            for z in self.others():
                total += self.ra[z, y].astype(f32)
            return total

        part[self.other(), :TOP] = sum_z(self.other(), 1 - place.yl).astype(bf16)
        self.over().start()
        self.total[:TOP] = sum_z(place.s, place.yl)
        for z in range(4):
            self.along_y((1 - place.yl) * 4 + z).wait_recv()
        for z in self.others():
            block = place.yl * 4 + z
            part[block, TOP:] = (part[block, TOP:].astype(f32) + self.rb[z].astype(f32)).astype(bf16)
            self.back(z).start()
        self.total[TOP:] = part[place.s, TOP:].astype(f32) + self.rb[place.z].astype(f32)

    def last(self):
        self.over().wait_recv()
        self.total[:TOP] += self.ra2[...].astype(f32)
        for z in self.others():
            self.remote(
                self.part.at[self.place.yl * 4 + z, self.low], self.rb2.at[z],
                self.base + 13 + z, (self.place.d, self.place.yl * 4 + z),
            ).wait_recv()
            self.total[TOP:] += self.rb2[z].astype(f32)

    def sent(self):
        place = self.place
        for z in self.others():
            for y in range(2):
                self.along_z(y * 4 + z, place.z).wait_send()
            self.back(z).wait_send()
        for z in range(4):
            self.along_y((1 - place.yl) * 4 + z).wait_send()
        self.over().wait_send()


class Reduce:
    def __init__(self, place, remote, view, read, write, gx, gy, base):
        self.place, self.view, self.read, self.write, self.gx, self.gy = place, view, read, write, gx, gy
        self.along = [
            remote(
                view(y * 4 + lax.rem(place.x + k, 4)), gx.at[k - 1, y], base + 2 * k + y,
                place.big_peer(k),
            )
            for k in (1, 2, 3)
            for y in range(2)
        ]
        self.other = (1 - place.yh) * 4 + place.x
        self.over = remote(view(self.other), gy, base + 8, place.big_peer(4))

    def begin(self):
        for copy in self.along:
            copy.start()

    def total(self, big, y):
        total = self.read(big)
        for k in range(3):
            total += self.gx[k, y]
        return total

    def middle(self):
        for copy in self.along:
            copy.wait_recv()
        self.write(self.other, self.total(self.other, 1 - self.place.yh))
        self.over.start()

    def last(self):
        total = self.total(self.place.big, self.place.yh)
        self.over.wait_recv()
        return total + self.gy[...]

    def sent(self):
        for copy in self.along + [self.over]:
            copy.wait_send()


class Direct:
    def __init__(self, place, remote, src, view, base):
        own, core = view(place.big), place.core_peer()
        self.copies = [remote(src, own, base + k, place.big_peer(k)) for k in range(1, 8)]
        self.cores = [remote(src, own, base + 8, core)]
        for k in range(1, 8):
            block = view(lax.rem(place.yh + k // 4, 2) * 4 + lax.rem(place.x + 4 - k % 4, 4))
            self.cores.append(remote(block, block, base + 8 + k, core))

    def begin(self):
        for copy in self.copies + self.cores[:1]:
            copy.start()

    def forward(self):
        for k in range(1, 8):
            self.copies[k - 1].wait_recv()
            self.cores[k].start()

    def sent(self):
        for copy in self.copies + self.cores:
            copy.wait_send()


def dot(a, b, ca, cb, precision=None):
    return lax.dot_general(
        a, b, (((ca,), (cb,)), ((), ())), precision=precision, preferred_element_type=f32
    )


def mm(a, b, ca=1, cb=0):
    return dot(a.astype(f32), b.astype(f32), ca, cb, highest)


def lanes(shape):
    return lax.broadcasted_iota(jnp.int32, shape, 1)


def rows_of(shape):
    return lax.broadcasted_iota(jnp.int32, shape, 0)


def widen(m):
    low = lanes((m.shape[0], 128)) < HD
    return jnp.concatenate(
        [jnp.where(low, m[:, 2 * i : 2 * i + 1], m[:, 2 * i + 1 : 2 * i + 2]) for i in range(3)],
        axis=1,
    )


def lower_ones():
    return (rows_of((BLOCK, BLOCK)) >= lanes((BLOCK, BLOCK))).astype(f32)


def head_ones():
    return (rows_of((OWN, BLOCK)) // HD == lanes((OWN, BLOCK))).astype(f32)


def split_pair(pair):
    low = lanes(pair.shape) < HD
    zero = jnp.zeros_like(pair)
    return jnp.concatenate([jnp.where(low, pair, zero), jnp.where(low, zero, pair)], axis=0)


def head_mixing(cumulative, turned, h):
    causal = rows_of((BLOCK, BLOCK)) >= lanes((BLOCK, BLOCK))
    differ = cumulative[:, h : h + 1] - turned[h : h + 1, :]
    return jnp.exp(jnp.where(causal, differ, -jnp.inf))


def softplus(v):
    return jnp.maximum(v, 0.0) + jnp.log1p(jnp.exp(-jnp.abs(v)))


TB = 256
HALF = DI // 8


def dot3(a, b, ca, cb):
    a_hi, b_hi = a.astype(bf16), b.astype(bf16)
    a_lo, b_lo = (a - a_hi.astype(f32)).astype(bf16), (b - b_hi.astype(f32)).astype(bf16)
    left = jnp.concatenate([a_hi, a_hi, a_lo], axis=ca)
    right = jnp.concatenate([b_hi, b_lo, b_hi], axis=cb)
    return dot(left, right, ca, cb)


def dot_exact(a, ones, ca, cb):
    a_hi = a.astype(bf16)
    a_lo = (a - a_hi.astype(f32)).astype(bf16)
    low = ones.astype(bf16)
    return dot(
        jnp.concatenate([a_hi, a_lo], axis=ca), jnp.concatenate([low, low], axis=cb), ca, cb
    )


def ones_dot(ones, a, ca, cb):
    a_hi = a.astype(bf16)
    a_lo = (a - a_hi.astype(f32)).astype(bf16)
    low = ones.astype(bf16)
    return dot(
        jnp.concatenate([low, low], axis=ca), jnp.concatenate([a_hi, a_lo], axis=cb), ca, cb
    )


def decay_parts(log_decay):
    cumulative = ones_dot(lower_ones(), log_decay, 1, 0)
    return cumulative, cumulative.T, widen(cumulative)


def two_blocks(ref, i, columns):
    return ref[i, :, :, :columns].reshape(TB, columns)


def block_of(ref, b, columns):
    four = pl.ds(4 * lax.rem(b, 2), 4)
    return ref[b // 2, four, :, :columns].reshape(BLOCK, columns)


def forward_block(act, dt, log_decay, before):
    x, keys, query = act[:, :OWN], act[:, OWN : OWN + NS], act[:, OWN + NS :]
    cumulative, turned, wide = decay_parts(log_decay)
    contact = dot3(query, keys, 1, 1)
    scaled = x * widen(dt)
    within = []
    for p in range(3):
        pair = split_pair(scaled[:, 128 * p : 128 * p + 128])
        both = jnp.concatenate(
            [head_mixing(cumulative, turned, 2 * p + q) * contact for q in range(2)], axis=1
        )
        within.append(dot3(both, pair, 1, 0))
    last = wide[BLOCK - 1 : BLOCK, :]
    core = jnp.concatenate(within, axis=1) + dot3(query, before, 1, 0) * jnp.exp(wide)
    after = jnp.exp(last) * before + dot3(keys, scaled * jnp.exp(last - wide), 0, 0)
    return core, after


def whole_kernel(
    hid, cot, in_ref, out_w, conv_in, gain_in, head_in,
    out_ref, igrad_ref, slabs, gos, total_small,
    n_ref, ct_ref, w_ref, z_ref, big_a, big_b, raw_ref, core_ref, y_ref, dm_ref, st_ref, dcore_ref,
    dp_ref, mixed_ref, po_ref, ra_ref, rb_ref, ra2_ref, rb2_ref, own_out, wq_f, wq, wo_ref, sm_ref, gain_ref, conv_ref,
    sums_ref, got_sums, turned_sums, rz, ro, own_o, gz, gz2, go, go2, rx, gx, gx2, ia_ref, ib_ref, ia2_ref, ib2_ref,
    piece_z, piece_x, ow_z, ow_x, slab_ref, piece_o_ref, small_out, smalls_dp, sg, sg_all, small, hd_ref, gvec, cvec, dgain_ref, dskip_ref, dconv_ref, dhead_ref,
    state, halo, hid_v, cot_v, send, recv, own,
):
    place = Place()
    me = place.s
    wq_load = pltpu.make_async_copy(
        in_ref.at[pl.ds(pl.multiple_of(48 * place.x, 8), 48), :], wq_f, own.at[7]
    )
    wq_load.start()
    wq[:, WIDE - 128 :] = jnp.zeros((48, 128), bf16)
    small[...] = jnp.zeros_like(small)
    small[:5, :416] = conv_in[...].astype(bf16).astype(f32)
    small[5, :576] = gain_in[...].astype(bf16).astype(f32)
    hd_ref[...] = jnp.zeros_like(hd_ref)
    hd_ref[:3, :6] = head_in[...].astype(bf16).astype(f32)
    hd_ref[3:4, :] = widen(hd_ref[:, :128])[2:3]
    barrier = pltpu.get_barrier_semaphore()
    core_peer = place.core_peer()
    bigs = [place.big_peer(k) for k in range(1, 8)]
    x_peers = bigs[:3]
    group = [place.shard_peer(k) for k in range(1, 8)]
    everyone = bigs + [core_peer] + [place.other_core_of(k) for k in range(1, 8)]
    for peer in group + everyone:
        pl.semaphore_signal(barrier, inc=1, device_id=peer, device_id_type=MESH)
    pl.semaphore_wait(barrier, 22)

    def remote(src, dst, index, peer, other=None):
        return pltpu.make_async_remote_copy(
            src_ref=src,
            dst_ref=dst,
            send_sem=send.at[index],
            recv_sem=recv.at[index if other is None else other],
            device_id=peer,
            device_id_type=MESH,
        )

    quarter = pl.multiple_of(48 * place.x, 16)

    def weight_parts(them):
        at = pl.multiple_of(them * OWN, 128)
        rows = pl.ds(quarter, 48)
        return (
            (wq.at[:, pl.ds(at, OWN)], w_ref.at[me, rows, pl.ds(0, OWN)]),
            (wq.at[:, pl.ds(at + DI, OWN)], w_ref.at[me, rows, pl.ds(OWN, OWN)]),
            (wq.at[:, pl.ds(2 * DI, OWN)], w_ref.at[me, rows, pl.ds(2 * OWN, OWN)]),
        )

    locals_ = [
        pltpu.make_async_copy(hid, n_ref.at[me], own.at[1]),
        pltpu.make_async_copy(cot, ct_ref.at[me], own.at[2]),
        pltpu.make_async_copy(hid, hid_v, own.at[3]),
        pltpu.make_async_copy(cot, cot_v, own.at[14]),
    ]
    for copy in locals_:
        copy.start()
    mine = place.yl == place.c
    wo_parts = [
        pltpu.make_async_copy(
            out_w.at[pl.ds(32 * (p % 12), 32), pl.ds(768 * (p // 12), 768)],
            big_a.at[p // 8, p % 8],
            own.at[17 + p],
        )
        for p in range(24)
    ]
    for copy in wo_parts:
        copy.start()
    wq_load.wait()
    wq[:, :PROJ] = wq_f[...].astype(bf16)
    own_w = [
        pltpu.make_async_copy(src, dst, own.at[4 + i])
        for i, (src, dst) in enumerate(weight_parts(me))
    ]
    smalls = [remote(small, sm_ref.at[me], k, place.shard_peer(k)) for k in range(1, 8)]
    hids = Gather(place, remote, hid, n_ref, 8)
    cots = Gather(place, remote, cot, ct_ref, 20)
    weights = []
    for k in range(1, 8):
        weights.append(
            [
                remote(src, dst, 40 + 3 * k + i, place.shard_peer(k))
                for i, (src, dst) in enumerate(weight_parts(place.shard_of(k)))
            ]
        )

    def w_begin(some):
        @pl.when(mine)
        def _():
            for i in some:
                own_w[i].start()
            for parts in weights:
                for i in some:
                    parts[i].start()

    w_begin((1, 2))
    for copy in smalls:
        copy.start()
    hids.begin()
    w_begin((0,))

    def w_arrived(some):
        for k in range(1, 8):
            @pl.when(lax.rem(place.yl + k // 4, 2) == place.c)
            def _(k=k):
                for i in some:
                    weights[k - 1][i].wait_recv()

        @pl.when(mine)
        def _():
            for i in some:
                own_w[i].wait()

    w_up, w_down = place.big_peer(1), place.big_peer(3)

    class Quarters:
        def __init__(self, columns, base):
            def quarter(k, lo=0, n=4):
                rows = pl.ds(pl.multiple_of(48 * lax.rem(place.x + k, 4), 16), 48)
                return w_ref.at[pl.ds(4 * place.c + lo, n), rows, columns]

            def on(view, index, peer):
                return remote(view, view, base + index, peer)

            self.copies = [
                on(quarter(0), 0, w_up),
                on(quarter(0), 1, w_down),
                on(quarter(0), 2, core_peer),
                on(quarter(3, 0, 2), 3, w_up),
                on(quarter(3), 4, core_peer),
                on(quarter(1, 2, 2), 5, w_down),
                on(quarter(1), 6, core_peer),
                on(quarter(2, 0, 2), 7, core_peer),
                on(quarter(2, 2, 2), 8, core_peer),
            ]

        def begin(self):
            for copy in self.copies[:3]:
                copy.start()

        def after(self, arrived, *indices):
            self.copies[arrived].wait_recv()
            for index in indices:
                self.copies[index].start()

        def first(self):
            self.after(0, 3, 4)
            self.after(1, 5, 6)

        def second(self):
            self.after(3, 7)
            self.after(5, 8)

        def last(self):
            for index in (2, 4, 6, 7, 8):
                self.copies[index].wait_recv()

    w_scan = Quarters(pl.ds(OWN, 768), 32)
    w_gate = Quarters(pl.ds(0, OWN), 240)
    w_arrived((1, 2))
    w_scan.begin()
    locals_[0].wait()
    hids.first()
    w_scan.first()
    hids.second()
    w_arrived((0,))
    w_gate.begin()
    cots.begin()
    w_scan.second()

    sm_ref[me] = small[...]
    for copy in smalls:
        copy.wait_recv()
    gain_ref[...] = jnp.concatenate([sm_ref[p, 5:6, :576] for p in range(8)], axis=1)
    conv_ref[...] = jnp.concatenate([sm_ref[p, :, :416] for p in range(8)], axis=1)
    gg_at = pl.ds(pl.multiple_of(D + OWN * me, 128), OWN)
    cv_at = pl.ds(pl.multiple_of(OWN * me, 128), OWN)

    def conv_row(k):
        return jnp.concatenate([conv_ref[k : k + 1, cv_at], conv_ref[k : k + 1, DI:]], axis=1)

    hids.last()
    hids.sent()
    w_scan.last()

    for copy in wo_parts:
        copy.wait()
    for p in range(24):
        at = 768 * (p // 12)
        rows = slice(32 * (p % 12), 32 * (p % 12) + 32)
        wo_ref[rows, at : at + 768] = big_a[p // 8, p % 8].astype(bf16)
    state[...] = jnp.zeros_like(state)
    halo[...] = jnp.zeros_like(halo)
    skip = hd_ref[3:4, :]

    @pl.loop(0, LEN // TB)
    def _(i):
        two = pl.ds(2 * i, 2)

        @pl.when(i == 1)
        def _():
            w_gate.first()

        @pl.when(i == 2)
        def _():
            w_gate.second()

        @pl.when(i == 3)
        def _():
            cots.first()

        u = n_ref[two].reshape(TB, D).astype(f32)
        scale = lax.rsqrt(jnp.mean(u * u, axis=1, keepdims=True) + epsilon)
        normed = (u * scale * gain_ref[:, :D]).astype(bf16)
        n_ref[two] = normed.reshape(2, BLOCK, D)
        project = dot(normed, w_ref[:, :, OWN:].reshape(D, 768), 1, 0)
        xbc = project[:, :640]
        raw = pltpu.roll(project[:, 640:], 128 - 6 * me, 1)
        big_a[i, :, :, :640] = xbc.reshape(8, 32, 640)
        raw_ref[two] = raw.reshape(2, BLOCK, 128)
        extended = jnp.concatenate([halo[...], xbc], axis=0)
        halo[...] = xbc[TB - 8 :, :]
        conv = conv_row(KCONV)
        for k in range(KCONV):
            conv = conv + conv_row(k) * extended[5 + k : 5 + k + TB, :]
        big_b[i, :, :, :640] = conv.reshape(8, 32, 640)
        act = conv * jax.nn.sigmoid(conv)
        dt = softplus(raw + hd_ref[0:1, :128])
        log_decay = -jnp.exp(hd_ref[1:2, :128]) * dt
        for j in range(TB // BLOCK):
            at = slice(j * BLOCK, (j + 1) * BLOCK)
            before = state[...]
            st_ref[2 * i + j] = before
            core, after = forward_block(act[at], dt[at], log_decay[at], before)
            state[...] = after
            core_ref[2 * i + j] = core
            y_ref[i, 4 * j : 4 * j + 4] = (core + skip * act[at, :OWN]).reshape(4, 32, OWN)

    cots.second()
    w_gate.last()

    @pl.loop(0, LEN // TB)
    def _(i):
        normed = n_ref[pl.ds(2 * i, 2)].reshape(TB, D)
        z = dot(normed, w_ref[:, :, :OWN].reshape(D, OWN), 1, 0)
        z_ref[i] = z.reshape(8, 32, OWN)

    locals_[1].wait()
    cots.last()

    @pl.loop(0, LEN // TB)
    def _(i):
        two = pl.ds(2 * i, 2)
        dm = dot(ct_ref[two].reshape(TB, D), wo_ref[...], 1, 1)
        dm_ref[i] = dm.reshape(8, 32, OWN)
        z = two_blocks(z_ref, i, OWN)
        gated = two_blocks(y_ref, i, OWN) * (z * jax.nn.sigmoid(z))
        ones = jnp.ones((8, OWN), f32)
        first = ones_dot(ones, gated * gated, 1, 1)
        second = ones_dot(ones, gated * (gain_ref[:, gg_at] * dm), 1, 1)
        for j in range(2):
            sums_ref[pl.ds(2 * i + j, 1), :] = first[0:1, 128 * j : 128 * j + 128]
            sums_ref[pl.ds(2 * i + j + 8, 1), :] = second[0:1, 128 * j : 128 * j + 128]

    sums = [remote(sums_ref, got_sums.at[me], 64 + k, place.shard_peer(k)) for k in range(1, 8)]
    for copy in sums:
        copy.start()
    got_sums[me] = sums_ref[...]
    for copy in sums:
        copy.wait_recv()
    totals = got_sums[0]
    for j in range(1, 8):
        totals += got_sums[j]
    turned_sums[...] = jnp.concatenate([totals, jnp.zeros((112, 128), f32)], axis=0).T
    gain = gain_ref[:, gg_at]
    lane = lanes((BLOCK, 128))
    dgain_ref[...] = jnp.zeros_like(dgain_ref)
    dskip_ref[...] = jnp.zeros_like(dskip_ref)
    dconv_ref[...] = jnp.zeros_like(dconv_ref)
    dhead_ref[...] = jnp.zeros_like(dhead_ref)

    outs = Scatter(place, remote, po_ref, ra_ref, rb_ref, ra2_ref, rb2_ref, own_out, 72)

    @pl.loop(0, BLOCKS // 2)
    def _(i):
        pair = lax.rem(me // 2 + 1 + i, BLOCKS // 2)
        column = turned_sums[...]
        for j in range(2):
            b = 2 * pair + j
            first = jnp.sum(jnp.where(lane == b, column, 0.0), axis=1, keepdims=True)
            second = jnp.sum(jnp.where(lane == b + 8, column, 0.0), axis=1, keepdims=True)
            z, y, dm = block_of(z_ref, b, OWN), block_of(y_ref, b, OWN), block_of(dm_ref, b, OWN)
            sig_z = jax.nn.sigmoid(z)
            gate = z * sig_z
            scale = lax.rsqrt(first * (1.0 / DI) + epsilon)
            unit = y * gate * scale
            mixed_ref[b] = (unit * gain).astype(bf16)
            dgain_ref[0:1, :] += jnp.sum(dm * unit, axis=0, keepdims=True)
            dgated = scale * (gain * dm) - unit * (scale * scale * (second * (1.0 / DI)))
            dz = dgated * y * (sig_z * (1.0 + z * (1.0 - sig_z)))
            dp_ref[b, :, :OWN] = dz.astype(bf16)
            dcore_ref[b] = dgated * gate
        two = pl.ds(2 * pair, 2)
        part = dot(mixed_ref[two].reshape(TB, OWN), wo_ref[...], 1, 0)
        po_ref[two] = part.astype(bf16).reshape(2, BLOCK, D)
        outs.send(2 * pair)
        outs.send(2 * pair + 1)

    def weight_grad(q, columns):
        left = n_ref[:, :, pl.ds(pl.multiple_of(384 * q, 128), 384)].reshape(LEN, 384)
        return dot(left, dp_ref[:, :, columns].reshape(LEN, -1), 0, 0)

    def out_grad(h, q):
        at = pl.multiple_of(768 * h + 384 * q, 128)
        return dot(mixed_ref[...].reshape(LEN, OWN), ct_ref[:, :, pl.ds(at, 384)].reshape(LEN, 384), 0, 0)

    other = 1 - place.c
    zs = slice(0, OWN)
    late = slice(OWN, COLS)

    def rows24(ref):
        return ref.at[:, :, pl.ds(0, 24), :]

    @pl.loop(0, 2)
    def _(q):
        two = pl.ds(2 * q, 2)
        y_ref[two, :, :24, :] = weight_grad(2 * other + q, zs).reshape(2, 8, 24, OWN)
        z_ref[two, :, :24, :] = out_grad(other, q).reshape(2, 8, 24, OWN)

    swap_z = remote(rows24(y_ref), rz, 156, core_peer)
    swap_o = remote(rows24(z_ref), ro, 157, core_peer)
    swap_z.start()
    swap_o.start()

    @pl.loop(0, 2)
    def _(q):
        two = pl.ds(2 * q, 2)
        dm_ref[two, :, :24, :] = weight_grad(2 * place.c + q, zs).reshape(2, 8, 24, OWN)
        own_o[q] = out_grad(place.c, q).reshape(8, 2, 24, OWN)

    def rows_fns(ref, first, n):
        some = pl.ds(first, n)

        def view(big):
            return ref.at[some, big, pl.ds(0, 24), :]

        def read(big):
            return ref[some, big, :24, :]

        def write(big, total):
            ref[some, big, :24, :] = total

        return view, read, write

    def write_o(big, total):
        own_o[:, big] = total

    sum_z = Reduce(place, remote, *rows_fns(dm_ref, 0, 4), gz, gz2, 92)
    sum_x = Reduce(place, remote, *rows_fns(big_b, 0, 4), gx, gx2, 102)
    sum_o = Reduce(
        place, remote, lambda big: own_o.at[:, big], lambda big: own_o[:, big], write_o, go, go2, 112
    )

    state[...] = jnp.zeros_like(state)
    halo[...] = jnp.zeros_like(halo)

    @pl.loop(0, BLOCKS)
    def _(i):
        b = BLOCKS - 1 - i

        @pl.when(i == 1)
        def _():
            swap_z.wait_recv()
            swap_o.wait_recv()
            for r in range(4):
                dm_ref[r, :, :24, :] += rz[r]
            for q in range(2):
                own_o[q] += ro[2 * q : 2 * q + 2].reshape(8, 2, 24, OWN)
            sum_z.begin()
            sum_o.begin()

        pl.when(i == 7)(outs.middle)

        conv = block_of(big_b, b, 640)
        raw, core, dcore = raw_ref[b], core_ref[b], dcore_ref[b]
        sig = jax.nn.sigmoid(conv)
        act = conv * sig
        x, keys, query = act[:, :OWN], act[:, OWN : OWN + NS], act[:, OWN + NS :]
        shifted = raw + hd_ref[0:1, :128]
        dt = softplus(shifted)
        rate = jnp.exp(hd_ref[1:2, :128])
        log_decay = -rate * dt
        dskip_ref[0:1, :] += jnp.sum(dcore * x, axis=0, keepdims=True)
        cumulative, turned, wide = decay_parts(log_decay)
        contact = dot3(query, keys, 1, 1)
        dt_wide = widen(dt)
        scaled = x * dt_wide
        dcontact = jnp.zeros((BLOCK, BLOCK), f32)
        dscaled = []
        for p in range(3):
            at = slice(128 * p, 128 * p + 128)
            mixing = [head_mixing(cumulative, turned, 2 * p + q) for q in range(2)]
            both = jnp.concatenate([m * contact for m in mixing], axis=0)
            pair = split_pair(dcore[:, at])
            dscaled.append(dot3(both, pair, 0, 0))
            dmix = dot3(pair, scaled[:, at], 1, 1)
            dcontact += dmix[:BLOCK] * mixing[0] + dmix[BLOCK:] * mixing[1]
        last = wide[BLOCK - 1 : BLOCK, :]
        before = st_ref[b]
        after_adj = state[...]
        left = jnp.exp(last - wide)
        from_core = dcore * jnp.exp(wide)
        dquery = dot3(from_core, before, 1, 1) + dot3(dcontact, keys, 1, 0)
        carried = dot3(keys, after_adj, 1, 0) * left
        dscaled = jnp.concatenate(dscaled, axis=1) + carried
        dkeys = dot3(scaled * left, after_adj, 1, 1) + dot3(dcontact, query, 0, 0)
        end = jnp.exp(last)
        state[...] = end * after_adj + dot3(query, from_core, 0, 0)
        heads = head_ones()
        last_add = dot_exact(
            jnp.sum(carried * scaled, axis=0, keepdims=True)
            + end * jnp.sum(after_adj * before, axis=0, keepdims=True),
            heads, 1, 0,
        )
        dcum = dot_exact(dcore * core - dscaled * scaled, heads, 1, 0)
        dlog = ones_dot(lower_ones(), dcum, 0, 0) + last_add
        ddt = dot_exact(dscaled * x, heads, 1, 0) - rate * dlog
        draw = ddt * jax.nn.sigmoid(shifted)
        dhead_ref[0:1, :] += jnp.sum(draw, axis=0, keepdims=True)
        dhead_ref[1:2, :] += jnp.sum(dlog * log_decay, axis=0, keepdims=True)
        dx = dscaled * dt_wide + skip * dcore
        dact = jnp.concatenate([dx, dkeys, dquery], axis=1)
        dconv = dact * (sig * (1.0 + conv * (1.0 - sig)))
        extended = jnp.concatenate([dconv, halo[...]], axis=0)
        halo[...] = dconv[:8, :]
        xbc = block_of(big_a, b, 640)
        dxbc = jnp.zeros_like(xbc)
        for k in range(KCONV):
            moved = extended[3 - k : 3 - k + BLOCK, :]
            dxbc += conv_row(k) * moved
            dconv_ref[k : k + 1, :] += jnp.sum(xbc * moved, axis=0, keepdims=True)
        dconv_ref[KCONV : KCONV + 1, :] += jnp.sum(dconv, axis=0, keepdims=True)
        dp_ref[b, :, OWN : OWN + 640] = dxbc.astype(bf16)
        draw_own = jnp.where(lane < 6, draw, 0.0)
        dp_ref[b, :, 1024:] = pltpu.roll(draw_own, 6 * me, 1).astype(bf16)

    @pl.loop(0, 2)
    def _(q):
        two = pl.ds(2 * q, 2)
        big_a[two, :, :24, :] = weight_grad(2 * other + q, late).reshape(2, 8, 24, 768)

    swap_x = remote(rows24(big_a), rx, 158, core_peer)
    swap_x.start()

    @pl.loop(0, 2)
    def _(q):
        two = pl.ds(2 * q, 2)
        big_b[two, :, :24, :] = weight_grad(2 * place.c + q, late).reshape(2, 8, 24, 768)

    cots.sent()
    ins = Scatter(place, remote, ct_ref, ia_ref, ib_ref, ia2_ref, ib2_ref, own_out, 122)

    @pl.loop(0, BLOCKS // 2)
    def _(i):
        pair = lax.rem(me // 2 + 1 + i, BLOCKS // 2)
        two = pl.ds(2 * pair, 2)
        part = dot(dp_ref[two].reshape(TB, COLS), w_ref[...].reshape(D, COLS), 1, 1)
        ct_ref[two] = part.astype(bf16).reshape(2, BLOCK, D)
        ins.send(2 * pair)
        ins.send(2 * pair + 1)

        @pl.when(i == 0)
        def _():
            swap_x.wait_recv()
            for r in range(4):
                big_b[r, :, :24, :] += rx[r]
            sum_x.begin()

    sum_z.middle()
    sum_o.middle()

    at_o = pl.multiple_of(768 * place.c, 128)
    o_all = Spread(
        place, remote, piece_o_ref,
        lambda big, lo, hi: gos.at[big, :, pl.ds(pl.multiple_of(at_o + lo, 128), hi - lo)],
        (256, 384, 768), 160,
    )
    z_all = Spread(
        place, remote, slab_ref.at[:, pl.ds(0, DI)],
        lambda big, lo, hi: slabs.at[big, :, pl.ds(lo, hi - lo)], (768, 1536, DI), 180,
    )
    x_all = Direct(
        place, remote, slab_ref.at[:, pl.ds(DI, WIDE - DI)],
        lambda big: slabs.at[big, :, pl.ds(DI, WIDE - DI)], 200,
    )

    def to_owners(piece, ow, base):
        copies = []
        for k in range(1, 8):
            them = place.shard_of(k)
            copy = remote(piece.at[lax.rem(them, 4)], ow.at[me], base + k, place.shard_peer(k))
            goes = them // 4 == place.c
            pl.when(goes)(copy.start)
            copies.append((copy, goes))

        @pl.when(mine)
        def _():
            ow[me] = piece[place.z]

        return copies

    piece_z[...] = sum_z.last()
    owners_z = to_owners(piece_z, ow_z, 140)
    total_o = sum_o.last()
    for q in range(2):
        piece_o_ref[:, 384 * q : 384 * q + 384] = total_o[q].reshape(48, 384).astype(bf16)
    o_all.begin()
    own_go = pltpu.make_async_copy(
        piece_o_ref, gos.at[place.big, :, pl.ds(at_o, 768)], own.at[15]
    )
    own_go.start()

    outs.last()
    locals_[2].wait()
    out_ref[...] = (own_out[...] + hid_v[...].astype(f32)).astype(bf16)

    @pl.when(mine)
    def _():
        for copy, _ in owners_z:
            copy.wait_recv()
        for j in range(8):
            slab_ref[:, OWN * j : OWN * (j + 1)] = ow_z[j].astype(bf16)
        z_all.begin()

    ins.middle()
    for n in range(4):
        o_all.step(n)
        pl.when(mine)(functools.partial(z_all.step, n))
    sum_x.middle()
    for n in range(4, 8):
        o_all.step(n)
        pl.when(mine)(functools.partial(z_all.step, n))
    piece_x[...] = sum_x.last()
    owners_x = to_owners(piece_x, ow_x, 232)
    ins.last()
    locals_[3].wait()
    u = hid_v[...].astype(f32)
    scale = lax.rsqrt(jnp.mean(u * u, axis=1, keepdims=True) + epsilon)
    d_normed = own_out[...]
    gained = gain_ref[:, :D] * d_normed
    unit = u * scale
    grad = scale * gained - unit * (scale * scale * jnp.mean(u * gained, axis=1, keepdims=True))
    igrad_ref[...] = (cot_v[...].astype(f32) + grad).astype(bf16)

    sg[...] = jnp.zeros_like(sg)
    sg[0:1, :] = jnp.sum(d_normed * unit, axis=0, keepdims=True)
    sg[1:6, :640] = dconv_ref[0:5, :]
    sg[1:2, 640:1024] = dgain_ref[0:1, :]
    sgs = [remote(sg, sg_all.at[me], 148 + k, place.shard_peer(k)) for k in range(1, 8)]
    for copy in sgs:
        copy.start()
    sg_all[me] = sg[...]

    @pl.when(mine)
    def _():
        for copy, _ in owners_x:
            copy.wait_recv()
        common = ow_x[0, :, OWN:]
        for j in range(1, 8):
            common += ow_x[j, :, OWN:]
        for j in range(8):
            slab_ref[:, DI + OWN * j : DI + OWN * (j + 1)] = ow_x[j, :, :OWN].astype(bf16)
        slab_ref[:, 2 * DI :] = common.astype(bf16)
        x_all.begin()

    own_slab = pltpu.make_async_copy(slab_ref, slabs.at[place.big], own.at[16])
    pl.when(mine)(own_slab.start)
    for copy in sgs:
        copy.wait_recv()
    small_out[...] = jnp.zeros_like(small_out)
    gvec[:, :D] = sg_all[0, 0:1, :]
    cvec[...] = jnp.zeros_like(cvec)
    cvec[:5, DI:CONVC] = sg_all[0, 1:6, OWN:640]
    for j in range(1, 8):
        gvec[:, :D] += sg_all[j, 0:1, :]
        cvec[:5, DI:CONVC] += sg_all[j, 1:6, OWN:640]
    for j in range(8):
        gvec[:, D + OWN * j : D + OWN * (j + 1)] = sg_all[j, 1:2, 640:1024]
        cvec[:5, OWN * j : OWN * (j + 1)] = sg_all[j, 1:6, :OWN]
    near = gvec[:, pl.ds(pl.multiple_of(128 * (9 * me // 2), 128), 640)]
    small_out[5:6, :576] = jnp.where(lax.rem(me, 2) == 1, near[:, 64:640], near[:, :576])
    near = cvec[:, pl.ds(pl.multiple_of(128 * (13 * me // 4), 128), 640)]
    shift = lax.rem(13 * me, 4)
    taps = near[:, :416]
    for k in range(1, 4):
        taps = jnp.where(shift == k, near[:, 32 * k : 32 * k + 416], taps)
    small_out[:5, :416] = taps[:5]
    small_out[6:7, :128] = dhead_ref[0:1, :]
    small_out[6:7, 128:256] = dhead_ref[1:2, :]
    small_out[6:7, 256:384] = dot_exact(dskip_ref[0:1, :], head_ones(), 1, 0)
    dps = [remote(small_out, smalls_dp.at[place.d], 216 + n, peer) for n, peer in enumerate(everyone)]
    for copy in dps:
        copy.start()
    smalls_dp[place.d] = small_out[...]

    @pl.when(mine)
    def _():
        x_all.forward()
        own_slab.wait()

    @pl.when(jnp.logical_not(mine))
    def _():
        for copy in z_all.cores + x_all.cores:
            copy.wait_recv()

    for copy in o_all.cores:
        copy.wait_recv()
    own_go.wait()
    for copy in dps:
        copy.wait_recv()
    total = smalls_dp[0]
    for j in range(1, 16):
        total += smalls_dp[j]
    total_small[...] = total

    for copy in smalls + sums + w_scan.copies + w_gate.copies + sgs + dps + [swap_z, swap_o, swap_x]:
        copy.wait_send()
    for group_of in (outs, ins, sum_z, sum_o, sum_x, o_all):
        group_of.sent()
    for copy, goes in owners_z + owners_x:
        pl.when(goes)(copy.wait_send)

    @pl.when(mine)
    def _():
        z_all.sent()
        x_all.sent()
        for parts in weights:
            for copy in parts:
                copy.wait_send()


def sds(shape, dtype=f32):
    return jax.ShapeDtypeStruct(shape, dtype)


def run_whole(hid, cot, in_master, out_master, conv, gain, head):
    any_spec = pl.BlockSpec(memory_space=pl.ANY)
    vmem = pl.BlockSpec(memory_space=pltpu.VMEM)

    def v(*shape, dtype=f32):
        return pltpu.VMEM(shape, dtype)

    tokens = (8, BLOCK, D)
    part = (8, BLOCK, OWN)
    split = (4, 8, 32, OWN)
    landing = [
        v(4, 2, TOP, D, dtype=bf16), v(4, BLOCK - TOP, D, dtype=bf16), v(TOP, D, dtype=bf16),
        v(4, BLOCK - TOP, D, dtype=bf16),
    ]
    return pl.pallas_call(
        whole_kernel,
        in_specs=[any_spec] * 4 + [vmem] * 3,
        out_specs=(vmem, vmem, any_spec, any_spec, vmem),
        out_shape=(
            sds((BLOCK, D), bf16), sds((BLOCK, D), bf16), sds((8, 24, WIDE), bf16),
            sds((8, 48, D), bf16), sds((8, 640)),
        ),
        scratch_shapes=[
            v(*tokens, dtype=bf16), v(*tokens, dtype=bf16), v(8, 192, COLS, dtype=bf16), v(*split),
            v(4, 8, 32, 768), v(4, 8, 32, 768), v(8, BLOCK, 128), v(*part), v(*split), v(*split),
            v(8, NS, OWN), v(*part),
            v(8, BLOCK, COLS, dtype=bf16), v(*part, dtype=bf16), v(*tokens, dtype=bf16),
            *landing, v(BLOCK, D), v(48, PROJ),
            v(48, WIDE, dtype=bf16),
            v(OWN, D, dtype=bf16), v(8, 8, 640), v(1, 4608), v(8, CONVC),
            v(16, 128), v(8, 16, 128), v(BLOCK, 128), v(4, 8, 24, OWN), v(4, 8, 24, OWN),
            v(2, 8, 2, 24, OWN), v(3, 2, 4, 24, OWN), v(4, 24, OWN), v(3, 2, 2, 2, 24, OWN),
            v(2, 2, 24, OWN), v(4, 8, 24, 768), v(3, 2, 4, 24, 768), v(4, 24, 768), *landing,
            v(4, 24, OWN), v(4, 24, 768), v(8, 24, OWN), v(8, 24, 768),
            v(24, WIDE, dtype=bf16), v(48, 768, dtype=bf16), v(8, 640), v(16, 8, 640), v(8, D), v(8, 8, D), v(8, 640), v(8, OWN), v(1, 4736),
            v(8, 3456), v(8, OWN), v(8, OWN), v(8, 640), v(8, 128), v(NS, OWN), v(8, 640), v(BLOCK, D, dtype=bf16), v(BLOCK, D, dtype=bf16),
            pltpu.SemaphoreType.DMA((250,)), pltpu.SemaphoreType.DMA((250,)),
            pltpu.SemaphoreType.DMA((41,)),
        ],
        compiler_params=pltpu.CompilerParams(
            collective_id=1, has_side_effects=True, vmem_limit_bytes=62 * 2**20
        ),
    )(hid, cot, in_master, out_master, conv, gain, head)


class Spread:
    def __init__(self, place, remote, src, view, cuts, base):
        one, two, end = cuts

        def at(dy, dx, lo, hi):
            return view(lax.rem(place.yh + dy, 2) * 4 + lax.rem(place.x + dx, 4), lo, hi)

        def onward(part, index, peer):
            return remote(part, part, base + index, peer)

        up, down, over = place.big_peer(1), place.big_peer(3), place.big_peer(4)
        own = view(place.big, 0, end)
        self.copies = [
            remote(src, own, base, up),
            remote(src, own, base + 1, down),
            remote(src, own, base + 2, over),
            onward(at(0, 3, 0, two), 3, up),
            onward(at(0, 1, two, end), 4, down),
            onward(at(0, 3, two, end), 5, over),
            onward(at(0, 1, two, end), 6, over),
            onward(at(0, 2, two, end), 7, over),
            onward(at(1, 0, 0, two), 8, up),
            onward(at(1, 0, 0, two), 9, down),
            onward(at(1, 3, 0, one), 10, up),
            onward(at(1, 1, one, two), 11, down),
        ]
        core = place.core_peer()
        self.cores = [remote(src, own, base + 12, core)]
        for n, (dy, dx, _, _) in enumerate(ARRIVALS[1:]):
            block = at(dy, dx, 0, end)
            self.cores.append(remote(block, block, base + 13 + n, core))

    def begin(self):
        for index in (2, 0, 1):
            self.copies[index].start()
        self.cores[0].start()

    def step(self, n):
        _, _, needs, sends = ARRIVALS[n]
        for index in needs:
            self.copies[index].wait_recv()
        for index in sends:
            self.copies[index].start()
        if n:
            self.cores[n].start()

    def sent(self):
        for copy in self.copies + self.cores:
            copy.wait_send()


ARRIVALS = (
    (0, 0, (), ()),
    (1, 0, (2,), (8, 9)),
    (0, 3, (0,), (3, 5)),
    (0, 1, (1,), (4, 6)),
    (0, 2, (3, 4), (7,)),
    (1, 3, (8, 5), (10,)),
    (1, 1, (9, 6), (11,)),
    (1, 2, (10, 11, 7), ()),
)


def adam_update(master, first, second, gradient, rate, decay):
    first_new = beta_one * first + (1.0 - beta_one) * gradient
    second_new = beta_two * second + (1.0 - beta_two) * (gradient * gradient)
    square = second_new * (1.0 / (1.0 - beta_two**STEP))
    root = square * lax.rsqrt(square) + adam_epsilon
    scaled = first_new * (1.0 / (1.0 - beta_one**STEP)) / root
    return (first_new, second_new, master - rate * (scaled + decay * master))


def adam_kernel(in_sum, out_sum, small, layer, grad, *refs):
    state, results = refs[:15], refs[15:30]
    for group, total in enumerate((in_sum, out_sum)):
        master, first, second = state[3 * group : 3 * group + 3]
        columns = master.shape[1]
        half = master.shape[0] // 2
        for part, lo in [(p, q) for p in range(2) for q in range(0, half, 16)]:
            inner = slice(lo, min(lo + 16, half))
            some = slice(half * part + inner.start, half * part + inner.stop)
            new = adam_update(
                master[some], first[some], second[some], total[part, inner, :columns].astype(f32),
                rates[group], decays[group],
            )
            for result, value in zip(results[3 * group : 3 * group + 3], new):
                result[some] = value
    refs[30][...] = layer[...]
    refs[31][...] = grad[...]

    @pl.when(pl.program_id(0) == 0)
    def _():
        def update(group, gradient, *index):
            values = [ref[index] for ref in state[3 * group : 3 * group + 3]]
            new = adam_update(*values, gradient, rates[group], decays[group])
            for result, value in zip(results[3 * group : 3 * group + 3], new):
                result[index] = value

        update(2, small[5, :576], slice(None))
        update(3, small[:5, :416], slice(None), slice(None))
        for row in range(3):
            at = 128 * row
            update(4, small[6:7, at : at + 6], slice(row, row + 1), slice(None))


def run_adam(in_sum, out_sum, small, layer, grad, *state):
    in_block = pl.BlockSpec((48, PROJ), lambda i: (i, 0))
    out_block = pl.BlockSpec((96, D), lambda i: (i, 0))
    tokens = pl.BlockSpec((BLOCK // 4, D), lambda i: (i, 0))
    vmem = pl.BlockSpec(memory_space=pltpu.VMEM)
    blocks = [in_block] * 3 + [out_block] * 3 + [vmem] * 9
    return pl.pallas_call(
        adam_kernel,
        grid=(4,),
        in_specs=[
            pl.BlockSpec((2, 24, WIDE), lambda i: (i, 0, 0)),
            pl.BlockSpec((2, 48, D), lambda i: (i, 0, 0)),
            vmem, tokens, tokens,
        ]
        + blocks,
        out_specs=tuple(blocks + [tokens, tokens]),
        out_shape=tuple([sds(a.shape) for a in state] + [sds((BLOCK, D), bf16)] * 2),
        compiler_params=pltpu.CompilerParams(vmem_limit_bytes=60 * 2**20),
    )(in_sum, out_sum, small, layer, grad, *state)


def on_device(hidden, cotangent, *state):
    in_master, out_master, gain_master, conv_master, head_master = state[::3]
    layer_out, input_grad, total_w, total_o, total = run_whole(
        hidden[0], cotangent[0], in_master, out_master, conv_master, gain_master, head_master
    )
    done = run_adam(total_w, total_o, total, layer_out, input_grad, *state)
    return (done[15][None], done[16][None]) + tuple(done[:15])


def solution(mesh):
    rows, columns = P("shard", None), P(None, "shard")
    tokens = P("dp", "shard", None)
    state = (rows,) * 6 + (P("shard"),) * 3 + (columns,) * 6
    return jax.shard_map(
        on_device,
        mesh=mesh,
        in_specs=(tokens, tokens) + state,
        out_specs=(tokens, tokens) + state,
        check_vma=False,
    )
```

```python
import functools

import jax
import jax.numpy as jnp
from jax import lax
from jax.experimental import pallas as pl
from jax.experimental.pallas import tpu as pltpu
from jax.sharding import PartitionSpec as P

D = 1536
DI = 3072
H = 48
HD = 64
NS = 128
KCONV = 4
STEP = 5
BLOCK = 128
CONVC = 3328
PROJ = 6448
LEN = 1024
OWN = 384
COLS = 1152
WIDE = 6528
BLOCKS = LEN // BLOCK

f32 = jnp.float32
bf16 = jnp.bfloat16
highest = lax.Precision.HIGHEST
MESH = pl.DeviceIdType.MESH
epsilon = 1e-05
beta_one = 0.9
beta_two = 0.95
adam_epsilon = 1e-08
rates = (0.05, 0.04, 0.25, 0.5, 0.5)
decays = (0.1, 0.1, 0.0, 0.0, 0.0)
TOP = 80


class Place:
    def __init__(self):
        self.d = lax.axis_index("dp")
        self.s = lax.axis_index("shard")
        self.c = lax.rem(self.d, 2)
        self.x = lax.rem(self.d // 2, 4)
        self.yh = self.d // 8
        self.big = self.d // 2
        self.z = lax.rem(self.s, 4)
        self.yl = self.s // 4

    def shard_of(self, k):
        return lax.rem(self.yl + k // 4, 2) * 4 + lax.rem(self.z + k % 4, 4)

    def shard_peer(self, k):
        return (self.d, self.shard_of(k))

    def big_of(self, k):
        return lax.rem(self.yh + k // 4, 2) * 4 + lax.rem(self.x + k % 4, 4)

    def big_peer(self, k):
        return (self.big_of(k) * 2 + self.c, self.s)

    def z_peer(self, k):
        return (self.d, self.yl * 4 + lax.rem(self.z + k, 4))

    def y_partner(self):
        return (self.d, (1 - self.yl) * 4 + self.z)

    def core_peer(self):
        return (self.big * 2 + 1 - self.c, self.s)

    def other_core_of(self, k):
        return (self.big_of(k) * 2 + 1 - self.c, self.s)


class Gather:
    def __init__(self, place, remote, src, buf, base):
        def at(dy, dz, lo, hi):
            index = lax.rem(place.yl + dy, 2) * 4 + lax.rem(place.z + dz, 4)
            return buf.at[index, pl.ds(lo, hi - lo)]

        def onward(view, index, peer):
            return remote(view, view, base + index, peer)

        up, down, over = place.z_peer(1), place.z_peer(3), place.y_partner()
        self.copies = [
            remote(src, buf.at[place.s], base, up),
            remote(src, buf.at[place.s], base + 1, down),
            remote(src, buf.at[place.s], base + 2, over),
            onward(at(0, 3, 0, 64), 3, up),
            onward(at(0, 1, 64, 128), 4, down),
            onward(at(0, 3, 64, 128), 5, over),
            onward(at(0, 1, 64, 128), 6, over),
            onward(at(0, 2, 64, 128), 7, over),
            onward(at(1, 0, 0, 64), 8, up),
            onward(at(1, 0, 0, 64), 9, down),
            onward(at(1, 3, 0, 32), 10, up),
            onward(at(1, 1, 32, 64), 11, down),
        ]

    def after(self, arrived, *indices):
        self.copies[arrived].wait_recv()
        for index in indices:
            self.copies[index].start()

    def begin(self):
        for copy in (self.copies[2], self.copies[0], self.copies[1]):
            copy.start()

    def first(self):
        self.after(2, 8, 9)
        self.after(0, 3, 5)
        self.after(1, 4, 6)

    def second(self):
        self.after(8, 10)
        self.after(9, 11)
        self.after(4, 7)

    def last(self):
        for index in (3, 5, 6, 7, 10, 11):
            self.copies[index].wait_recv()

    def sent(self):
        for copy in self.copies:
            copy.wait_send()


class Scatter:
    def __init__(self, place, remote, part, ra, rb, ra2, rb2, total, base):
        self.place, self.remote, self.base = place, remote, base
        self.part, self.ra, self.rb, self.ra2, self.rb2, self.total = part, ra, rb, ra2, rb2, total
        self.top, self.low = pl.ds(0, TOP), pl.ds(TOP, BLOCK - TOP)

    def along_z(self, b, source):
        place = self.place
        return self.remote(
            self.part.at[b, self.top],
            self.ra.at[place.z, b // 4],
            self.base + b,
            (place.d, place.yl * 4 + lax.rem(b, 4)),
            self.base + source * 2 + b // 4,
        )

    def along_y(self, b):
        z = lax.rem(b, 4)
        return self.remote(
            self.part.at[b, self.low], self.rb.at[z], self.base + 8 + z, self.place.y_partner()
        )

    def send(self, b):
        pl.when(lax.rem(b, 4) != self.place.z)(self.along_z(b, self.place.z).start)
        pl.when(b // 4 != self.place.yl)(self.along_y(b).start)

    def other(self):
        return (1 - self.place.yl) * 4 + self.place.z

    def over(self):
        return self.remote(
            self.part.at[self.other(), self.top], self.ra2, self.base + 12, self.place.y_partner()
        )

    def back(self, z):
        place = self.place
        return self.remote(
            self.part.at[place.yl * 4 + z, self.low],
            self.rb2.at[place.z],
            self.base + 13 + z,
            (place.d, place.yl * 4 + z),
            self.base + 13 + place.z,
        )

    def others(self):
        return [lax.rem(self.place.z + k, 4) for k in (1, 2, 3)]

    def middle(self):
        place, part = self.place, self.part
        for z in self.others():
            for y in range(2):
                self.along_z(y * 4 + z, z).wait_recv()

        def sum_z(block, y):
            total = part[block, :TOP].astype(f32)
            for z in self.others():
                total += self.ra[z, y].astype(f32)
            return total

        part[self.other(), :TOP] = sum_z(self.other(), 1 - place.yl).astype(bf16)
        self.over().start()
        self.total[:TOP] = sum_z(place.s, place.yl)
        for z in range(4):
            self.along_y((1 - place.yl) * 4 + z).wait_recv()
        for z in self.others():
            block = place.yl * 4 + z
            part[block, TOP:] = (part[block, TOP:].astype(f32) + self.rb[z].astype(f32)).astype(bf16)
            self.back(z).start()
        self.total[TOP:] = part[place.s, TOP:].astype(f32) + self.rb[place.z].astype(f32)

    def last(self):
        self.over().wait_recv()
        self.total[:TOP] += self.ra2[...].astype(f32)
        for z in self.others():
            self.remote(
                self.part.at[self.place.yl * 4 + z, self.low], self.rb2.at[z],
                self.base + 13 + z, (self.place.d, self.place.yl * 4 + z),
            ).wait_recv()
            self.total[TOP:] += self.rb2[z].astype(f32)

    def sent(self):
        place = self.place
        for z in self.others():
            for y in range(2):
                self.along_z(y * 4 + z, place.z).wait_send()
            self.back(z).wait_send()
        for z in range(4):
            self.along_y((1 - place.yl) * 4 + z).wait_send()
        self.over().wait_send()


class Reduce:
    def __init__(self, place, remote, view, read, write, gx, gy, base):
        self.place, self.view, self.read, self.write, self.gx, self.gy = place, view, read, write, gx, gy
        self.along = [
            remote(
                view(y * 4 + lax.rem(place.x + k, 4)), gx.at[k - 1, y], base + 2 * k + y,
                place.big_peer(k),
            )
            for k in (1, 2, 3)
            for y in range(2)
        ]
        self.other = (1 - place.yh) * 4 + place.x
        self.over = remote(view(self.other), gy, base + 8, place.big_peer(4))

    def begin(self):
        for copy in self.along:
            copy.start()

    def total(self, big, y):
        total = self.read(big)
        for k in range(3):
            total += self.gx[k, y]
        return total

    def middle(self):
        for copy in self.along:
            copy.wait_recv()
        self.write(self.other, self.total(self.other, 1 - self.place.yh))
        self.over.start()

    def last(self):
        total = self.total(self.place.big, self.place.yh)
        self.over.wait_recv()
        return total + self.gy[...]

    def sent(self):
        for copy in self.along + [self.over]:
            copy.wait_send()


class Direct:
    def __init__(self, place, remote, src, view, base):
        own, core = view(place.big), place.core_peer()
        self.copies = [remote(src, own, base + k, place.big_peer(k)) for k in range(1, 8)]
        self.cores = [remote(src, own, base + 8, core)]
        for k in range(1, 8):
            block = view(lax.rem(place.yh + k // 4, 2) * 4 + lax.rem(place.x + 4 - k % 4, 4))
            self.cores.append(remote(block, block, base + 8 + k, core))

    def begin(self):
        for copy in self.copies + self.cores[:1]:
            copy.start()

    def forward(self):
        for k in range(1, 8):
            self.copies[k - 1].wait_recv()
            self.cores[k].start()

    def sent(self):
        for copy in self.copies + self.cores:
            copy.wait_send()


def dot(a, b, ca, cb, precision=None):
    return lax.dot_general(
        a, b, (((ca,), (cb,)), ((), ())), precision=precision, preferred_element_type=f32
    )


def mm(a, b, ca=1, cb=0):
    return dot(a.astype(f32), b.astype(f32), ca, cb, highest)


def lanes(shape):
    return lax.broadcasted_iota(jnp.int32, shape, 1)


def rows_of(shape):
    return lax.broadcasted_iota(jnp.int32, shape, 0)


def widen(m):
    low = lanes((m.shape[0], 128)) < HD
    return jnp.concatenate(
        [jnp.where(low, m[:, 2 * i : 2 * i + 1], m[:, 2 * i + 1 : 2 * i + 2]) for i in range(3)],
        axis=1,
    )


def lower_ones():
    return (rows_of((BLOCK, BLOCK)) >= lanes((BLOCK, BLOCK))).astype(f32)


def head_ones():
    return (rows_of((OWN, BLOCK)) // HD == lanes((OWN, BLOCK))).astype(f32)


def split_pair(pair):
    low = lanes(pair.shape) < HD
    zero = jnp.zeros_like(pair)
    return jnp.concatenate([jnp.where(low, pair, zero), jnp.where(low, zero, pair)], axis=0)


def head_mixing(cumulative, turned, h):
    causal = rows_of((BLOCK, BLOCK)) >= lanes((BLOCK, BLOCK))
    differ = cumulative[:, h : h + 1] - turned[h : h + 1, :]
    return jnp.exp(jnp.where(causal, differ, -jnp.inf))


def softplus(v):
    return jnp.maximum(v, 0.0) + jnp.log1p(jnp.exp(-jnp.abs(v)))


TB = 256
HALF = DI // 8


def dot3(a, b, ca, cb):
    a_hi, b_hi = a.astype(bf16), b.astype(bf16)
    a_lo, b_lo = (a - a_hi.astype(f32)).astype(bf16), (b - b_hi.astype(f32)).astype(bf16)
    left = jnp.concatenate([a_hi, a_hi, a_lo], axis=ca)
    right = jnp.concatenate([b_hi, b_lo, b_hi], axis=cb)
    return dot(left, right, ca, cb)


def dot_exact(a, ones, ca, cb):
    a_hi = a.astype(bf16)
    a_lo = (a - a_hi.astype(f32)).astype(bf16)
    low = ones.astype(bf16)
    return dot(
        jnp.concatenate([a_hi, a_lo], axis=ca), jnp.concatenate([low, low], axis=cb), ca, cb
    )


def ones_dot(ones, a, ca, cb):
    a_hi = a.astype(bf16)
    a_lo = (a - a_hi.astype(f32)).astype(bf16)
    low = ones.astype(bf16)
    return dot(
        jnp.concatenate([low, low], axis=ca), jnp.concatenate([a_hi, a_lo], axis=cb), ca, cb
    )


def decay_parts(log_decay):
    cumulative = ones_dot(lower_ones(), log_decay, 1, 0)
    return cumulative, cumulative.T, widen(cumulative)


def two_blocks(ref, i, columns):
    return ref[i, :, :, :columns].reshape(TB, columns)


def block_of(ref, b, columns):
    four = pl.ds(4 * lax.rem(b, 2), 4)
    return ref[b // 2, four, :, :columns].reshape(BLOCK, columns)


def forward_block(act, dt, log_decay, before):
    x, keys, query = act[:, :OWN], act[:, OWN : OWN + NS], act[:, OWN + NS :]
    cumulative, turned, wide = decay_parts(log_decay)
    contact = dot3(query, keys, 1, 1)
    scaled = x * widen(dt)
    within = []
    for p in range(3):
        pair = split_pair(scaled[:, 128 * p : 128 * p + 128])
        both = jnp.concatenate(
            [head_mixing(cumulative, turned, 2 * p + q) * contact for q in range(2)], axis=1
        )
        within.append(dot3(both, pair, 1, 0))
    last = wide[BLOCK - 1 : BLOCK, :]
    core = jnp.concatenate(within, axis=1) + dot3(query, before, 1, 0) * jnp.exp(wide)
    after = jnp.exp(last) * before + dot3(keys, scaled * jnp.exp(last - wide), 0, 0)
    return core, after


def whole_kernel(
    hid, cot, in_ref, out_w, conv_in, gain_in, head_in,
    out_ref, igrad_ref, slabs, gos, total_small,
    n_ref, ct_ref, w_ref, z_ref, big_a, big_b, raw_ref, core_ref, y_ref, dm_ref, st_ref, dcore_ref,
    dp_ref, mixed_ref, po_ref, ra_ref, rb_ref, ra2_ref, rb2_ref, own_out, wq_f, wq, wo_ref, sm_ref, gain_ref, conv_ref,
    sums_ref, got_sums, turned_sums, rz, ro, own_o, gz, gz2, go, go2, rx, gx, gx2, ia_ref, ib_ref, ia2_ref, ib2_ref,
    piece_z, piece_x, ow_z, ow_x, slab_ref, piece_o_ref, small_out, smalls_dp, sg, sg_all, small, hd_ref, gvec, cvec, dgain_ref, dskip_ref, dconv_ref, dhead_ref,
    state, halo, hid_v, cot_v, send, recv, own,
):
    place = Place()
    me = place.s
    wq_load = pltpu.make_async_copy(
        in_ref.at[pl.ds(pl.multiple_of(48 * place.x, 8), 48), :], wq_f, own.at[7]
    )
    wq_load.start()
    wq[:, WIDE - 128 :] = jnp.zeros((48, 128), bf16)
    small[...] = jnp.zeros_like(small)
    small[:5, :416] = conv_in[...].astype(bf16).astype(f32)
    small[5, :576] = gain_in[...].astype(bf16).astype(f32)
    hd_ref[...] = jnp.zeros_like(hd_ref)
    hd_ref[:3, :6] = head_in[...].astype(bf16).astype(f32)
    hd_ref[3:4, :] = widen(hd_ref[:, :128])[2:3]
    barrier = pltpu.get_barrier_semaphore()
    core_peer = place.core_peer()
    bigs = [place.big_peer(k) for k in range(1, 8)]
    x_peers = bigs[:3]
    group = [place.shard_peer(k) for k in range(1, 8)]
    everyone = bigs + [core_peer] + [place.other_core_of(k) for k in range(1, 8)]
    for peer in group + everyone:
        pl.semaphore_signal(barrier, inc=1, device_id=peer, device_id_type=MESH)
    pl.semaphore_wait(barrier, 22)

    def remote(src, dst, index, peer, other=None):
        return pltpu.make_async_remote_copy(
            src_ref=src,
            dst_ref=dst,
            send_sem=send.at[index],
            recv_sem=recv.at[index if other is None else other],
            device_id=peer,
            device_id_type=MESH,
        )

    quarter = pl.multiple_of(48 * place.x, 16)

    def weight_parts(them):
        at = pl.multiple_of(them * OWN, 128)
        rows = pl.ds(quarter, 48)
        return (
            (wq.at[:, pl.ds(at, OWN)], w_ref.at[me, rows, pl.ds(0, OWN)]),
            (wq.at[:, pl.ds(at + DI, OWN)], w_ref.at[me, rows, pl.ds(OWN, OWN)]),
            (wq.at[:, pl.ds(2 * DI, OWN)], w_ref.at[me, rows, pl.ds(2 * OWN, OWN)]),
        )

    locals_ = [
        pltpu.make_async_copy(hid, n_ref.at[me], own.at[1]),
        pltpu.make_async_copy(cot, ct_ref.at[me], own.at[2]),
        pltpu.make_async_copy(hid, hid_v, own.at[3]),
        pltpu.make_async_copy(cot, cot_v, own.at[14]),
    ]
    for copy in locals_:
        copy.start()
    mine = place.yl == place.c
    wo_parts = [
        pltpu.make_async_copy(
            out_w.at[pl.ds(32 * (p % 12), 32), pl.ds(768 * (p // 12), 768)],
            big_a.at[p // 8, p % 8],
            own.at[17 + p],
        )
        for p in range(24)
    ]
    for copy in wo_parts:
        copy.start()
    wq_load.wait()
    wq[:, :PROJ] = wq_f[...].astype(bf16)
    own_w = [
        pltpu.make_async_copy(src, dst, own.at[4 + i])
        for i, (src, dst) in enumerate(weight_parts(me))
    ]
    smalls = [remote(small, sm_ref.at[me], k, place.shard_peer(k)) for k in range(1, 8)]
    hids = Gather(place, remote, hid, n_ref, 8)
    cots = Gather(place, remote, cot, ct_ref, 20)
    weights = []
    for k in range(1, 8):
        weights.append(
            [
                remote(src, dst, 40 + 3 * k + i, place.shard_peer(k))
                for i, (src, dst) in enumerate(weight_parts(place.shard_of(k)))
            ]
        )

    def w_begin(some):
        @pl.when(mine)
        def _():
            for i in some:
                own_w[i].start()
            for parts in weights:
                for i in some:
                    parts[i].start()

    w_begin((1, 2))
    for copy in smalls:
        copy.start()
    hids.begin()
    w_begin((0,))

    def w_arrived(some):
        for k in range(1, 8):
            @pl.when(lax.rem(place.yl + k // 4, 2) == place.c)
            def _(k=k):
                for i in some:
                    weights[k - 1][i].wait_recv()

        @pl.when(mine)
        def _():
            for i in some:
                own_w[i].wait()

    w_up, w_down = place.big_peer(1), place.big_peer(3)

    class Quarters:
        def __init__(self, columns, base):
            def quarter(k, lo=0, n=4):
                rows = pl.ds(pl.multiple_of(48 * lax.rem(place.x + k, 4), 16), 48)
                return w_ref.at[pl.ds(4 * place.c + lo, n), rows, columns]

            def on(view, index, peer):
                return remote(view, view, base + index, peer)

            self.copies = [
                on(quarter(0), 0, w_up),
                on(quarter(0), 1, w_down),
                on(quarter(0), 2, core_peer),
                on(quarter(3, 0, 2), 3, w_up),
                on(quarter(3), 4, core_peer),
                on(quarter(1, 2, 2), 5, w_down),
                on(quarter(1), 6, core_peer),
                on(quarter(2, 0, 2), 7, core_peer),
                on(quarter(2, 2, 2), 8, core_peer),
            ]

        def begin(self):
            for copy in self.copies[:3]:
                copy.start()

        def after(self, arrived, *indices):
            self.copies[arrived].wait_recv()
            for index in indices:
                self.copies[index].start()

        def first(self):
            self.after(0, 3, 4)
            self.after(1, 5, 6)

        def second(self):
            self.after(3, 7)
            self.after(5, 8)

        def last(self):
            for index in (2, 4, 6, 7, 8):
                self.copies[index].wait_recv()

    w_scan = Quarters(pl.ds(OWN, 768), 32)
    w_gate = Quarters(pl.ds(0, OWN), 240)
    w_arrived((1, 2))
    w_scan.begin()
    locals_[0].wait()
    hids.first()
    cots.begin()
    w_scan.first()
    hids.second()
    w_arrived((0,))
    w_gate.begin()
    w_scan.second()

    sm_ref[me] = small[...]
    for copy in smalls:
        copy.wait_recv()
    gain_ref[...] = jnp.concatenate([sm_ref[p, 5:6, :576] for p in range(8)], axis=1)
    conv_ref[...] = jnp.concatenate([sm_ref[p, :, :416] for p in range(8)], axis=1)
    gg_at = pl.ds(pl.multiple_of(D + OWN * me, 128), OWN)
    cv_at = pl.ds(pl.multiple_of(OWN * me, 128), OWN)

    def conv_row(k):
        return jnp.concatenate([conv_ref[k : k + 1, cv_at], conv_ref[k : k + 1, DI:]], axis=1)

    hids.last()
    hids.sent()
    w_scan.last()

    for copy in wo_parts:
        copy.wait()
    for p in range(24):
        at = 768 * (p // 12)
        rows = slice(32 * (p % 12), 32 * (p % 12) + 32)
        wo_ref[rows, at : at + 768] = big_a[p // 8, p % 8].astype(bf16)
    state[...] = jnp.zeros_like(state)
    halo[...] = jnp.zeros_like(halo)
    skip = hd_ref[3:4, :]

    @pl.loop(0, LEN // TB)
    def _(i):
        two = pl.ds(2 * i, 2)

        @pl.when(i == 1)
        def _():
            w_gate.first()

        @pl.when(i == 2)
        def _():
            w_gate.second()

        @pl.when(i == 1)
        def _():
            cots.first()

        u = n_ref[two].reshape(TB, D).astype(f32)
        scale = lax.rsqrt(jnp.mean(u * u, axis=1, keepdims=True) + epsilon)
        normed = (u * scale * gain_ref[:, :D]).astype(bf16)
        n_ref[two] = normed.reshape(2, BLOCK, D)
        project = dot(normed, w_ref[:, :, OWN:].reshape(D, 768), 1, 0)
        xbc = project[:, :640]
        raw = pltpu.roll(project[:, 640:], 128 - 6 * me, 1)
        big_a[i, :, :, :640] = xbc.reshape(8, 32, 640)
        raw_ref[two] = raw.reshape(2, BLOCK, 128)
        extended = jnp.concatenate([halo[...], xbc], axis=0)
        halo[...] = xbc[TB - 8 :, :]
        conv = conv_row(KCONV)
        for k in range(KCONV):
            conv = conv + conv_row(k) * extended[5 + k : 5 + k + TB, :]
        big_b[i, :, :, :640] = conv.reshape(8, 32, 640)
        act = conv * jax.nn.sigmoid(conv)
        dt = softplus(raw + hd_ref[0:1, :128])
        log_decay = -jnp.exp(hd_ref[1:2, :128]) * dt
        for j in range(TB // BLOCK):
            at = slice(j * BLOCK, (j + 1) * BLOCK)
            before = state[...]
            st_ref[2 * i + j] = before
            core, after = forward_block(act[at], dt[at], log_decay[at], before)
            state[...] = after
            core_ref[2 * i + j] = core
            y_ref[i, 4 * j : 4 * j + 4] = (core + skip * act[at, :OWN]).reshape(4, 32, OWN)

    cots.second()
    w_gate.last()

    @pl.loop(0, LEN // TB)
    def _(i):
        normed = n_ref[pl.ds(2 * i, 2)].reshape(TB, D)
        z = dot(normed, w_ref[:, :, :OWN].reshape(D, OWN), 1, 0)
        z_ref[i] = z.reshape(8, 32, OWN)

    locals_[1].wait()
    cots.last()

    @pl.loop(0, LEN // TB)
    def _(i):
        two = pl.ds(2 * i, 2)
        dm = dot(ct_ref[two].reshape(TB, D), wo_ref[...], 1, 1)
        dm_ref[i] = dm.reshape(8, 32, OWN)
        z = two_blocks(z_ref, i, OWN)
        gated = two_blocks(y_ref, i, OWN) * (z * jax.nn.sigmoid(z))
        ones = jnp.ones((8, OWN), f32)
        first = ones_dot(ones, gated * gated, 1, 1)
        second = ones_dot(ones, gated * (gain_ref[:, gg_at] * dm), 1, 1)
        for j in range(2):
            sums_ref[pl.ds(2 * i + j, 1), :] = first[0:1, 128 * j : 128 * j + 128]
            sums_ref[pl.ds(2 * i + j + 8, 1), :] = second[0:1, 128 * j : 128 * j + 128]

    sums = [remote(sums_ref, got_sums.at[me], 64 + k, place.shard_peer(k)) for k in range(1, 8)]
    for copy in sums:
        copy.start()
    got_sums[me] = sums_ref[...]
    for copy in sums:
        copy.wait_recv()
    totals = got_sums[0]
    for j in range(1, 8):
        totals += got_sums[j]
    turned_sums[...] = jnp.concatenate([totals, jnp.zeros((112, 128), f32)], axis=0).T
    gain = gain_ref[:, gg_at]
    lane = lanes((BLOCK, 128))
    dgain_ref[...] = jnp.zeros_like(dgain_ref)
    dskip_ref[...] = jnp.zeros_like(dskip_ref)
    dconv_ref[...] = jnp.zeros_like(dconv_ref)
    dhead_ref[...] = jnp.zeros_like(dhead_ref)

    outs = Scatter(place, remote, po_ref, ra_ref, rb_ref, ra2_ref, rb2_ref, own_out, 72)

    @pl.loop(0, BLOCKS // 2)
    def _(i):
        pair = lax.rem(me // 2 + 1 + i, BLOCKS // 2)
        column = turned_sums[...]
        for j in range(2):
            b = 2 * pair + j
            first = jnp.sum(jnp.where(lane == b, column, 0.0), axis=1, keepdims=True)
            second = jnp.sum(jnp.where(lane == b + 8, column, 0.0), axis=1, keepdims=True)
            z, y, dm = block_of(z_ref, b, OWN), block_of(y_ref, b, OWN), block_of(dm_ref, b, OWN)
            sig_z = jax.nn.sigmoid(z)
            gate = z * sig_z
            scale = lax.rsqrt(first * (1.0 / DI) + epsilon)
            unit = y * gate * scale
            mixed_ref[b] = (unit * gain).astype(bf16)
            dgain_ref[0:1, :] += jnp.sum(dm * unit, axis=0, keepdims=True)
            dgated = scale * (gain * dm) - unit * (scale * scale * (second * (1.0 / DI)))
            dz = dgated * y * (sig_z * (1.0 + z * (1.0 - sig_z)))
            dp_ref[b, :, :OWN] = dz.astype(bf16)
            dcore_ref[b] = dgated * gate
        two = pl.ds(2 * pair, 2)
        part = dot(mixed_ref[two].reshape(TB, OWN), wo_ref[...], 1, 0)
        po_ref[two] = part.astype(bf16).reshape(2, BLOCK, D)
        outs.send(2 * pair)
        outs.send(2 * pair + 1)

    def weight_grad(q, columns):
        left = n_ref[:, :, pl.ds(pl.multiple_of(384 * q, 128), 384)].reshape(LEN, 384)
        return dot(left, dp_ref[:, :, columns].reshape(LEN, -1), 0, 0)

    def out_grad(h, q):
        at = pl.multiple_of(768 * h + 384 * q, 128)
        return dot(mixed_ref[...].reshape(LEN, OWN), ct_ref[:, :, pl.ds(at, 384)].reshape(LEN, 384), 0, 0)

    other = 1 - place.c
    zs = slice(0, OWN)
    late = slice(OWN, COLS)

    def rows24(ref):
        return ref.at[:, :, pl.ds(0, 24), :]

    @pl.loop(0, 2)
    def _(q):
        two = pl.ds(2 * q, 2)
        y_ref[two, :, :24, :] = weight_grad(2 * other + q, zs).reshape(2, 8, 24, OWN)
        z_ref[two, :, :24, :] = out_grad(other, q).reshape(2, 8, 24, OWN)

    swap_z = remote(rows24(y_ref), rz, 156, core_peer)
    swap_o = remote(rows24(z_ref), ro, 157, core_peer)
    swap_z.start()
    swap_o.start()

    @pl.loop(0, 2)
    def _(q):
        two = pl.ds(2 * q, 2)
        dm_ref[two, :, :24, :] = weight_grad(2 * place.c + q, zs).reshape(2, 8, 24, OWN)
        own_o[q] = out_grad(place.c, q).reshape(8, 2, 24, OWN)

    def rows_fns(ref, first, n):
        some = pl.ds(first, n)

        def view(big):
            return ref.at[some, big, pl.ds(0, 24), :]

        def read(big):
            return ref[some, big, :24, :]

        def write(big, total):
            ref[some, big, :24, :] = total

        return view, read, write

    def write_o(big, total):
        own_o[:, big] = total

    sum_z = Reduce(place, remote, *rows_fns(dm_ref, 0, 4), gz, gz2, 92)
    sum_x = Reduce(place, remote, *rows_fns(big_b, 0, 4), gx, gx2, 102)
    sum_o = Reduce(
        place, remote, lambda big: own_o.at[:, big], lambda big: own_o[:, big], write_o, go, go2, 112
    )

    state[...] = jnp.zeros_like(state)
    halo[...] = jnp.zeros_like(halo)

    @pl.loop(0, BLOCKS)
    def _(i):
        b = BLOCKS - 1 - i

        @pl.when(i == 1)
        def _():
            swap_z.wait_recv()
            swap_o.wait_recv()
            for r in range(4):
                dm_ref[r, :, :24, :] += rz[r]
            for q in range(2):
                own_o[q] += ro[2 * q : 2 * q + 2].reshape(8, 2, 24, OWN)
            sum_z.begin()
            sum_o.begin()

        pl.when(i == 7)(outs.middle)

        conv = block_of(big_b, b, 640)
        raw, core, dcore = raw_ref[b], core_ref[b], dcore_ref[b]
        sig = jax.nn.sigmoid(conv)
        act = conv * sig
        x, keys, query = act[:, :OWN], act[:, OWN : OWN + NS], act[:, OWN + NS :]
        shifted = raw + hd_ref[0:1, :128]
        dt = softplus(shifted)
        rate = jnp.exp(hd_ref[1:2, :128])
        log_decay = -rate * dt
        dskip_ref[0:1, :] += jnp.sum(dcore * x, axis=0, keepdims=True)
        cumulative, turned, wide = decay_parts(log_decay)
        contact = dot3(query, keys, 1, 1)
        dt_wide = widen(dt)
        scaled = x * dt_wide
        dcontact = jnp.zeros((BLOCK, BLOCK), f32)
        dscaled = []
        for p in range(3):
            at = slice(128 * p, 128 * p + 128)
            mixing = [head_mixing(cumulative, turned, 2 * p + q) for q in range(2)]
            both = jnp.concatenate([m * contact for m in mixing], axis=0)
            pair = split_pair(dcore[:, at])
            dscaled.append(dot3(both, pair, 0, 0))
            dmix = dot3(pair, scaled[:, at], 1, 1)
            dcontact += dmix[:BLOCK] * mixing[0] + dmix[BLOCK:] * mixing[1]
        last = wide[BLOCK - 1 : BLOCK, :]
        before = st_ref[b]
        after_adj = state[...]
        left = jnp.exp(last - wide)
        from_core = dcore * jnp.exp(wide)
        dquery = dot3(from_core, before, 1, 1) + dot3(dcontact, keys, 1, 0)
        carried = dot3(keys, after_adj, 1, 0) * left
        dscaled = jnp.concatenate(dscaled, axis=1) + carried
        dkeys = dot3(scaled * left, after_adj, 1, 1) + dot3(dcontact, query, 0, 0)
        end = jnp.exp(last)
        state[...] = end * after_adj + dot3(query, from_core, 0, 0)
        heads = head_ones()
        last_add = dot_exact(
            jnp.sum(carried * scaled, axis=0, keepdims=True)
            + end * jnp.sum(after_adj * before, axis=0, keepdims=True),
            heads, 1, 0,
        )
        dcum = dot_exact(dcore * core - dscaled * scaled, heads, 1, 0)
        dlog = ones_dot(lower_ones(), dcum, 0, 0) + last_add
        ddt = dot_exact(dscaled * x, heads, 1, 0) - rate * dlog
        draw = ddt * jax.nn.sigmoid(shifted)
        dhead_ref[0:1, :] += jnp.sum(draw, axis=0, keepdims=True)
        dhead_ref[1:2, :] += jnp.sum(dlog * log_decay, axis=0, keepdims=True)
        dx = dscaled * dt_wide + skip * dcore
        dact = jnp.concatenate([dx, dkeys, dquery], axis=1)
        dconv = dact * (sig * (1.0 + conv * (1.0 - sig)))
        extended = jnp.concatenate([dconv, halo[...]], axis=0)
        halo[...] = dconv[:8, :]
        xbc = block_of(big_a, b, 640)
        dxbc = jnp.zeros_like(xbc)
        for k in range(KCONV):
            moved = extended[3 - k : 3 - k + BLOCK, :]
            dxbc += conv_row(k) * moved
            dconv_ref[k : k + 1, :] += jnp.sum(xbc * moved, axis=0, keepdims=True)
        dconv_ref[KCONV : KCONV + 1, :] += jnp.sum(dconv, axis=0, keepdims=True)
        dp_ref[b, :, OWN : OWN + 640] = dxbc.astype(bf16)
        draw_own = jnp.where(lane < 6, draw, 0.0)
        dp_ref[b, :, 1024:] = pltpu.roll(draw_own, 6 * me, 1).astype(bf16)

    @pl.loop(0, 2)
    def _(q):
        two = pl.ds(2 * q, 2)
        big_a[two, :, :24, :] = weight_grad(2 * other + q, late).reshape(2, 8, 24, 768)

    swap_x = remote(rows24(big_a), rx, 158, core_peer)
    swap_x.start()

    @pl.loop(0, 2)
    def _(q):
        two = pl.ds(2 * q, 2)
        big_b[two, :, :24, :] = weight_grad(2 * place.c + q, late).reshape(2, 8, 24, 768)

    cots.sent()
    ins = Scatter(place, remote, ct_ref, ia_ref, ib_ref, ia2_ref, ib2_ref, own_out, 122)

    @pl.loop(0, BLOCKS // 2)
    def _(i):
        pair = lax.rem(me // 2 + 1 + i, BLOCKS // 2)
        two = pl.ds(2 * pair, 2)
        part = dot(dp_ref[two].reshape(TB, COLS), w_ref[...].reshape(D, COLS), 1, 1)
        ct_ref[two] = part.astype(bf16).reshape(2, BLOCK, D)
        ins.send(2 * pair)
        ins.send(2 * pair + 1)

        @pl.when(i == 0)
        def _():
            swap_x.wait_recv()
            for r in range(4):
                big_b[r, :, :24, :] += rx[r]
            sum_x.begin()

    sum_z.middle()
    sum_o.middle()

    at_o = pl.multiple_of(768 * place.c, 128)
    o_all = Spread(
        place, remote, piece_o_ref,
        lambda big, lo, hi: gos.at[big, :, pl.ds(pl.multiple_of(at_o + lo, 128), hi - lo)],
        (256, 384, 768), 160,
    )
    z_all = Spread(
        place, remote, slab_ref.at[:, pl.ds(0, DI)],
        lambda big, lo, hi: slabs.at[big, :, pl.ds(lo, hi - lo)], (768, 1536, DI), 180,
    )
    x_all = Direct(
        place, remote, slab_ref.at[:, pl.ds(DI, WIDE - DI)],
        lambda big: slabs.at[big, :, pl.ds(DI, WIDE - DI)], 200,
    )

    def to_owners(piece, ow, base):
        copies = []
        for k in range(1, 8):
            them = place.shard_of(k)
            copy = remote(piece.at[lax.rem(them, 4)], ow.at[me], base + k, place.shard_peer(k))
            goes = them // 4 == place.c
            pl.when(goes)(copy.start)
            copies.append((copy, goes))

        @pl.when(mine)
        def _():
            ow[me] = piece[place.z]

        return copies

    piece_z[...] = sum_z.last()
    owners_z = to_owners(piece_z, ow_z, 140)
    total_o = sum_o.last()
    for q in range(2):
        piece_o_ref[:, 384 * q : 384 * q + 384] = total_o[q].reshape(48, 384).astype(bf16)
    o_all.begin()
    own_go = pltpu.make_async_copy(
        piece_o_ref, gos.at[place.big, :, pl.ds(at_o, 768)], own.at[15]
    )
    own_go.start()

    outs.last()
    locals_[2].wait()
    out_ref[...] = (own_out[...] + hid_v[...].astype(f32)).astype(bf16)

    @pl.when(mine)
    def _():
        for copy, _ in owners_z:
            copy.wait_recv()
        for j in range(8):
            slab_ref[:, OWN * j : OWN * (j + 1)] = ow_z[j].astype(bf16)
        z_all.begin()

    ins.middle()
    for n in range(4):
        o_all.step(n)
        pl.when(mine)(functools.partial(z_all.step, n))
    sum_x.middle()
    for n in range(4, 8):
        o_all.step(n)
        pl.when(mine)(functools.partial(z_all.step, n))
    piece_x[...] = sum_x.last()
    owners_x = to_owners(piece_x, ow_x, 232)
    ins.last()
    locals_[3].wait()
    u = hid_v[...].astype(f32)
    scale = lax.rsqrt(jnp.mean(u * u, axis=1, keepdims=True) + epsilon)
    d_normed = own_out[...]
    gained = gain_ref[:, :D] * d_normed
    unit = u * scale
    grad = scale * gained - unit * (scale * scale * jnp.mean(u * gained, axis=1, keepdims=True))
    igrad_ref[...] = (cot_v[...].astype(f32) + grad).astype(bf16)

    sg[...] = jnp.zeros_like(sg)
    sg[0:1, :] = jnp.sum(d_normed * unit, axis=0, keepdims=True)
    sg[1:6, :640] = dconv_ref[0:5, :]
    sg[1:2, 640:1024] = dgain_ref[0:1, :]
    sgs = [remote(sg, sg_all.at[me], 148 + k, place.shard_peer(k)) for k in range(1, 8)]
    for copy in sgs:
        copy.start()
    sg_all[me] = sg[...]

    @pl.when(mine)
    def _():
        for copy, _ in owners_x:
            copy.wait_recv()
        common = ow_x[0, :, OWN:]
        for j in range(1, 8):
            common += ow_x[j, :, OWN:]
        for j in range(8):
            slab_ref[:, DI + OWN * j : DI + OWN * (j + 1)] = ow_x[j, :, :OWN].astype(bf16)
        slab_ref[:, 2 * DI :] = common.astype(bf16)
        x_all.begin()

    own_slab = pltpu.make_async_copy(slab_ref, slabs.at[place.big], own.at[16])
    pl.when(mine)(own_slab.start)
    for copy in sgs:
        copy.wait_recv()
    small_out[...] = jnp.zeros_like(small_out)
    gvec[:, :D] = sg_all[0, 0:1, :]
    cvec[...] = jnp.zeros_like(cvec)
    cvec[:5, DI:CONVC] = sg_all[0, 1:6, OWN:640]
    for j in range(1, 8):
        gvec[:, :D] += sg_all[j, 0:1, :]
        cvec[:5, DI:CONVC] += sg_all[j, 1:6, OWN:640]
    for j in range(8):
        gvec[:, D + OWN * j : D + OWN * (j + 1)] = sg_all[j, 1:2, 640:1024]
        cvec[:5, OWN * j : OWN * (j + 1)] = sg_all[j, 1:6, :OWN]
    near = gvec[:, pl.ds(pl.multiple_of(128 * (9 * me // 2), 128), 640)]
    small_out[5:6, :576] = jnp.where(lax.rem(me, 2) == 1, near[:, 64:640], near[:, :576])
    near = cvec[:, pl.ds(pl.multiple_of(128 * (13 * me // 4), 128), 640)]
    shift = lax.rem(13 * me, 4)
    taps = near[:, :416]
    for k in range(1, 4):
        taps = jnp.where(shift == k, near[:, 32 * k : 32 * k + 416], taps)
    small_out[:5, :416] = taps[:5]
    small_out[6:7, :128] = dhead_ref[0:1, :]
    small_out[6:7, 128:256] = dhead_ref[1:2, :]
    small_out[6:7, 256:384] = dot_exact(dskip_ref[0:1, :], head_ones(), 1, 0)
    dps = [remote(small_out, smalls_dp.at[place.d], 216 + n, peer) for n, peer in enumerate(everyone)]
    for copy in dps:
        copy.start()
    smalls_dp[place.d] = small_out[...]

    @pl.when(mine)
    def _():
        x_all.forward()
        own_slab.wait()

    @pl.when(jnp.logical_not(mine))
    def _():
        for copy in z_all.cores + x_all.cores:
            copy.wait_recv()

    for copy in o_all.cores:
        copy.wait_recv()
    own_go.wait()
    for copy in dps:
        copy.wait_recv()
    total = smalls_dp[0]
    for j in range(1, 16):
        total += smalls_dp[j]
    total_small[...] = total

    for copy in smalls + sums + w_scan.copies + w_gate.copies + sgs + dps + [swap_z, swap_o, swap_x]:
        copy.wait_send()
    for group_of in (outs, ins, sum_z, sum_o, sum_x, o_all):
        group_of.sent()
    for copy, goes in owners_z + owners_x:
        pl.when(goes)(copy.wait_send)

    @pl.when(mine)
    def _():
        z_all.sent()
        x_all.sent()
        for parts in weights:
            for copy in parts:
                copy.wait_send()


def sds(shape, dtype=f32):
    return jax.ShapeDtypeStruct(shape, dtype)


def run_whole(hid, cot, in_master, out_master, conv, gain, head):
    any_spec = pl.BlockSpec(memory_space=pl.ANY)
    vmem = pl.BlockSpec(memory_space=pltpu.VMEM)

    def v(*shape, dtype=f32):
        return pltpu.VMEM(shape, dtype)

    tokens = (8, BLOCK, D)
    part = (8, BLOCK, OWN)
    split = (4, 8, 32, OWN)
    landing = [
        v(4, 2, TOP, D, dtype=bf16), v(4, BLOCK - TOP, D, dtype=bf16), v(TOP, D, dtype=bf16),
        v(4, BLOCK - TOP, D, dtype=bf16),
    ]
    return pl.pallas_call(
        whole_kernel,
        in_specs=[any_spec] * 4 + [vmem] * 3,
        out_specs=(vmem, vmem, any_spec, any_spec, vmem),
        out_shape=(
            sds((BLOCK, D), bf16), sds((BLOCK, D), bf16), sds((8, 24, WIDE), bf16),
            sds((8, 48, D), bf16), sds((8, 640)),
        ),
        scratch_shapes=[
            v(*tokens, dtype=bf16), v(*tokens, dtype=bf16), v(8, 192, COLS, dtype=bf16), v(*split),
            v(4, 8, 32, 768), v(4, 8, 32, 768), v(8, BLOCK, 128), v(*part), v(*split), v(*split),
            v(8, NS, OWN), v(*part),
            v(8, BLOCK, COLS, dtype=bf16), v(*part, dtype=bf16), v(*tokens, dtype=bf16),
            *landing, v(BLOCK, D), v(48, PROJ),
            v(48, WIDE, dtype=bf16),
            v(OWN, D, dtype=bf16), v(8, 8, 640), v(1, 4608), v(8, CONVC),
            v(16, 128), v(8, 16, 128), v(BLOCK, 128), v(4, 8, 24, OWN), v(4, 8, 24, OWN),
            v(2, 8, 2, 24, OWN), v(3, 2, 4, 24, OWN), v(4, 24, OWN), v(3, 2, 2, 2, 24, OWN),
            v(2, 2, 24, OWN), v(4, 8, 24, 768), v(3, 2, 4, 24, 768), v(4, 24, 768), *landing,
            v(4, 24, OWN), v(4, 24, 768), v(8, 24, OWN), v(8, 24, 768),
            v(24, WIDE, dtype=bf16), v(48, 768, dtype=bf16), v(8, 640), v(16, 8, 640), v(8, D), v(8, 8, D), v(8, 640), v(8, OWN), v(1, 4736),
            v(8, 3456), v(8, OWN), v(8, OWN), v(8, 640), v(8, 128), v(NS, OWN), v(8, 640), v(BLOCK, D, dtype=bf16), v(BLOCK, D, dtype=bf16),
            pltpu.SemaphoreType.DMA((250,)), pltpu.SemaphoreType.DMA((250,)),
            pltpu.SemaphoreType.DMA((41,)),
        ],
        compiler_params=pltpu.CompilerParams(
            collective_id=1, has_side_effects=True, vmem_limit_bytes=62 * 2**20
        ),
    )(hid, cot, in_master, out_master, conv, gain, head)


class Spread:
    def __init__(self, place, remote, src, view, cuts, base):
        one, two, end = cuts

        def at(dy, dx, lo, hi):
            return view(lax.rem(place.yh + dy, 2) * 4 + lax.rem(place.x + dx, 4), lo, hi)

        def onward(part, index, peer):
            return remote(part, part, base + index, peer)

        up, down, over = place.big_peer(1), place.big_peer(3), place.big_peer(4)
        own = view(place.big, 0, end)
        self.copies = [
            remote(src, own, base, up),
            remote(src, own, base + 1, down),
            remote(src, own, base + 2, over),
            onward(at(0, 3, 0, two), 3, up),
            onward(at(0, 1, two, end), 4, down),
            onward(at(0, 3, two, end), 5, over),
            onward(at(0, 1, two, end), 6, over),
            onward(at(0, 2, two, end), 7, over),
            onward(at(1, 0, 0, two), 8, up),
            onward(at(1, 0, 0, two), 9, down),
            onward(at(1, 3, 0, one), 10, up),
            onward(at(1, 1, one, two), 11, down),
        ]
        core = place.core_peer()
        self.cores = [remote(src, own, base + 12, core)]
        for n, (dy, dx, _, _) in enumerate(ARRIVALS[1:]):
            block = at(dy, dx, 0, end)
            self.cores.append(remote(block, block, base + 13 + n, core))

    def begin(self):
        for index in (2, 0, 1):
            self.copies[index].start()
        self.cores[0].start()

    def step(self, n):
        _, _, needs, sends = ARRIVALS[n]
        for index in needs:
            self.copies[index].wait_recv()
        for index in sends:
            self.copies[index].start()
        if n:
            self.cores[n].start()

    def sent(self):
        for copy in self.copies + self.cores:
            copy.wait_send()


ARRIVALS = (
    (0, 0, (), ()),
    (1, 0, (2,), (8, 9)),
    (0, 3, (0,), (3, 5)),
    (0, 1, (1,), (4, 6)),
    (0, 2, (3, 4), (7,)),
    (1, 3, (8, 5), (10,)),
    (1, 1, (9, 6), (11,)),
    (1, 2, (10, 11, 7), ()),
)


def adam_update(master, first, second, gradient, rate, decay):
    first_new = beta_one * first + (1.0 - beta_one) * gradient
    second_new = beta_two * second + (1.0 - beta_two) * (gradient * gradient)
    square = second_new * (1.0 / (1.0 - beta_two**STEP))
    root = square * lax.rsqrt(square) + adam_epsilon
    scaled = first_new * (1.0 / (1.0 - beta_one**STEP)) / root
    return (first_new, second_new, master - rate * (scaled + decay * master))


def adam_kernel(in_sum, out_sum, small, layer, grad, *refs):
    state, results = refs[:15], refs[15:30]
    for group, total in enumerate((in_sum, out_sum)):
        master, first, second = state[3 * group : 3 * group + 3]
        columns = master.shape[1]
        half = master.shape[0] // 2
        for part, lo in [(p, q) for p in range(2) for q in range(0, half, 16)]:
            inner = slice(lo, min(lo + 16, half))
            some = slice(half * part + inner.start, half * part + inner.stop)
            new = adam_update(
                master[some], first[some], second[some], total[part, inner, :columns].astype(f32),
                rates[group], decays[group],
            )
            for result, value in zip(results[3 * group : 3 * group + 3], new):
                result[some] = value
    refs[30][...] = layer[...]
    refs[31][...] = grad[...]

    @pl.when(pl.program_id(0) == 0)
    def _():
        def update(group, gradient, *index):
            values = [ref[index] for ref in state[3 * group : 3 * group + 3]]
            new = adam_update(*values, gradient, rates[group], decays[group])
            for result, value in zip(results[3 * group : 3 * group + 3], new):
                result[index] = value

        update(2, small[5, :576], slice(None))
        update(3, small[:5, :416], slice(None), slice(None))
        for row in range(3):
            at = 128 * row
            update(4, small[6:7, at : at + 6], slice(row, row + 1), slice(None))


def run_adam(in_sum, out_sum, small, layer, grad, *state):
    in_block = pl.BlockSpec((48, PROJ), lambda i: (i, 0))
    out_block = pl.BlockSpec((96, D), lambda i: (i, 0))
    tokens = pl.BlockSpec((BLOCK // 4, D), lambda i: (i, 0))
    vmem = pl.BlockSpec(memory_space=pltpu.VMEM)
    blocks = [in_block] * 3 + [out_block] * 3 + [vmem] * 9
    return pl.pallas_call(
        adam_kernel,
        grid=(4,),
        in_specs=[
            pl.BlockSpec((2, 24, WIDE), lambda i: (i, 0, 0)),
            pl.BlockSpec((2, 48, D), lambda i: (i, 0, 0)),
            vmem, tokens, tokens,
        ]
        + blocks,
        out_specs=tuple(blocks + [tokens, tokens]),
        out_shape=tuple([sds(a.shape) for a in state] + [sds((BLOCK, D), bf16)] * 2),
        compiler_params=pltpu.CompilerParams(vmem_limit_bytes=60 * 2**20),
    )(in_sum, out_sum, small, layer, grad, *state)


def on_device(hidden, cotangent, *state):
    in_master, out_master, gain_master, conv_master, head_master = state[::3]
    layer_out, input_grad, total_w, total_o, total = run_whole(
        hidden[0], cotangent[0], in_master, out_master, conv_master, gain_master, head_master
    )
    done = run_adam(total_w, total_o, total, layer_out, input_grad, *state)
    return (done[15][None], done[16][None]) + tuple(done[:15])


def solution(mesh):
    rows, columns = P("shard", None), P(None, "shard")
    tokens = P("dp", "shard", None)
    state = (rows,) * 6 + (P("shard"),) * 3 + (columns,) * 6
    return jax.shard_map(
        on_device,
        mesh=mesh,
        in_specs=(tokens, tokens) + state,
        out_specs=(tokens, tokens) + state,
        check_vma=False,
    )
```
